32 devices in a mesh: tm: 8 (over y, x, core), chan: 4 (over z).
Axes of the slice: x: 2, y: 2, z: 4, core: 2. Of those that a mesh axis runs over, the one named last changes fastest.
Arguments:
- signal: bfloat16 [16384, 512], P('tm', 'chan'), may hold values from -6 to 6
- segment_ids: int32 [16384], replicated, may hold values from 0 to 8, as said below
- v_section: bfloat16 [256, 16, 512], P('chan'), may hold values from -6 to 6
- g_section: bfloat16 [512], replicated, may hold values from 1.5 to 3
- b_section: bfloat16 [256], P('chan'), may hold values from -2 to 2
- v_dilated: bfloat16 [3, 256, 3, 256], P(None, 'chan'), may hold values from -6 to 6
- g_dilated: bfloat16 [3, 256], P(None, 'chan'), may hold values from 0.59765625 to 1.3984375
- b_dilated: bfloat16 [3, 256], P(None, 'chan'), may hold values from -2 to 2
- v_mix: bfloat16 [3, 256, 256], P(None, 'chan'), may hold values from -6 to 6
- g_mix: bfloat16 [3, 256], P(None, 'chan'), may hold values from 0.59765625 to 1.3984375
- b_mix: bfloat16 [3, 256], P(None, 'chan'), may hold values from -2 to 2
- v_skip: bfloat16 [3, 256, 256], P(None, 'chan'), may hold values from -6 to 6
- g_skip: bfloat16 [3, 256], P(None, 'chan'), may hold values from 0.59765625 to 1.3984375
- b_skip: bfloat16 [3, 256], P(None, 'chan'), may hold values from -2 to 2
- cotangent: bfloat16 [256, 131072], P('chan', 'tm'), may hold values from -6 to 6
Outputs:
- output: bfloat16 [256, 131072], P('chan', 'tm')
- signal_grad: bfloat16 [16384, 512], P('tm', 'chan')
- v_section_grad: float32 [256, 16, 512], P('chan')
- g_section_grad: float32 [512], replicated
- b_section_grad: float32 [256], P('chan')
- v_dilated_grad: float32 [3, 256, 3, 256], P(None, 'chan')
- g_dilated_grad: float32 [3, 256], P(None, 'chan')
- b_dilated_grad: float32 [3, 256], P(None, 'chan')
- v_mix_grad: float32 [3, 256, 256], P(None, 'chan')
- g_mix_grad: float32 [3, 256], P(None, 'chan')
- b_mix_grad: float32 [3, 256], P(None, 'chan')
- v_skip_grad: float32 [3, 256, 256], P(None, 'chan')
- g_skip_grad: float32 [3, 256], P(None, 'chan')
- b_skip_grad: float32 [3, 256], P(None, 'chan')
The draws below stay inside these ranges and needn't reach their ends.
Inputs may be any that keep to these rules, and one draw needn't show every extreme that they name: `segment_ids`: ids never fall; they rise by one at exactly one frame inside each aligned block of 2048 frames, never at a block's first frame.
All inputs are finite; a program needn't handle non-finite values.
Results may differ from the reference program's by a relative error of at most 0.014.
Values may be sent and summed in bfloat16 or wider, within the bound.
No kernel may reach another device: no remote copies, remote signals or barrier semaphores. Data moves between devices by JAX's collectives and lax.ppermute only.
A program may use at most 256 MiB of HBM per device.

```python
from functools import partial
import jax
import jax.numpy as jnp
from jax import lax

CIN = 512
CH = 256
KT = 16
TAPS = 3
BLOCKS = 3
TIN_DEV = 2048
TIN = 16384
FRAMES = 131072


def draw_segment_ids(key, part):
    key = jax.random.fold_in(key, 11)
    places = jax.random.randint(key, (TIN // TIN_DEV,), 1, TIN_DEV)
    frames = jnp.arange(TIN, dtype=jnp.int32)
    rising = (frames % TIN_DEV == places[frames // TIN_DEV]).astype(jnp.int32)
    return jnp.cumsum(rising).astype(jnp.int32)


def steps_of(own_key, dims, pieces, smallest, top_value):
    factor_of, own = 1.0, jax.random.fold_in(own_key, 6)
    for dim, parts in pieces:
        heights = jnp.exp(jax.random.uniform(jax.random.fold_in(own, dim), (parts,), jnp.float32, smallest / len(pieces), top_value / len(pieces)))
        factor_of = factor_of * jnp.repeat(heights, dims[dim] // parts).reshape([-1 if axis == dim else 1 for axis in range(len(dims))])
    return factor_of


def noise(own_key, shape, deviation, most, split=(), kind=jnp.bfloat16):
    array = deviation * jax.random.normal(own_key, shape, jnp.float32)
    if split:
        array = array * steps_of(own_key, shape, split, -0.22, 0.18)
    return jnp.clip(array, -most, most).astype(kind)


def setup_inputs(seed: int = 0) -> dict:
    key_of = jax.random.split(jax.random.key(seed), 16)
    return {
        "signal": noise(key_of[0], (TIN, CIN), 1.0, 6.0, ((0, 8), (1, 4))),
        "segment_ids": draw_segment_ids(jax.random.fold_in(key_of[15], 71), 0),
        "v_section": noise(key_of[2], (CH, KT, CIN), 1.0, 6.0, ((0, 4),)),
        "g_section": jnp.clip(jax.random.uniform(key_of[3], (CIN,), jnp.float32, 1.5, 3.0), 1.5, 3.0).astype(jnp.bfloat16),
        "b_section": noise(key_of[4], (CH,), 0.3, 2.0, ((0, 4),)),
        "v_dilated": noise(key_of[5], (BLOCKS, CH, TAPS, CH), 1.0, 6.0, ((1, 4),)),
        "g_dilated": jnp.clip(0.59765625 + 0.80078125 * jax.random.uniform(key_of[6], (BLOCKS, CH), jnp.float32) ** steps_of(key_of[6], (BLOCKS, CH), ((1, 4),), -0.2, 0.2), 0.59765625, 1.3984375).astype(jnp.bfloat16),
        "b_dilated": noise(key_of[7], (BLOCKS, CH), 0.3, 2.0, ((1, 4),)),
        "v_mix": noise(key_of[8], (BLOCKS, CH, CH), 1.0, 6.0, ((1, 4),)),
        "g_mix": jnp.clip(0.59765625 + 0.80078125 * jax.random.uniform(key_of[9], (BLOCKS, CH), jnp.float32) ** steps_of(key_of[9], (BLOCKS, CH), ((1, 4),), -0.2, 0.2), 0.59765625, 1.3984375).astype(jnp.bfloat16),
        "b_mix": noise(key_of[10], (BLOCKS, CH), 0.3, 2.0, ((1, 4),)),
        "v_skip": noise(key_of[11], (BLOCKS, CH, CH), 1.0, 6.0, ((1, 4),)),
        "g_skip": jnp.clip(0.59765625 + 0.80078125 * jax.random.uniform(key_of[12], (BLOCKS, CH), jnp.float32) ** steps_of(key_of[12], (BLOCKS, CH), ((1, 4),), -0.2, 0.2), 0.59765625, 1.3984375).astype(jnp.bfloat16),
        "b_skip": noise(key_of[13], (BLOCKS, CH), 0.3, 2.0, ((1, 4),)),
        "cotangent": noise(key_of[14], (CH, FRAMES), 1.0, 6.0, ((0, 4), (1, 8))),
    }


@jax.custom_vjp
def low(v):
    return lax.optimization_barrier(v.astype(jnp.bfloat16)).astype(jnp.float32)

@jax.custom_vjp
def low_back(v):
    return v

def low_keep(v):
    return (low(v), None)

def low_pass(kept, grad):
    return (grad,)

def back_keep(v):
    return (v, None)

def back_low(kept, grad):
    return (low(grad),)
low.defvjp(low_keep, low_pass)
low_back.defvjp(back_keep, back_low)
EPSILON = 1e-06

def product(left_side, right_side):
    return jnp.dot(left_side, right_side, precision=lax.Precision.HIGHEST, preferred_element_type=jnp.float32)

def shifted(values, offset):
    if offset > 0:
        filler = jnp.zeros((offset,) + values.shape[1:], values.dtype)
        return jnp.concatenate([values[offset:], filler], axis=0)
    if offset < 0:
        filler = jnp.zeros((-offset,) + values.shape[1:], values.dtype)
        return jnp.concatenate([filler, values[:offset]], axis=0)
    return values

def matched(frame_ids, offset):
    padded = jnp.pad(frame_ids, 16, constant_values=-1)
    row_count = frame_ids.shape[0]
    return (padded[16:16 + row_count] == padded[16 + offset:16 + offset + row_count]).astype(jnp.float32)

def normed(v_values, gain_values, sum_axes):
    return gain_values * v_values / jnp.sqrt(lax.optimization_barrier(jnp.sum(v_values * v_values, axis=sum_axes, keepdims=True)) + EPSILON)

def residual_block(hidden, v_three, g_three, b_three, v_one, g_one, b_one, v_two, g_two, b_two, frame_ids=None, dilate=1):
    w_three = low(normed(v_three, g_three, (0, 1)))
    activated = low(jax.nn.silu(hidden))
    inner_sum = b_three
    for tap_index in range(3):
        offset = (tap_index - 1) * dilate
        inner_sum = inner_sum + matched(frame_ids, offset)[:, None] * product(shifted(activated, offset), w_three[tap_index])
    inner_sum = low_back(inner_sum)
    mixed_rows = low(jax.nn.silu(inner_sum))
    w_one = low(normed(v_one, g_one, (0,)))
    w_two = low(normed(v_two, g_two, (0,)))
    combined = product(mixed_rows, w_one) + b_one + product(hidden, w_two) + b_two
    return low(low_back(combined))

def reference(signal, segment_ids, v_section, g_section, b_section, v_dilated, g_dilated, b_dilated, v_mix, g_mix, b_mix, v_skip, g_skip, b_skip, cotangent):
    frame_ids = jnp.repeat(segment_ids, 8)
    same_prev = matched(segment_ids, -1)[:, None, None]
    same_next = matched(segment_ids, 1)[:, None, None]

    def forward(signal, v_section, g_section, b_section, v_dilated, g_dilated, b_dilated, v_mix, g_mix, b_mix, v_skip, g_skip, b_skip):
        v_section = jnp.transpose(v_section, (1, 2, 0))
        v_dilated = jnp.transpose(v_dilated, (0, 2, 3, 1))
        v_mix = jnp.transpose(v_mix, (0, 2, 1))
        v_skip = jnp.transpose(v_skip, (0, 2, 1))
        activated = low(jax.nn.silu(signal))
        weight = low(normed(v_section, g_section[None, :, None], (0, 2)))
        centre = jnp.einsum('ti,rio->tro', activated, weight[4:12], precision=lax.Precision.HIGHEST)
        early_sum = same_prev * jnp.einsum('ti,rio->tro', shifted(activated, -1), weight[12:16], precision=lax.Precision.HIGHEST)
        late_sum = same_next * jnp.einsum('ti,rio->tro', shifted(activated, 1), weight[0:4], precision=lax.Precision.HIGHEST)
        section_sum = (centre + jnp.concatenate([early_sum, late_sum], axis=1)).reshape(-1, weight.shape[2]) + b_section
        hidden = low(low_back(section_sum))
        for block_index in range(BLOCKS):
            block_fn = jax.checkpoint(partial(residual_block, frame_ids=frame_ids, dilate=3 ** block_index))
            hidden = block_fn(hidden, v_dilated[block_index], g_dilated[block_index], b_dilated[block_index], v_mix[block_index], g_mix[block_index], b_mix[block_index], v_skip[block_index], g_skip[block_index], b_skip[block_index])
        return hidden.T
    primals = [signal, v_section, g_section, b_section, v_dilated, g_dilated, b_dilated, v_mix, g_mix, b_mix, v_skip, g_skip, b_skip]
    primals = [entry.astype(jnp.float32) for entry in primals]
    output, pullback = jax.vjp(forward, *primals)
    gradients = pullback(cotangent.astype(jnp.float32))
    return (output.astype(jnp.bfloat16), gradients[0].astype(jnp.bfloat16), gradients[1], gradients[2], gradients[3], gradients[4], gradients[5], gradients[6], gradients[7], gradients[8], gradients[9], gradients[10], gradients[11], gradients[12])
```

```python
import jax
import jax.numpy as jnp
from jax import lax
from jax.experimental import pallas as pl
from jax.experimental.pallas import tpu as pltpu
from jax.sharding import PartitionSpec as P

EPSILON = 1e-06
F32 = jnp.float32
BF16 = jnp.bfloat16
HALO = 8
VMEM_BYTES = 60 * 1024 * 1024


def xor_pairs(axis, bit):
    return [(i, i ^ bit) for i in range(lax.axis_size(axis))]


def swap(values, axis, bit):
    return lax.ppermute(values, axis, xor_pairs(axis, bit))


def spread(piece):
    half = piece.shape[0] // 2
    by_x = swap(piece, "tm", 2)
    by_y = swap(piece, "tm", 4)
    far_a = swap(by_y[:half], "tm", 2)
    far_b = swap(by_x[half:], "tm", 4)
    near = [piece, by_x, by_y, far_a, far_b]
    return near + [swap(entry, "tm", 1) for entry in near]


SPREAD_PLACES = [(0, 0, 2), (2, 0, 2), (4, 0, 2), (6, 0, 1), (6, 1, 1)]
SPREAD_PLACES = SPREAD_PLACES + [(a + 1, first, count) for a, first, count in SPREAD_PLACES]


def edges(block, dim, width):
    count = lax.axis_size("tm")
    forward = [(i, i + 1) for i in range(count - 1)]
    backward = [(target, source) for source, target in forward]
    size = block.shape[dim]
    low = lax.ppermute(lax.slice_in_dim(block, size - width, None, axis=dim), "tm", forward)
    high = lax.ppermute(lax.slice_in_dim(block, 0, width, axis=dim), "tm", backward)
    return low, high


def nt(left, right):
    return lax.dot_general(left, right, (((1,), (1,)), ((), ())), preferred_element_type=F32)


def nn(left, right):
    return lax.dot_general(left, right, (((1,), (0,)), ((), ())), preferred_element_type=F32)


def tn(left, right):
    return lax.dot_general(left, right, (((0,), (0,)), ((), ())), preferred_element_type=F32)


def sigmoid(values):
    return 0.5 * jnp.tanh(0.5 * values) + 0.5


def doubled(mask):
    return jnp.concatenate([mask, mask], axis=1)


def moved(values, rows):
    return pltpu.roll(values, (-rows) % values.shape[0], 0)


def spread_phases(store, mask_ref, phase, values, dilate):
    def masked(rows, mask_index):
        return (moved(values, rows) * doubled(mask_ref[mask_index])).astype(BF16)

    store[9 + phase] = values.astype(BF16)

    @pl.when(phase >= 8 - min(dilate, 8))
    def _():
        store[1 + phase] = masked(-1, 0)

    @pl.when(phase <= min(dilate, 8) - 1)
    def _():
        store[17 + phase] = masked(1, 1)

    if dilate > 8:

        @pl.when(phase == 7)
        def _():
            store[0] = masked(-2, 2)

        @pl.when(phase == 0)
        def _():
            store[25] = masked(2, 3)


def weight_copies(places, refs, wsec, wblk, sem):
    turn, chan = places[0], places[1]
    copies = []
    for ref, (place, first, _) in zip(refs, SPREAD_PLACES, strict=True):
        pair = 2 * (turn ^ place)
        for k in range(ref.shape[0]):
            rows = pl.ds(pl.multiple_of(64 * (chan ^ (2 * first + k)), 64), 64)
            copies.append(
                pltpu.make_async_copy(
                    ref.at[k, :, :, 0:512], wsec.at[pl.ds(pair, 2), rows, :], sem
                )
            )
            copies.append(
                pltpu.make_async_copy(
                    ref.at[k, :, :, 512:768], wblk.at[pl.ds(pair, 2), rows, :], sem
                )
            )
    return copies


def forward_kernel(
    places,
    sig0,
    sig1,
    sig2,
    sig3,
    mask_ref,
    gain_ref,
    *rest,
):
    pieces = rest[:10]
    hid_out, act_out, mix_out, dsi_out, dsh_out = rest[10:15]
    sact_out, dsig_out, stat_out = rest[15:18]
    outs = rest[18:22]
    wsec, wblk, cat, bias, hid, mix, dsi, dsh, act, wide, turned, wsem, ssem, osem = rest[22:]
    chan = places[1]
    rows = sig0.shape[0]
    own = rows - 2 * HALO
    loads = weight_copies(places, pieces, wsec, wblk, wsem)
    for copy in loads:
        copy.start()
    for k, ref in enumerate((sig0, sig1, sig2, sig3)):
        lanes = pl.ds(pl.multiple_of(128 * (chan ^ k), 128), 128)
        values = ref[...].astype(F32)
        s = sigmoid(values)
        a = values * s
        sact_out[:, lanes] = a.astype(BF16)
        dsig_out[:, lanes] = (s + a * (1.0 - s))[:own]
    for copy in loads:
        copy.wait()

    def square(k, total):
        part = wsec[k].astype(F32)
        return total + jnp.sum((part * part).reshape(32, 8, 512), axis=0)

    total = lax.fori_loop(0, 16, square, jnp.zeros((8, 512), F32))
    norm = jnp.sqrt(jnp.sum(total, axis=0, keepdims=True) + EPSILON)
    scale = gain_ref[...] / norm
    stat_out[...] = jnp.concatenate([norm, scale, jnp.zeros((6, 512), F32)], axis=0)
    bias[...] = jnp.transpose(wblk[15].astype(F32))[:16]
    scaled = sact_out[...].astype(F32) * scale
    cat[0] = scaled.astype(BF16)
    cat[1] = (moved(scaled, -1) * doubled(doubled(mask_ref[0]))).astype(BF16)
    cat[2] = (moved(scaled, 1) * doubled(doubled(mask_ref[1]))).astype(BF16)

    def section(r, carry):
        total = nt(cat[0], wsec[r + 4]) + nt(cat[1 + r // 4], wsec[lax.rem(r + 12, 16)])
        hid[0, r] = (total + bias[0:1]).astype(BF16)
        return carry

    lax.fori_loop(0, 8, section, 0)

    def save(b, r, part, whole, out):
        pltpu.make_async_copy(part, whole, out).start()

    for b in range(3):
        dilate = 3**b

        def widen(p, carry):
            h = hid[b, p].astype(F32)
            s = sigmoid(h)
            a = h * s
            dsh[b, p] = (s + a * (1.0 - s)).astype(BF16)
            spread_phases(act, mask_ref, p, a, dilate)
            pltpu.make_async_copy(hid.at[b, p], hid_out.at[b, p], ssem).start()
            pltpu.make_async_copy(dsh.at[b, p], dsh_out.at[b, p], ssem).start()
            pltpu.make_async_copy(act.at[9 + p], act_out.at[b, p], osem).start()
            return carry

        lax.fori_loop(0, 8, widen, 0)

        def block(r, carry):
            inner = (
                nt(act[9 + r - dilate], wblk[5 * b])
                + nt(act[9 + r], wblk[5 * b + 1])
                + nt(act[9 + r + dilate], wblk[5 * b + 2])
                + bias[1 + b : 2 + b]
            )
            s = sigmoid(inner)
            m = inner * s
            mixed = m.astype(BF16)
            mix[b, r] = mixed
            dsi[b, r] = (s + m * (1.0 - s)).astype(BF16)
            pltpu.make_async_copy(mix.at[b, r], mix_out.at[b, r], ssem).start()
            pltpu.make_async_copy(dsi.at[b, r], dsi_out.at[b, r], ssem).start()
            after = nt(mixed, wblk[5 * b + 3]) + nt(hid[b, r], wblk[5 * b + 4])
            after = after + (bias[4 + b : 5 + b] + bias[7 + b : 8 + b])
            if b < 2:
                hid[b + 1, r] = after.astype(BF16)
            else:
                for half in range(2):
                    wide[half, pl.ds(r, own, stride=8), :] = after[:own, 128 * half : 128 * half + 128]
            return carry

        lax.fori_loop(0, 8, block, 0)
        for p in range(8):
            pltpu.make_async_copy(act.at[9 + p], act_out.at[b, p], osem).wait()

    def turn(q, carry):
        frames = pl.ds(pl.multiple_of(128 * q, 128), 128)
        for half in range(2):
            part = wide[half, frames, :]
            turned[128 * half : 128 * half + 128, frames] = jnp.transpose(part).astype(BF16)
        return carry

    lax.fori_loop(0, 8 * own // 128, turn, 0)
    final = []
    for k, out in enumerate(outs):
        part = turned.at[pl.ds(pl.multiple_of(64 * (chan ^ k), 64), 64), :]
        final.append(pltpu.make_async_copy(part, out, osem))
    for copy in final:
        copy.start()
    for source, out in ((hid, hid_out), (dsh, dsh_out), (mix, mix_out), (dsi, dsi_out)):
        for b in range(3):
            for p in range(8):
                pltpu.make_async_copy(source.at[b, p], out.at[b, p], ssem).wait()
    for copy in final:
        copy.wait()


def backward_kernel(
    places,
    cot0,
    cot1,
    cot2,
    cot3,
    mask_ref,
    sact_ref,
    dsig_ref,
    stat_ref,
    hid_in,
    act_in,
    mix_in,
    dsi_in,
    dsh_in,
    *rest,
):
    pieces = rest[:10]
    even_out, odd_out = rest[10:12]
    sgrads = rest[12:16]
    (wsec, wblk, turned, wide, grad, inner, both, act, dsi, dsh) = rest[16:26]
    (acc_one, acc_three, through, sums, staged, wsem, csem, bsem, osem) = rest[26:]
    turn_index, chan = places[0], places[1]
    rows = mask_ref.shape[1]
    own = rows - 2 * HALO

    loads = weight_copies(places, pieces, wsec, wblk, wsem)
    cots = []
    for k, ref in enumerate((cot0, cot1, cot2, cot3)):
        part = turned.at[pl.ds(pl.multiple_of(64 * (chan ^ k), 64), 64), :]
        cots.append(pltpu.make_async_copy(ref, part, csem))

    def kept(b):
        slot = b % 2
        return [
            pltpu.make_async_copy(mix_in.at[b, :, 0:own], both.at[slot, :, :, 0:256], bsem.at[slot]),
            pltpu.make_async_copy(hid_in.at[b, :, 0:own], both.at[slot, :, :, 256:512], bsem.at[slot]),
            pltpu.make_async_copy(act_in.at[b, :, 0:own], act.at[slot], bsem.at[slot]),
            pltpu.make_async_copy(dsi_in.at[b], dsi.at[slot], bsem.at[slot]),
            pltpu.make_async_copy(dsh_in.at[b], dsh.at[slot], bsem.at[slot]),
        ]

    for copy in cots + loads + kept(2) + kept(1):
        copy.start()
    for copy in cots:
        copy.wait()

    def turn(q, carry):
        frames = pl.ds(pl.multiple_of(128 * q, 128), 128)
        for half in range(2):
            part = turned[128 * half : 128 * half + 128, frames].astype(F32)
            wide[half, frames, :] = jnp.transpose(part)
        return carry

    lax.fori_loop(0, 8 * rows // 128, turn, 0)

    def phases(r, carry):
        for half in range(2):
            part = wide[half, pl.ds(r, rows, stride=8), :]
            grad[r, :, 128 * half : 128 * half + 128] = part.astype(BF16)
        return carry

    lax.fori_loop(0, 8, phases, 0)
    for copy in loads:
        copy.wait()
    sums[...] = jnp.zeros_like(sums)

    def own_sum(values):
        return jnp.sum(values[:own].reshape(own // 8, 8, 256), axis=0)

    for b in (2, 1, 0):
        dilate = 3**b
        slot = b % 2
        for copy in kept(b):
            copy.wait()
        acc_one[...] = jnp.zeros_like(acc_one)
        acc_three[...] = jnp.zeros_like(acc_three)

        def first(r, carry):
            g = grad[r]
            down = nn(g, wblk[5 * b + 3])
            ig = down * dsi[slot, r].astype(F32)
            spread_phases(inner, mask_ref, r, ig, dilate)
            acc_one[...] += tn(g[:own], both[slot, r])
            sums[1 + b] += own_sum(ig)
            sums[4 + b] += own_sum(g.astype(F32))
            return carry

        lax.fori_loop(0, 8, first, 0)

        def second(r, carry):
            low, mid, high = inner[9 + r - dilate], inner[9 + r], inner[9 + r + dilate]
            deep = nn(high, wblk[5 * b]) + nn(mid, wblk[5 * b + 1]) + nn(low, wblk[5 * b + 2])
            back = nn(grad[r], wblk[5 * b + 4]) + dsh[slot, r].astype(F32) * deep
            grad[r] = back.astype(BF16)
            a = act[slot, r]
            acc_three[:, 0:256] += tn(a, high[:own])
            acc_three[:, 256:512] += tn(a, mid[:own])
            acc_three[:, 512:768] += tn(a, low[:own])
            return carry

        lax.fori_loop(0, 8, second, 0)
        for tap in range(3):
            part = jnp.transpose(acc_three[:, 256 * tap : 256 * tap + 256])
            staged[5 * b + tap, :, 512:768] = part.astype(BF16)
        staged[5 * b + 3, :, 512:768] = acc_one[:, 0:256].astype(BF16)
        staged[5 * b + 4, :, 512:768] = acc_one[:, 256:512].astype(BF16)
        if b == 2:
            for copy in kept(0):
                copy.start()

    def taps(r, carry):
        g = grad[r].astype(F32)
        sums[0] += own_sum(g)
        inner[r + 4] = grad[r]
        early = r < 4
        nearby = jnp.where(early, moved(g, 1), moved(g, -1))
        mask = jnp.where(early, mask_ref[1], mask_ref[0])
        inner[lax.rem(r + 12, 16)] = (nearby * doubled(mask)).astype(BF16)
        return carry

    lax.fori_loop(0, 8, taps, 0)
    through[...] = jnp.zeros_like(through)

    def collect(k, carry):
        through[...] += nn(inner[k, 0:own], wsec[k])
        return carry

    lax.fori_loop(0, 16, collect, 0)
    deep = through[...]
    sact = sact_ref[0:own]
    gains = jnp.sum(sact.astype(F32) * deep, axis=0, keepdims=True)
    signal_grad = deep * stat_ref[1:2] * dsig_ref[...]
    through[...] = signal_grad
    for k, out in enumerate(sgrads):
        lanes = pl.ds(pl.multiple_of(128 * (chan ^ k), 128), 128)
        out[...] = through[:, lanes].astype(BF16)
    biases = jnp.concatenate(
        [jnp.sum(sums[index], axis=0, keepdims=True) for index in range(8)]
        + [jnp.zeros((120, 256), F32)],
        axis=0,
    )
    staged[15, :, 512:640] = jnp.transpose(biases).astype(BF16)
    gain_rows = jnp.concatenate(
        [gains[:, 128 * q : 128 * q + 128] for q in range(4)] + [jnp.zeros((60, 128), F32)], axis=0
    ).astype(BF16)
    for part in range(4):
        staged[15, 64 * part : 64 * part + 64, 640:768] = gain_rows

    def finish(pair, carry):
        for tap in range(2):
            k = 2 * pair + tap
            staged[k, :, 0:512] = tn(inner[k, 0:own], sact).astype(BF16)
        place = pair ^ turn_index
        source = staged.at[pl.ds(2 * pair, 2)]

        @pl.when(lax.rem(place, 2) == 0)
        def _():
            pltpu.make_async_copy(source, even_out.at[place // 2], osem).start()

        @pl.when(lax.rem(place, 2) == 1)
        def _():
            pltpu.make_async_copy(source, odd_out.at[place // 2], osem).start()

        return carry

    lax.fori_loop(0, 8, finish, 0)
    for pair in range(8):
        pltpu.make_async_copy(staged.at[pl.ds(2 * pair, 2)], even_out.at[0], osem).wait()


def shape_of(shape, kind=BF16):
    return jax.ShapeDtypeStruct(shape, kind)


SPEC_VMEM = pl.BlockSpec(memory_space=pltpu.VMEM)
SPEC_ANY = pl.BlockSpec(memory_space=pl.ANY)
SPEC_SMEM = pl.BlockSpec(memory_space=pltpu.SMEM)


def run_forward(places, signals, masks, gain, pieces):
    rows = masks.shape[1]
    own = rows - 2 * HALO
    kept = shape_of((3, 8, rows, 256))
    out_shape = [kept] * 5 + [
        shape_of((rows, 512)),
        shape_of((own, 512), F32),
        shape_of((8, 512), F32),
    ]
    out_shape = out_shape + [shape_of((64, 8 * own))] * 4
    return pl.pallas_call(
        forward_kernel,
        out_shape=out_shape,
        in_specs=[SPEC_SMEM] + [SPEC_VMEM] * 6 + [SPEC_ANY] * 10,
        out_specs=[SPEC_ANY] * 5 + [SPEC_VMEM] * 3 + [SPEC_ANY] * 4,
        scratch_shapes=[
            pltpu.VMEM((16, 256, 512), BF16),
            pltpu.VMEM((16, 256, 256), BF16),
            pltpu.VMEM((3, rows, 512), BF16),
            pltpu.VMEM((16, 256), F32),
            pltpu.VMEM((3, 8, rows, 256), BF16),
            pltpu.VMEM((3, 8, rows, 256), BF16),
            pltpu.VMEM((3, 8, rows, 256), BF16),
            pltpu.VMEM((3, 8, rows, 256), BF16),
            pltpu.VMEM((26, rows, 256), BF16),
            pltpu.VMEM((2, 8 * own, 128), F32),
            pltpu.VMEM((256, 8 * own), BF16),
            pltpu.SemaphoreType.DMA,
            pltpu.SemaphoreType.DMA,
            pltpu.SemaphoreType.DMA,
        ],
        compiler_params=pltpu.CompilerParams(vmem_limit_bytes=VMEM_BYTES),
        name="forward_blocks",
    )(places, *signals, masks, gain, *pieces)


def run_backward(places, cotangents, masks, sact, dsig, stat, kept, pieces):
    rows = masks.shape[1]
    own = rows - 2 * HALO
    return pl.pallas_call(
        backward_kernel,
        out_shape=[shape_of((4, 2, 256, 768))] * 2 + [shape_of((own, 128))] * 4,
        in_specs=[SPEC_SMEM]
        + [SPEC_ANY] * 4
        + [SPEC_VMEM] * 4
        + [SPEC_ANY] * 5
        + [SPEC_ANY] * 10,
        out_specs=[SPEC_ANY] * 2 + [SPEC_VMEM] * 4,
        scratch_shapes=[
            pltpu.VMEM((16, 256, 512), BF16),
            pltpu.VMEM((16, 256, 256), BF16),
            pltpu.VMEM((256, 8 * rows), BF16),
            pltpu.VMEM((2, 8 * rows, 128), F32),
            pltpu.VMEM((8, rows, 256), BF16),
            pltpu.VMEM((26, rows, 256), BF16),
            pltpu.VMEM((2, 8, own, 512), BF16),
            pltpu.VMEM((2, 8, own, 256), BF16),
            pltpu.VMEM((2, 8, rows, 256), BF16),
            pltpu.VMEM((2, 8, rows, 256), BF16),
            pltpu.VMEM((256, 512), F32),
            pltpu.VMEM((256, 768), F32),
            pltpu.VMEM((own, 512), F32),
            pltpu.VMEM((8, 8, 256), F32),
            pltpu.VMEM((16, 256, 768), BF16),
            pltpu.SemaphoreType.DMA,
            pltpu.SemaphoreType.DMA,
            pltpu.SemaphoreType.DMA((2,)),
            pltpu.SemaphoreType.DMA,
        ],
        compiler_params=pltpu.CompilerParams(vmem_limit_bytes=VMEM_BYTES),
        name="backward_blocks",
    )(places, *cotangents, masks, sact, dsig, stat, *kept, *pieces)


def exchange(values, axis, cut):
    me = lax.axis_index(axis)
    parts = [cut(me)]
    for k in (1, 2, 3):
        parts.append(swap(cut(me ^ k), axis, k))
    return parts


def normed(v_values, gain_values, sum_axes):
    norm_values = jnp.sqrt(jnp.sum(v_values * v_values, axis=sum_axes, keepdims=True) + EPSILON)
    return gain_values * v_values / norm_values, norm_values


def norm_back(grad_w, v_values, gain_values, norm_values, sum_axes):
    grad_g = jnp.sum(grad_w * v_values, axis=sum_axes, keepdims=True) / norm_values
    grad_v = gain_values / norm_values * (grad_w - grad_g / norm_values * v_values)
    return grad_v, grad_g


def body(
    signal,
    segment_ids,
    v_section,
    g_section,
    b_section,
    v_dilated,
    g_dilated,
    b_dilated,
    v_mix,
    g_mix,
    b_mix,
    v_skip,
    g_skip,
    b_skip,
    cotangent,
):
    tm_index, chan = lax.axis_index("tm"), lax.axis_index("chan")
    turn = tm_index % 8
    places = jnp.stack([turn, chan]).astype(jnp.int32)
    own = signal.shape[0] // 4
    rows = own + 2 * HALO
    start = tm_index * signal.shape[0] + chan * own

    padded = jnp.pad(segment_ids, HALO + 2, constant_values=-1)
    nearby = lax.dynamic_slice_in_dim(padded, start, rows + 4)

    def same(offset):
        flags = (nearby[2 : 2 + rows] == nearby[2 + offset : 2 + offset + rows]).astype(F32)
        flags = jnp.concatenate([flags[HALO:], flags[:HALO]])
        return jnp.broadcast_to(flags[:, None], (rows, 128))

    masks = jnp.stack([same(-1), same(1), same(-2), same(2)])

    low, high = edges(signal, 0, HALO)
    longer = jnp.concatenate([low, signal, high], axis=0)

    def cut_signal(place):
        block = lax.dynamic_slice_in_dim(longer, place * own, rows, axis=0)
        return jnp.concatenate([block[HALO:], block[:HALO]], axis=0)

    signals = exchange(longer, "chan", cut_signal)

    three_v, three_g = v_dilated.astype(F32), g_dilated.astype(F32)[:, :, None, None]
    mix_v, mix_g = v_mix.astype(F32), g_mix.astype(F32)[:, :, None]
    skip_v, skip_g = v_skip.astype(F32), g_skip.astype(F32)[:, :, None]
    w_three, three_norm = normed(three_v, three_g, (2, 3))
    w_mix, mix_norm = normed(mix_v, mix_g, (2,))
    w_skip, skip_norm = normed(skip_v, skip_g, (2,))
    matrices = jnp.concatenate(
        [jnp.transpose(w_three, (0, 2, 1, 3)), w_mix[:, None], w_skip[:, None]], axis=1
    ).astype(BF16)
    matrices = matrices.reshape(15, 64, 256)
    small = jnp.concatenate([b_section[None], b_dilated, b_mix, b_skip], axis=0).T
    small = jnp.pad(small, ((0, 0), (0, 246)))
    matrices = jnp.concatenate([matrices, small[None]], axis=0)
    piece = jnp.concatenate(
        [
            jnp.transpose(lax.dynamic_slice_in_dim(v_section, 2 * turn, 2, axis=1), (1, 0, 2)),
            lax.dynamic_slice_in_dim(matrices, 2 * turn, 2, axis=0),
        ],
        axis=2,
    )
    column = jnp.stack([piece] + [swap(piece, "chan", k) for k in (1, 2, 3)])
    pieces = spread(column)

    frames = 8 * own
    rim = 8 * HALO
    low, high = edges(cotangent, 1, rim)

    def cut_cotangent(place):
        main = lax.dynamic_slice_in_dim(cotangent, place * frames, frames, axis=1)
        after_start = jnp.minimum((place + 1) * frames, 3 * frames)
        before_start = jnp.maximum(place * frames - rim, 0)
        after = lax.dynamic_slice_in_dim(cotangent, after_start, rim, axis=1)
        before = lax.dynamic_slice_in_dim(cotangent, before_start, rim, axis=1)
        after = jnp.where(place == 3, high, after)
        before = jnp.where(place == 0, low, before)
        return jnp.concatenate([main, after, before], axis=1)

    cotangents = exchange(cotangent, "chan", cut_cotangent)

    section_gain = g_section.astype(F32)
    results = run_forward(places, signals, masks, section_gain[None], pieces)
    kept, sact, dsig, stat, outs = results[:5], results[5], results[6], results[7], results[8:]

    received = [outs[0]] + [swap(outs[k], "chan", k) for k in (1, 2, 3)]
    output = jnp.zeros((64, 4 * frames), BF16)
    for k in range(4):
        output = lax.dynamic_update_slice_in_dim(output, received[k], (chan ^ k) * frames, axis=1)

    results = run_backward(places, cotangents, masks, sact, dsig, stat, kept, pieces)
    even, odd, sgrads = results[0], results[1], results[2:]

    received = [sgrads[0]] + [swap(sgrads[k], "chan", k) for k in (1, 2, 3)]
    signal_grad = jnp.zeros((4 * own, 128), BF16)
    for k in range(4):
        signal_grad = lax.dynamic_update_slice_in_dim(
            signal_grad, received[k], (chan ^ k) * own, axis=0
        )

    quarter = even + swap(odd, "tm", 1)
    far_a = swap(quarter[3, :1], "tm", 2)
    far_b = swap(quarter[3, 1:], "tm", 4)
    for_y = jnp.concatenate([quarter[2, :1] + far_a, quarter[2, 1:]], axis=0)
    for_x = jnp.concatenate([quarter[1, :1], quarter[1, 1:] + far_b], axis=0)
    summed = quarter[0] + swap(for_x, "tm", 2) + swap(for_y, "tm", 4)

    def cut_rows(place):
        return lax.dynamic_slice_in_dim(summed, place * 64, 64, axis=1)

    parts = exchange(summed, "chan", cut_rows)
    mine = parts[0] + parts[1] + parts[2] + parts[3]
    bit = 8
    while bit < lax.axis_size("tm"):
        mine = mine + swap(mine, "tm", bit)
        bit = 2 * bit
    gathered = spread(mine)
    slots = [None] * 8
    for a in (0, 1):
        base = gathered[5 * a : 5 * a + 5]
        slots[a], slots[2 + a], slots[4 + a] = base[0], base[1], base[2]
        slots[6 + a] = jnp.concatenate([base[3], base[4]], axis=0)
    slots = jnp.stack(slots)
    slots = jnp.take(slots, jnp.arange(8) ^ turn, axis=0).reshape(16, 64, 768).astype(F32)

    grad_section = jnp.transpose(slots[:, :, 0:512], (1, 0, 2))
    grad_blocks = slots[:15, :, 512:768].reshape(3, 5, 64, 256)
    aux = slots[15, :, 512:768]
    section_norm = stat[0]
    section_gain_grad = aux[0:4, 128:256].reshape(512) / section_norm
    section_v_grad = (
        section_gain
        / section_norm
        * (grad_section - section_gain_grad / section_norm * v_section.astype(F32))
    )
    bias_grads = aux[:, 0:7].T
    three_v_grad, three_g_grad = norm_back(
        jnp.transpose(grad_blocks[:, 0:3], (0, 2, 1, 3)), three_v, three_g, three_norm, (2, 3)
    )
    mix_v_grad, mix_g_grad = norm_back(grad_blocks[:, 3], mix_v, mix_g, mix_norm, (2,))
    skip_v_grad, skip_g_grad = norm_back(grad_blocks[:, 4], skip_v, skip_g, skip_norm, (2,))
    return (
        output,
        signal_grad,
        section_v_grad,
        section_gain_grad,
        bias_grads[0],
        three_v_grad,
        three_g_grad.reshape(3, 64),
        bias_grads[1:4],
        mix_v_grad,
        mix_g_grad.reshape(3, 64),
        bias_grads[4:7],
        skip_v_grad,
        skip_g_grad.reshape(3, 64),
        bias_grads[4:7],
    )


def solution(mesh):
    return jax.shard_map(
        body,
        mesh=mesh,
        in_specs=(
            P("tm", "chan"),
            P(),
            P("chan", None, None),
            P(),
            P("chan"),
            P(None, "chan", None, None),
            P(None, "chan"),
            P(None, "chan"),
            P(None, "chan", None),
            P(None, "chan"),
            P(None, "chan"),
            P(None, "chan", None),
            P(None, "chan"),
            P(None, "chan"),
            P("chan", "tm"),
        ),
        out_specs=(
            P("chan", "tm"),
            P("tm", "chan"),
            P("chan", None, None),
            P(),
            P("chan"),
            P(None, "chan", None, None),
            P(None, "chan"),
            P(None, "chan"),
            P(None, "chan", None),
            P(None, "chan"),
            P(None, "chan"),
            P(None, "chan", None),
            P(None, "chan"),
            P(None, "chan"),
        ),
        check_vma=False,
    )
```

```python
import jax
import jax.numpy as jnp
from jax import lax
from jax.experimental import pallas as pl
from jax.experimental.pallas import tpu as pltpu
from jax.sharding import PartitionSpec as P

EPSILON = 1e-06
F32 = jnp.float32
BF16 = jnp.bfloat16
HALO = 8
VMEM_BYTES = 60 * 1024 * 1024
MIB = 1024 * 1024


def xor_pairs(axis, bit):
    return [(i, i ^ bit) for i in range(lax.axis_size(axis))]


def swap(values, axis, bit):
    return lax.ppermute(values, axis, xor_pairs(axis, bit))


def spread(piece):
    half = piece.shape[0] // 2
    by_x = swap(piece, "tm", 2)
    by_y = swap(piece, "tm", 4)
    far_a = swap(by_y[:half], "tm", 2)
    far_b = swap(by_x[half:], "tm", 4)
    near = [piece, by_x, by_y, far_a, far_b]
    return near + [swap(entry, "tm", 1) for entry in near]


SPREAD_PLACES = [(0, 0, 2), (2, 0, 2), (4, 0, 2), (6, 0, 1), (6, 1, 1)]
SPREAD_PLACES = SPREAD_PLACES + [(a + 1, first, count) for a, first, count in SPREAD_PLACES]


def nt(left, right):
    return lax.dot_general(left, right, (((1,), (1,)), ((), ())), preferred_element_type=F32)


def nn(left, right):
    return lax.dot_general(left, right, (((1,), (0,)), ((), ())), preferred_element_type=F32)


def tn(left, right):
    return lax.dot_general(left, right, (((0,), (0,)), ((), ())), preferred_element_type=F32)


def sigmoid(values):
    return 0.5 * jnp.tanh(0.5 * values) + 0.5


def doubled(mask):
    return jnp.concatenate([mask, mask], axis=1)


def moved(values, rows):
    return pltpu.roll(values, (-rows) % values.shape[0], 0)


def fill_masks(ids_ref, mask_ref):
    rows = mask_ref.shape[1]
    for index, step in enumerate((-1, 1, -2, 2)):
        inside = ids_ref[16 : 8 + rows] == ids_ref[16 + step : 8 + rows + step]
        before = ids_ref[8:16] == ids_ref[8 + step : 16 + step]
        mask_ref[index, 0 : rows - 8] = inside.astype(F32)
        mask_ref[index, rows - 8 : rows] = before.astype(F32)


def edge_tile(chan, tile, edge, dim):
    half = tile.shape[dim] // 2
    after = lax.broadcasted_iota(jnp.int32, tile.shape, dim) < half
    is_last = jnp.where(chan == 3, 1, 0)
    is_first = jnp.where(chan == 0, 1, 0)
    return jnp.where(jnp.where(after, is_last, is_first) == 1, edge, tile)


def pack_weights_kernel(
    places, sec_ref, three_ref, mix_ref, skip_ref, bs, bt, bm, bk, gt, gm, gk, out, wide, rows, mats
):
    turn = places[0]
    for q in range(4):
        part = sec_ref[:, :, 128 * q : 128 * q + 128].astype(F32)
        wide[q] = part.reshape(1024, 128)
    rows[...] = jnp.zeros_like(rows)
    rows[0:1, 0:64] = bs[...].astype(F32)
    for index, ref in enumerate((bt, bm, bk, gt, gm, gk)):
        rows[1 + 3 * index : 4 + 3 * index, 0:64] = ref[...].astype(F32)
    columns = jnp.transpose(rows[...])[0:64]
    for b in range(3):
        three = three_ref[b].astype(F32)
        gain = columns[:, 10 + b : 11 + b]
        total = jnp.sum(jnp.sum(three * three, axis=0), axis=1, keepdims=True)
        scale = gain / jnp.sqrt(total + EPSILON)
        for tap in range(3):
            mats[5 * b + tap] = (three[tap] * scale).astype(BF16)
        for index, ref in ((3, mix_ref), (4, skip_ref)):
            part = ref[b].astype(F32)
            gain = columns[:, 3 * index + 4 + b : 3 * index + 5 + b]
            total = jnp.sum(part * part, axis=1, keepdims=True)
            mats[5 * b + index] = (part * (gain / jnp.sqrt(total + EPSILON))).astype(BF16)
    mats[15, :, 0:128] = columns.astype(BF16)
    mats[15, :, 128:256] = jnp.zeros((64, 128), BF16)
    for tap in range(2):
        for q in range(4):
            part = wide[q, pl.ds(2 * turn + tap, 64, stride=16), :]
            out[tap, :, 128 * q : 128 * q + 128] = part.astype(BF16)
        out[tap, :, 512:768] = mats[2 * turn + tap]


def pack_frames_kernel(places, piece, signal, cotangent, *rest):
    sigs, edges, cots = rest[0:4], rest[4:8], rest[8:12]
    chan = places[1]
    own = signal.shape[0] // 4
    frames = 8 * own
    lower = lax.broadcasted_iota(jnp.int32, (16, 128), 0) < HALO
    for k in range(4):
        dest = chan ^ k
        sigs[k][0:own] = signal[pl.ds(pl.multiple_of(dest * own, own), own)]
        after = pl.multiple_of(jnp.minimum(dest + 1, 3) * own, 16)
        before = pl.multiple_of(jnp.maximum(dest * own - 16, 0), 16)
        tile = jnp.where(
            lower, signal[pl.ds(after, 16)].astype(F32), signal[pl.ds(before, 16)].astype(F32)
        )
        sigs[k][own : own + 16] = tile.astype(BF16)
        first = signal[0:16].astype(F32)
        last = signal[4 * own - 16 : 4 * own].astype(F32)
        edges[k][0:16] = jnp.where(dest == 3, first, last).astype(BF16)
    lower = lax.broadcasted_iota(jnp.int32, (64, 128), 1) < 8 * HALO
    for k in range(4):
        dest = chan ^ k
        lanes = pl.ds(pl.multiple_of(dest * frames, frames), frames)
        cots[k][:, 0:frames] = cotangent[:, lanes]
        after = pl.multiple_of(jnp.minimum(dest + 1, 3) * frames, 128)
        before = pl.multiple_of(jnp.maximum(dest * frames - 128, 0), 128)
        tile = jnp.where(
            lower,
            cotangent[:, pl.ds(after, 128)].astype(F32),
            cotangent[:, pl.ds(before, 128)].astype(F32),
        )
        cots[k][:, frames : frames + 128] = tile.astype(BF16)
        first = cotangent[:, 0:128].astype(F32)
        last = cotangent[:, 4 * frames - 128 : 4 * frames].astype(F32)
        edges[k][16:80] = jnp.where(dest == 3, first, last).astype(BF16)


def finish_kernel(places, sec_ref, three_ref, mix_ref, skip_ref, gt, gm, gk, stat, *rest):
    pieces = rest[:10]
    sec_out, gain_out, bs, three_out, gt_out, bt, mix_out, gm_out, bm, skip_out, gk_out, bk = rest[10:22]
    wide, rows, mats = rest[22:]
    turn = places[0]
    for ref, (place, first, _) in zip(pieces, SPREAD_PLACES, strict=True):
        pair = 2 * (turn ^ place)
        taps = 1 if place >= 6 else 2
        for tap in range(taps):
            k = pair + tap + first
            part = ref[tap].astype(F32)
            for q in range(4):
                wide[q, pl.ds(k, 64, stride=16), :] = part[:, 128 * q : 128 * q + 128]
            mats[k] = part[:, 512:768]
    aux = mats[15]
    norm, scale = stat[0:1], stat[1:2]
    gains = jnp.concatenate([aux[q : q + 1, 128:256] for q in range(4)], axis=1) / norm
    gain_out[...] = gains
    ratio = gains / norm
    for q in range(4):
        lanes = slice(128 * q, 128 * q + 128)
        part = sec_ref[:, :, lanes].astype(F32).reshape(1024, 128)
        grad = scale[:, lanes] * (wide[q] - ratio[:, lanes] * part)
        sec_out[:, :, lanes] = grad.reshape(64, 16, 128)
    rows[...] = jnp.zeros_like(rows)
    for index, ref in enumerate((gt, gm, gk)):
        rows[3 * index : 3 * index + 3, 0:64] = ref[...].astype(F32)
    columns = jnp.transpose(rows[...])[0:64]
    results = []
    for b in range(3):
        three = three_ref[b].astype(F32)
        norm = jnp.sqrt(jnp.sum(jnp.sum(three * three, axis=0), axis=1, keepdims=True) + EPSILON)
        total = mats[5 * b] * three[0] + mats[5 * b + 1] * three[1] + mats[5 * b + 2] * three[2]
        gain = jnp.sum(total, axis=1, keepdims=True) / norm
        results.append(gain)
        for tap in range(3):
            grad = mats[5 * b + tap] - gain / norm * three[tap]
            three_out[b, tap] = columns[:, b : b + 1] / norm * grad
    for index, (ref, out) in enumerate(((mix_ref, mix_out), (skip_ref, skip_out))):
        for b in range(3):
            part = ref[b].astype(F32)
            grad = mats[5 * b + 3 + index]
            norm = jnp.sqrt(jnp.sum(part * part, axis=1, keepdims=True) + EPSILON)
            gain = jnp.sum(grad * part, axis=1, keepdims=True) / norm
            results.append(gain)
            place = 3 + 3 * index + b
            out[b] = columns[:, place : place + 1] / norm * (grad - gain / norm * part)
    lane = lax.broadcasted_iota(jnp.int32, (64, 128), 1)
    table = jnp.where(lane < 7, aux[:, 0:128], 0.0)
    for index, gain in enumerate(results):
        table = jnp.where(lane == 8 + index, gain, table)
    rows[:, 0:64] = jnp.transpose(table)
    bs[...] = rows[0:1, 0:64]
    bt[...] = rows[1:4, 0:64]
    bm[...] = rows[4:7, 0:64]
    bk[...] = rows[4:7, 0:64]
    gt_out[...] = rows[8:11, 0:64]
    gm_out[...] = rows[11:14, 0:64]
    gk_out[...] = rows[14:17, 0:64]


def spread_phases(store, mask_ref, phase, values, dilate):
    def masked(rows, mask_index):
        return (moved(values, rows) * doubled(mask_ref[mask_index])).astype(BF16)

    store[9 + phase] = values.astype(BF16)

    @pl.when(phase >= 8 - min(dilate, 8))
    def _():
        store[1 + phase] = masked(-1, 0)

    @pl.when(phase <= min(dilate, 8) - 1)
    def _():
        store[17 + phase] = masked(1, 1)

    if dilate > 8:

        @pl.when(phase == 7)
        def _():
            store[0] = masked(-2, 2)

        @pl.when(phase == 0)
        def _():
            store[25] = masked(2, 3)


def weight_copies(places, refs, wsec, wblk, sem):
    turn, chan = places[0], places[1]
    copies = []
    for ref, (place, first, _) in zip(refs, SPREAD_PLACES, strict=True):
        pair = 2 * (turn ^ place)
        for k in range(ref.shape[0]):
            rows = pl.ds(pl.multiple_of(64 * (chan ^ (2 * first + k)), 64), 64)
            copies.append(
                pltpu.make_async_copy(
                    ref.at[k, :, :, 0:512], wsec.at[pl.ds(pair, 2), rows, :], sem
                )
            )
            copies.append(
                pltpu.make_async_copy(
                    ref.at[k, :, :, 512:768], wblk.at[pl.ds(pair, 2), rows, :], sem
                )
            )
    return copies


def forward_kernel(
    places,
    sig0,
    sig1,
    sig2,
    sig3,
    edge0,
    edge1,
    edge2,
    edge3,
    ids_ref,
    gain_ref,
    *rest,
):
    pieces = rest[:10]
    hid_out, act_out, mix_out, dsi_out, dsh_out = rest[10:15]
    sact_out, dsig_out, stat_out = rest[15:18]
    outs = rest[18:22]
    wsec, wblk, cat, bias, hid, mix, dsi, dsh, act, wide, turned, mask_ref, wsem, ssem, osem = rest[22:]
    chan = places[1]
    rows = sig0.shape[0]
    own = rows - 2 * HALO
    loads = weight_copies(places, pieces, wsec, wblk, wsem)
    for copy in loads:
        copy.start()
    fill_masks(ids_ref, mask_ref)
    pairs = ((sig0, edge0), (sig1, edge1), (sig2, edge2), (sig3, edge3))
    for k, (ref, edge) in enumerate(pairs):
        lanes = pl.ds(pl.multiple_of(128 * (chan ^ k), 128), 128)
        values = ref[0:own].astype(F32)
        s = sigmoid(values)
        a = values * s
        sact_out[0:own, lanes] = a.astype(BF16)
        dsig_out[:, lanes] = s + a * (1.0 - s)
        tile = edge_tile(chan, ref[own:rows].astype(F32), edge[0:16].astype(F32), 0)
        sact_out[own:rows, lanes] = (tile * sigmoid(tile)).astype(BF16)
    for copy in loads:
        copy.wait()

    def square(k, total):
        part = wsec[k].astype(F32)
        return total + jnp.sum((part * part).reshape(32, 8, 512), axis=0)

    total = lax.fori_loop(0, 16, square, jnp.zeros((8, 512), F32))
    norm = jnp.sqrt(jnp.sum(total, axis=0, keepdims=True) + EPSILON)
    scale = gain_ref[...] / norm
    stat_out[...] = jnp.concatenate([norm, scale, jnp.zeros((6, 512), F32)], axis=0)
    bias[...] = jnp.transpose(wblk[15].astype(F32))[:16]
    scaled = sact_out[...].astype(F32) * scale
    cat[0] = scaled.astype(BF16)
    cat[1] = (moved(scaled, -1) * doubled(doubled(mask_ref[0]))).astype(BF16)
    cat[2] = (moved(scaled, 1) * doubled(doubled(mask_ref[1]))).astype(BF16)

    def section(r, carry):
        total = nt(cat[0], wsec[r + 4]) + nt(cat[1 + r // 4], wsec[lax.rem(r + 12, 16)])
        hid[0, r] = (total + bias[0:1]).astype(BF16)
        return carry

    lax.fori_loop(0, 8, section, 0)

    def save(b, r, part, whole, out):
        pltpu.make_async_copy(part, whole, out).start()

    for b in range(3):
        dilate = 3**b

        def widen(p, carry):
            h = hid[b, p].astype(F32)
            s = sigmoid(h)
            a = h * s
            dsh[b, p] = (s + a * (1.0 - s)).astype(BF16)
            spread_phases(act, mask_ref, p, a, dilate)
            pltpu.make_async_copy(hid.at[b, p], hid_out.at[b, p], ssem).start()
            pltpu.make_async_copy(dsh.at[b, p], dsh_out.at[b, p], ssem).start()
            pltpu.make_async_copy(act.at[9 + p], act_out.at[b, p], osem).start()
            return carry

        lax.fori_loop(0, 8, widen, 0)

        def block(r, carry):
            inner = (
                nt(act[9 + r - dilate], wblk[5 * b])
                + nt(act[9 + r], wblk[5 * b + 1])
                + nt(act[9 + r + dilate], wblk[5 * b + 2])
                + bias[1 + b : 2 + b]
            )
            s = sigmoid(inner)
            m = inner * s
            mixed = m.astype(BF16)
            mix[b, r] = mixed
            dsi[b, r] = (s + m * (1.0 - s)).astype(BF16)
            pltpu.make_async_copy(mix.at[b, r], mix_out.at[b, r], ssem).start()
            pltpu.make_async_copy(dsi.at[b, r], dsi_out.at[b, r], ssem).start()
            after = nt(mixed, wblk[5 * b + 3]) + nt(hid[b, r], wblk[5 * b + 4])
            after = after + (bias[4 + b : 5 + b] + bias[7 + b : 8 + b])
            if b < 2:
                hid[b + 1, r] = after.astype(BF16)
            else:
                for half in range(2):
                    wide[half, pl.ds(r, own, stride=8), :] = after[:own, 128 * half : 128 * half + 128]
            return carry

        lax.fori_loop(0, 8, block, 0)
        for p in range(8):
            pltpu.make_async_copy(act.at[9 + p], act_out.at[b, p], osem).wait()

    def turn(q, carry):
        frames = pl.ds(pl.multiple_of(128 * q, 128), 128)
        for half in range(2):
            part = wide[half, frames, :]
            turned[128 * half : 128 * half + 128, frames] = jnp.transpose(part).astype(BF16)
        return carry

    lax.fori_loop(0, 8 * own // 128, turn, 0)
    final = []
    for k, out in enumerate(outs):
        part = turned.at[pl.ds(pl.multiple_of(64 * (chan ^ k), 64), 64), :]
        final.append(pltpu.make_async_copy(part, out, osem))
    for copy in final:
        copy.start()
    for source, out in ((hid, hid_out), (dsh, dsh_out), (mix, mix_out), (dsi, dsi_out)):
        for b in range(3):
            for p in range(8):
                pltpu.make_async_copy(source.at[b, p], out.at[b, p], ssem).wait()
    for copy in final:
        copy.wait()


def backward_kernel(
    places,
    cot0,
    cot1,
    cot2,
    cot3,
    edge0,
    edge1,
    edge2,
    edge3,
    ids_ref,
    sact_ref,
    dsig_ref,
    stat_ref,
    hid_in,
    act_in,
    mix_in,
    dsi_in,
    dsh_in,
    *rest,
):
    pieces = rest[:10]
    even_out, odd_out = rest[10:12]
    sgrads = rest[12:16]
    (wsec, wblk, turned, wide, grad, inner, both, act, dsi, dsh) = rest[16:26]
    (acc_one, acc_three, through, sums, staged, mask_ref, wsem, csem, bsem, osem) = rest[26:]
    turn_index, chan = places[0], places[1]
    rows = mask_ref.shape[1]
    own = rows - 2 * HALO

    loads = weight_copies(places, pieces, wsec, wblk, wsem)
    cots = []
    for k, ref in enumerate((cot0, cot1, cot2, cot3)):
        part = turned.at[pl.ds(pl.multiple_of(64 * (chan ^ k), 64), 64), :]
        cots.append(pltpu.make_async_copy(ref, part, csem))

    def kept(b):
        slot = b % 2
        return [
            pltpu.make_async_copy(mix_in.at[b, :, 0:own], both.at[slot, :, :, 0:256], bsem.at[slot]),
            pltpu.make_async_copy(hid_in.at[b, :, 0:own], both.at[slot, :, :, 256:512], bsem.at[slot]),
            pltpu.make_async_copy(act_in.at[b, :, 0:own], act.at[slot], bsem.at[slot]),
            pltpu.make_async_copy(dsi_in.at[b], dsi.at[slot], bsem.at[slot]),
            pltpu.make_async_copy(dsh_in.at[b], dsh.at[slot], bsem.at[slot]),
        ]

    for copy in cots + loads + kept(2) + kept(1):
        copy.start()
    fill_masks(ids_ref, mask_ref)
    for copy in cots:
        copy.wait()
    for k, edge in enumerate((edge0, edge1, edge2, edge3)):
        part = pl.ds(pl.multiple_of(64 * (chan ^ k), 64), 64)
        tile = turned[part, 8 * own : 8 * rows].astype(F32)
        tile = edge_tile(chan, tile, edge[16:80].astype(F32), 1)
        turned[part, 8 * own : 8 * rows] = tile.astype(BF16)

    def turn(q, carry):
        frames = pl.ds(pl.multiple_of(128 * q, 128), 128)
        for half in range(2):
            part = turned[128 * half : 128 * half + 128, frames].astype(F32)
            wide[half, frames, :] = jnp.transpose(part)
        return carry

    lax.fori_loop(0, 8 * rows // 128, turn, 0)

    def phases(r, carry):
        for half in range(2):
            part = wide[half, pl.ds(r, rows, stride=8), :]
            grad[r, :, 128 * half : 128 * half + 128] = part.astype(BF16)
        return carry

    lax.fori_loop(0, 8, phases, 0)
    for copy in loads:
        copy.wait()
    sums[...] = jnp.zeros_like(sums)

    def own_sum(values):
        return jnp.sum(values[:own].reshape(own // 8, 8, 256), axis=0)

    for b in (2, 1, 0):
        dilate = 3**b
        slot = b % 2
        for copy in kept(b):
            copy.wait()
        acc_one[...] = jnp.zeros_like(acc_one)
        acc_three[...] = jnp.zeros_like(acc_three)

        def first(r, carry):
            g = grad[r]
            down = nn(g, wblk[5 * b + 3])
            ig = down * dsi[slot, r].astype(F32)
            spread_phases(inner, mask_ref, r, ig, dilate)
            acc_one[...] += tn(g[:own], both[slot, r])
            sums[1 + b] += own_sum(ig)
            sums[4 + b] += own_sum(g.astype(F32))
            return carry

        lax.fori_loop(0, 8, first, 0)

        def second(r, carry):
            low, mid, high = inner[9 + r - dilate], inner[9 + r], inner[9 + r + dilate]
            deep = nn(high, wblk[5 * b]) + nn(mid, wblk[5 * b + 1]) + nn(low, wblk[5 * b + 2])
            back = nn(grad[r], wblk[5 * b + 4]) + dsh[slot, r].astype(F32) * deep
            grad[r] = back.astype(BF16)
            a = act[slot, r]
            acc_three[:, 0:256] += tn(a, high[:own])
            acc_three[:, 256:512] += tn(a, mid[:own])
            acc_three[:, 512:768] += tn(a, low[:own])
            return carry

        lax.fori_loop(0, 8, second, 0)
        for tap in range(3):
            part = jnp.transpose(acc_three[:, 256 * tap : 256 * tap + 256])
            staged[5 * b + tap, :, 512:768] = part.astype(BF16)
        staged[5 * b + 3, :, 512:768] = acc_one[:, 0:256].astype(BF16)
        staged[5 * b + 4, :, 512:768] = acc_one[:, 256:512].astype(BF16)
        if b == 2:
            for copy in kept(0):
                copy.start()

    def taps(r, carry):
        g = grad[r].astype(F32)
        sums[0] += own_sum(g)
        inner[r + 4] = grad[r]
        early = r < 4
        nearby = jnp.where(early, moved(g, 1), moved(g, -1))
        mask = jnp.where(early, mask_ref[1], mask_ref[0])
        inner[lax.rem(r + 12, 16)] = (nearby * doubled(mask)).astype(BF16)
        return carry

    lax.fori_loop(0, 8, taps, 0)
    through[...] = jnp.zeros_like(through)

    def collect(k, carry):
        through[...] += nn(inner[k, 0:own], wsec[k])
        return carry

    lax.fori_loop(0, 16, collect, 0)
    deep = through[...]
    sact = sact_ref[0:own]
    gains = jnp.sum(sact.astype(F32) * deep, axis=0, keepdims=True)
    signal_grad = deep * stat_ref[1:2] * dsig_ref[...]
    through[...] = signal_grad
    for k, out in enumerate(sgrads):
        lanes = pl.ds(pl.multiple_of(128 * (chan ^ k), 128), 128)
        out[...] = through[:, lanes].astype(BF16)
    biases = jnp.concatenate(
        [jnp.sum(sums[index], axis=0, keepdims=True) for index in range(8)]
        + [jnp.zeros((120, 256), F32)],
        axis=0,
    )
    staged[15, :, 512:640] = jnp.transpose(biases).astype(BF16)
    gain_rows = jnp.concatenate(
        [gains[:, 128 * q : 128 * q + 128] for q in range(4)] + [jnp.zeros((60, 128), F32)], axis=0
    ).astype(BF16)
    for part in range(4):
        staged[15, 64 * part : 64 * part + 64, 640:768] = gain_rows

    def finish(pair, carry):
        for tap in range(2):
            k = 2 * pair + tap
            staged[k, :, 0:512] = tn(inner[k, 0:own], sact).astype(BF16)
        place = pair ^ turn_index
        source = staged.at[pl.ds(2 * pair, 2)]

        @pl.when(lax.rem(place, 2) == 0)
        def _():
            pltpu.make_async_copy(source, even_out.at[place // 2], osem).start()

        @pl.when(lax.rem(place, 2) == 1)
        def _():
            pltpu.make_async_copy(source, odd_out.at[place // 2], osem).start()

        return carry

    lax.fori_loop(0, 8, finish, 0)
    for pair in range(8):
        pltpu.make_async_copy(staged.at[pl.ds(2 * pair, 2)], even_out.at[0], osem).wait()


def shape_of(shape, kind=BF16):
    return jax.ShapeDtypeStruct(shape, kind)


SPEC_VMEM = pl.BlockSpec(memory_space=pltpu.VMEM)
SPEC_ANY = pl.BlockSpec(memory_space=pl.ANY)
SPEC_SMEM = pl.BlockSpec(memory_space=pltpu.SMEM)


def params():
    return pltpu.CompilerParams(vmem_limit_bytes=VMEM_BYTES)


def cost(flops, moved_bytes):
    return pl.CostEstimate(flops=int(flops), bytes_accessed=int(moved_bytes), transcendentals=0)


def run_pack_weights(places, *arrays):
    return pl.pallas_call(
        pack_weights_kernel,
        out_shape=shape_of((2, 64, 768)),
        in_specs=[SPEC_SMEM] + [SPEC_VMEM] * 11,
        out_specs=SPEC_VMEM,
        scratch_shapes=[
            pltpu.VMEM((4, 1024, 128), F32),
            pltpu.VMEM((128, 128), F32),
            pltpu.VMEM((16, 64, 256), BF16),
        ],
        compiler_params=params(),
        cost_estimate=cost(2e7, 3e6),
        name="pack_weights",
    )(places, *arrays)


def run_pack_frames(places, piece, signal, cotangent):
    own = signal.shape[0] // 4
    rows = own + 2 * HALO
    out_shape = [shape_of((rows, 128))] * 4 + [shape_of((80, 128))] * 4
    out_shape = out_shape + [shape_of((64, 8 * rows))] * 4
    return pl.pallas_call(
        pack_frames_kernel,
        out_shape=out_shape,
        in_specs=[SPEC_SMEM, SPEC_ANY, SPEC_VMEM, SPEC_VMEM],
        out_specs=[SPEC_VMEM] * 12,
        compiler_params=params(),
        cost_estimate=cost(1e6, 6e6),
        name="pack_frames",
    )(places, piece, signal, cotangent)


def run_finish(places, v_section, three, v_mix, v_skip, g_dilated, g_mix, g_skip, stat, pieces):
    small = shape_of((3, 64), F32)
    out_shape = [
        shape_of((64, 16, 512), F32),
        shape_of((1, 512), F32),
        shape_of((1, 64), F32),
        shape_of((3, 3, 64, 256), F32),
        small,
        small,
        shape_of((3, 64, 256), F32),
        small,
        small,
        shape_of((3, 64, 256), F32),
        small,
        small,
    ]
    return pl.pallas_call(
        finish_kernel,
        out_shape=out_shape,
        in_specs=[SPEC_SMEM] + [SPEC_VMEM] * 18,
        out_specs=[SPEC_VMEM] * 12,
        scratch_shapes=[
            pltpu.VMEM((4, 1024, 128), F32),
            pltpu.VMEM((128, 128), F32),
            pltpu.VMEM((16, 64, 256), F32),
        ],
        compiler_params=params(),
        cost_estimate=cost(2e7, 8e6),
        name="finish_weights",
    )(places, v_section, three, v_mix, v_skip, g_dilated, g_mix, g_skip, stat, *pieces)


def run_forward(places, signals, edges, ids, gain, pieces):
    rows = signals[0].shape[0]
    own = rows - 2 * HALO
    kept = shape_of((3, 8, rows, 256))
    out_shape = [kept] * 5 + [
        shape_of((rows, 512)),
        shape_of((own, 512), F32),
        shape_of((8, 512), F32),
    ]
    out_shape = out_shape + [shape_of((64, 8 * own))] * 4
    return pl.pallas_call(
        forward_kernel,
        out_shape=out_shape,
        in_specs=[SPEC_SMEM] + [SPEC_VMEM] * 10 + [SPEC_ANY] * 10,
        out_specs=[SPEC_ANY] * 5 + [SPEC_VMEM] * 3 + [SPEC_ANY] * 4,
        scratch_shapes=[
            pltpu.VMEM((16, 256, 512), BF16),
            pltpu.VMEM((16, 256, 256), BF16),
            pltpu.VMEM((3, rows, 512), BF16),
            pltpu.VMEM((16, 256), F32),
            pltpu.VMEM((3, 8, rows, 256), BF16),
            pltpu.VMEM((3, 8, rows, 256), BF16),
            pltpu.VMEM((3, 8, rows, 256), BF16),
            pltpu.VMEM((3, 8, rows, 256), BF16),
            pltpu.VMEM((26, rows, 256), BF16),
            pltpu.VMEM((2, 8 * own, 128), F32),
            pltpu.VMEM((256, 8 * own), BF16),
            pltpu.VMEM((4, rows, 128), F32),
            pltpu.SemaphoreType.DMA,
            pltpu.SemaphoreType.DMA,
            pltpu.SemaphoreType.DMA,
        ],
        compiler_params=params(),
        cost_estimate=cost(2 * 1245184 * 8 * rows, 50e6),
        name="forward_blocks",
    )(places, *signals, *edges, ids, gain, *pieces)


def run_backward(places, cotangents, edges, ids, sact, dsig, stat, kept, pieces):
    rows = sact.shape[0]
    own = rows - 2 * HALO
    return pl.pallas_call(
        backward_kernel,
        out_shape=[shape_of((4, 2, 256, 768))] * 2 + [shape_of((own, 128))] * 4,
        in_specs=[SPEC_SMEM]
        + [SPEC_ANY] * 4
        + [SPEC_VMEM] * 8
        + [SPEC_ANY] * 5
        + [SPEC_ANY] * 10,
        out_specs=[SPEC_ANY] * 2 + [SPEC_VMEM] * 4,
        scratch_shapes=[
            pltpu.VMEM((16, 256, 512), BF16),
            pltpu.VMEM((16, 256, 256), BF16),
            pltpu.VMEM((256, 8 * rows), BF16),
            pltpu.VMEM((2, 8 * rows, 128), F32),
            pltpu.VMEM((8, rows, 256), BF16),
            pltpu.VMEM((26, rows, 256), BF16),
            pltpu.VMEM((2, 8, own, 512), BF16),
            pltpu.VMEM((2, 8, own, 256), BF16),
            pltpu.VMEM((2, 8, rows, 256), BF16),
            pltpu.VMEM((2, 8, rows, 256), BF16),
            pltpu.VMEM((256, 512), F32),
            pltpu.VMEM((256, 768), F32),
            pltpu.VMEM((own, 512), F32),
            pltpu.VMEM((8, 8, 256), F32),
            pltpu.VMEM((16, 256, 768), BF16),
            pltpu.VMEM((4, rows, 128), F32),
            pltpu.SemaphoreType.DMA,
            pltpu.SemaphoreType.DMA,
            pltpu.SemaphoreType.DMA((2,)),
            pltpu.SemaphoreType.DMA,
        ],
        compiler_params=params(),
        cost_estimate=cost(2 * 2490368 * 8 * rows, 60e6),
        name="backward_blocks",
    )(places, *cotangents, *edges, ids, sact, dsig, stat, *kept, *pieces)


def exchange(values, axis, cut):
    me = lax.axis_index(axis)
    parts = [cut(me)]
    for k in (1, 2, 3):
        parts.append(swap(cut(me ^ k), axis, k))
    return parts


def body(
    signal,
    segment_ids,
    v_section,
    g_section,
    b_section,
    v_dilated,
    g_dilated,
    b_dilated,
    v_mix,
    g_mix,
    b_mix,
    v_skip,
    g_skip,
    b_skip,
    cotangent,
):
    tm_index, chan = lax.axis_index("tm"), lax.axis_index("chan")
    tm_size = lax.axis_size("tm")
    turn = tm_index % 8
    places = jnp.stack([turn, chan]).astype(jnp.int32)
    own = signal.shape[0] // 4
    rows = own + 2 * HALO
    start = tm_index * signal.shape[0] + chan * own

    three_v = jnp.transpose(v_dilated, (0, 2, 1, 3))
    piece = run_pack_weights(
        places,
        v_section,
        three_v,
        v_mix,
        v_skip,
        b_section[None],
        b_dilated,
        b_mix,
        b_skip,
        g_dilated,
        g_mix,
        g_skip,
    )
    by_chan = [piece] + [swap(piece, "chan", k) for k in (1, 2, 3)]

    packed = run_pack_frames(places, piece, signal, cotangent)
    signals, edges, cotangents = list(packed[0:4]), list(packed[4:8]), list(packed[8:12])
    by_chan, _ = lax.optimization_barrier((by_chan, packed[0]))
    pieces = spread(jnp.stack(by_chan))
    for k in (1, 2, 3):
        signals[k] = swap(signals[k], "chan", k)
    for k in range(4):
        pairs = []
        for m in range(tm_size):
            if m > 0:
                pairs.append((4 * m + (3 ^ k), 4 * m - 1))
            if m < tm_size - 1:
                pairs.append((4 * m + k, 4 * m + 4))
        edges[k] = lax.ppermute(edges[k], ("tm", "chan"), pairs)
    for k in (1, 2, 3):
        cotangents[k] = swap(cotangents[k], "chan", k)
    padded = jnp.pad(segment_ids, 16, constant_values=-1)
    nearby = lax.dynamic_slice_in_dim(padded, start, own + 32)
    ids = jnp.broadcast_to(nearby[:, None], (own + 32, 128))

    frames = 8 * own
    results = run_forward(places, signals, edges, ids, g_section[None].astype(F32), pieces)
    kept, sact, dsig, stat, outs = results[:5], results[5], results[6], results[7], results[8:]

    received = [outs[0]] + [swap(outs[k], "chan", k) for k in (1, 2, 3)]
    results = run_backward(places, cotangents, edges, ids, sact, dsig, stat, kept, pieces)
    even, odd, sgrads = results[0], results[1], results[2:]
    odd, received = lax.optimization_barrier((odd, received))
    output = jnp.zeros((64, 4 * frames), BF16)
    for k in range(4):
        output = lax.dynamic_update_slice_in_dim(output, received[k], (chan ^ k) * frames, axis=1)

    quarter = even + swap(odd, "tm", 1)
    far_a = swap(quarter[3, :1], "tm", 2)
    far_b = swap(quarter[3, 1:], "tm", 4)
    for_y = jnp.concatenate([quarter[2, :1] + far_a, quarter[2, 1:]], axis=0)
    for_x = jnp.concatenate([quarter[1, :1], quarter[1, 1:] + far_b], axis=0)
    summed = quarter[0] + swap(for_x, "tm", 2) + swap(for_y, "tm", 4)

    def cut_rows(place):
        return lax.dynamic_slice_in_dim(summed, place * 64, 64, axis=1)

    parts = exchange(summed, "chan", cut_rows)
    mine = parts[0] + parts[1] + parts[2] + parts[3]
    bit = 8
    while bit < tm_size:
        mine = mine + swap(mine, "tm", bit)
        bit = 2 * bit
    gathered = spread(mine)

    received = [sgrads[0]] + [swap(sgrads[k], "chan", k) for k in (1, 2, 3)]
    signal_grad = jnp.zeros((4 * own, 128), BF16)
    for k in range(4):
        signal_grad = lax.dynamic_update_slice_in_dim(
            signal_grad, received[k], (chan ^ k) * own, axis=0
        )
    (sec, gain, bs, three, gt, bt, mix, gm, bm, skip, gk, bk) = run_finish(
        places, v_section, three_v, v_mix, v_skip, g_dilated, g_mix, g_skip, stat, gathered
    )
    return (
        output,
        signal_grad,
        sec,
        gain.reshape(512),
        bs.reshape(64),
        jnp.transpose(three, (0, 2, 1, 3)),
        gt,
        bt,
        mix,
        gm,
        bm,
        skip,
        gk,
        bk,
    )


def solution(mesh):
    return jax.shard_map(
        body,
        mesh=mesh,
        in_specs=(
            P("tm", "chan"),
            P(),
            P("chan", None, None),
            P(),
            P("chan"),
            P(None, "chan", None, None),
            P(None, "chan"),
            P(None, "chan"),
            P(None, "chan", None),
            P(None, "chan"),
            P(None, "chan"),
            P(None, "chan", None),
            P(None, "chan"),
            P(None, "chan"),
            P("chan", "tm"),
        ),
        out_specs=(
            P("chan", "tm"),
            P("tm", "chan"),
            P("chan", None, None),
            P(),
            P("chan"),
            P(None, "chan", None, None),
            P(None, "chan"),
            P(None, "chan"),
            P(None, "chan", None),
            P(None, "chan"),
            P(None, "chan"),
            P(None, "chan", None),
            P(None, "chan"),
            P(None, "chan"),
        ),
        check_vma=False,
    )
```

```python
import jax
import jax.numpy as jnp
from jax import lax
from jax.experimental import pallas as pl
from jax.experimental.pallas import tpu as pltpu
from jax.sharding import PartitionSpec as P

EPSILON = 1e-06
F32 = jnp.float32
BF16 = jnp.bfloat16
HALO = 8
EARLY = 4
VMEM_BYTES = 60 * 1024 * 1024


def xor_pairs(axis, bit):
    return [(i, i ^ bit) for i in range(lax.axis_size(axis))]


def swap(values, axis, bit):
    return lax.ppermute(values, axis, xor_pairs(axis, bit))


def spread(piece):
    half = piece.shape[0] // 2
    by_x = swap(piece, "tm", 2)
    by_y = swap(piece, "tm", 4)
    far_a = swap(by_y[:half], "tm", 2)
    far_b = swap(by_x[half:], "tm", 4)
    near = [piece, by_x, by_y, far_a, far_b]
    return near + [swap(entry, "tm", 1) for entry in near]


def gather_weights(column, signals):
    by_x = swap(column, "tm", 2)
    by_y = swap(column, "tm", 4)
    by_x, by_y, signals = lax.optimization_barrier((by_x, by_y, signals))
    far_a = swap(by_y[:2], "tm", 2)
    far_b = swap(by_x[2:], "tm", 4)
    near = lax.optimization_barrier([column, by_x, by_y, far_a, far_b])
    return near + [swap(entry, "tm", 1) for entry in near], signals


WEIGHT_PLACES = [(0, 0, 4), (2, 0, 4), (4, 0, 4), (6, 0, 2), (6, 2, 2)]
WEIGHT_PLACES = WEIGHT_PLACES + [(a + 1, first, count) for a, first, count in WEIGHT_PLACES]


SPREAD_PLACES = [(0, 0, 2), (2, 0, 2), (4, 0, 2), (6, 0, 1), (6, 1, 1)]
SPREAD_PLACES = SPREAD_PLACES + [(a + 1, first, count) for a, first, count in SPREAD_PLACES]


def nt(left, right):
    return lax.dot_general(left, right, (((1,), (1,)), ((), ())), preferred_element_type=F32)


def nn(left, right):
    return lax.dot_general(left, right, (((1,), (0,)), ((), ())), preferred_element_type=F32)


def tn(left, right):
    return lax.dot_general(left, right, (((0,), (0,)), ((), ())), preferred_element_type=F32)


def sigmoid(values):
    return 0.5 * jnp.tanh(0.5 * values) + 0.5


def silu_half(half):
    turn = jnp.tanh(half)
    product = half * turn
    return half + product, turn, product


def slope_twice(half, turn, product):
    return (1.0 + turn) + (half - product * turn)


def to_rows(flat, values, target):
    count = values.shape[0] // 16
    for group in range(16):
        start = group * (count + 1)
        flat[start : start + count] = values[group * count : group * count + count]
    for tile in range(count):
        part = flat[pl.ds(tile, 16, stride=count + 1)]
        target[16 * tile : 16 * tile + 16] = part.astype(BF16)


def fill_masks(ids_ref, flat, mask_ref):
    rows = mask_ref.shape[1]
    own = rows - 2 * HALO
    for index, step in enumerate((-1, 1, -2, 2)):
        inside = (ids_ref[16 : 8 + rows] == ids_ref[16 + step : 8 + rows + step]).astype(F32)
        before = (ids_ref[8:16] == ids_ref[8 + step : 16 + step]).astype(F32)
        to_rows(flat, inside[0:own], mask_ref.at[index])
        halo = jnp.concatenate([inside[own : own + 8], before], axis=0)
        mask_ref[index, own:rows] = halo.astype(BF16)


def masked_move(store, target, values, mask_ref, step):
    rows = values.shape[0]
    own = rows - 2 * HALO
    index = {-1: 0, 1: 1, -2: 2, 2: 3}[step]
    place = lax.broadcasted_iota(jnp.int32, (16, values.shape[1]), 0)

    def tile(number):
        return values[16 * number : 16 * number + 16].astype(F32)

    def turned(part, count):
        return pltpu.roll(part, count % 16, 0)

    count = own // 16
    halo = tile(count)
    size = abs(step)
    if step > 0:
        last = {}
        outer = turned(halo, -step)
        for n in range(step):
            inner_part = turned(tile(n), -1)
            last[count - step + n] = jnp.where(place == 15, turned(halo, -1 - n), inner_part)
            outer = jnp.where(place == 16 - step + n, turned(tile(n), n - step), outer)
        kept = (0, own - 16 * size, 16 * size)
    else:
        last = {}
        outer = turned(halo, size)
        for n in range(size):
            source = tile(count - size + n)
            last[n] = jnp.where(place == 0, turned(halo, size - n), turned(source, 1))
            outer = jnp.where(place == n, turned(source, n + 1), outer)
        kept = (16 * size, own, -16 * size)
    last[count] = outer
    wide = values.shape[1] // 128

    def masked(part, first):
        mask = mask_ref[index, first : first + part.shape[0]]
        return part * jnp.concatenate([mask] * wide, axis=1)

    first, end, offset = kept
    store[target, first:end] = masked(values[first + offset : end + offset], first)
    for number, part in last.items():
        store[target, 16 * number : 16 * number + 16] = masked(part.astype(BF16), 16 * number)


def move_far(store, mask_ref):
    masked_move(store, 0, store[16], mask_ref, -2)
    masked_move(store, 25, store[9], mask_ref, 2)


def move_near(store, mask_ref, dilate):
    def before(phase, carry):
        masked_move(store, 1 + phase, store[9 + phase], mask_ref, -1)
        return carry

    def after(phase, carry):
        masked_move(store, 17 + phase, store[9 + phase], mask_ref, 1)
        return carry

    lax.fori_loop(8 - dilate, 8, before, 0)
    lax.fori_loop(0, dilate, after, 0)


def move_each(store, mask_ref, phase, values):
    masked_move(store, 1 + phase, values, mask_ref, -1)
    masked_move(store, 17 + phase, values, mask_ref, 1)


def pack_weights_kernel(
    places, sec_ref, three_ref, mix_ref, skip_ref, bs, bt, bm, bk, gt, gm, gk, out, wide, rows, mats
):
    turn = places[0]
    for q in range(4):
        part = sec_ref[:, :, 128 * q : 128 * q + 128].astype(F32)
        wide[q] = part.reshape(1024, 128)
    rows[...] = jnp.zeros_like(rows)
    rows[0:1, 0:64] = bs[...].astype(F32)
    for index, ref in enumerate((bt, bm, bk, gt, gm, gk)):
        rows[1 + 3 * index : 4 + 3 * index, 0:64] = ref[...].astype(F32)
    columns = jnp.transpose(rows[...])[0:64]
    for b in range(3):
        three = three_ref[b].astype(F32)
        gain = columns[:, 10 + b : 11 + b]
        total = jnp.sum(jnp.sum(three * three, axis=0), axis=1, keepdims=True)
        scale = 0.5 * gain / jnp.sqrt(total + EPSILON)
        for tap in range(3):
            mats[5 * b + tap] = (three[tap] * scale).astype(BF16)
        for index, ref in ((3, mix_ref), (4, skip_ref)):
            part = ref[b].astype(F32)
            gain = columns[:, 3 * index + 4 + b : 3 * index + 5 + b]
            total = jnp.sum(part * part, axis=1, keepdims=True)
            gain = 0.5 * gain if index == 3 else gain
            mats[5 * b + index] = (part * (gain / jnp.sqrt(total + EPSILON))).astype(BF16)
    mats[15, :, 0:128] = columns.astype(BF16)
    mats[15, :, 128:256] = jnp.zeros((64, 128), BF16)
    for tap in range(2):
        for q in range(4):
            part = wide[q, pl.ds(2 * turn + tap, 64, stride=16), :]
            out[tap, :, 128 * q : 128 * q + 128] = part.astype(BF16)
        out[tap, :, 512:768] = mats[2 * turn + tap]


def pack_frames_kernel(places, low, high, signal, cotangent, *rest):
    firsts, seconds = rest[0:4], rest[4:8]
    chan = places[1]
    own = signal.shape[0] // 4
    frames = 8 * own
    count = own // 64
    row = lax.broadcasted_iota(jnp.int32, (16, 128), 0)
    lane = lax.broadcasted_iota(jnp.int32, (64, 128), 1)

    def halo(dest, after, before, edges, is_after):
        last, first = jnp.where(dest == 3, 1, 0), jnp.where(dest == 0, 1, 0)
        after = jnp.where(last == 1, edges[1].astype(F32), after.astype(F32))
        before = jnp.where(first == 1, edges[0].astype(F32), before.astype(F32))
        return jnp.where(is_after, after, before).astype(BF16)

    for k in range(4):
        dest = chan ^ k
        part = signal[pl.ds(pl.multiple_of(dest * own, own), own)]
        firsts[k][0:count] = part.reshape(count, 64, 128)
        after = pl.multiple_of(jnp.minimum(dest + 1, 3) * own, 16)
        before = pl.multiple_of(jnp.maximum(dest * own - 16, 0), 16)
        edges = (low[0:16], high[0:16])
        firsts[k][count] = jnp.zeros((64, 128), BF16)
        firsts[k][count, 0:16] = halo(
            dest, signal[pl.ds(after, 16)], signal[pl.ds(before, 16)], edges, row < HALO
        )
        for q in range(frames // 128):
            lanes = pl.ds(pl.multiple_of(dest * frames + 128 * q, 128), 128)
            part = cotangent[:, lanes]
            if q < EARLY:
                firsts[k][count + 1 + q] = part
            else:
                seconds[k][q - EARLY] = part
        after = pl.multiple_of(jnp.minimum(dest + 1, 3) * frames, 128)
        before = pl.multiple_of(jnp.maximum(dest * frames - 128, 0), 128)
        edges = (low[16:80], high[16:80])
        seconds[k][frames // 128 - EARLY] = halo(
            dest,
            cotangent[:, pl.ds(after, 128)],
            cotangent[:, pl.ds(before, 128)],
            edges,
            lane < 8 * HALO,
        )


def finish_kernel(places, sec_ref, three_ref, mix_ref, skip_ref, gt, gm, gk, stat, *rest):
    pieces = rest[:10]
    sec_out, gain_out, bs, three_out, gt_out, bt, mix_out, gm_out, bm, skip_out, gk_out, bk = rest[10:22]
    wide, rows, mats = rest[22:]
    turn = places[0]
    for ref, (place, first, _) in zip(pieces, SPREAD_PLACES, strict=True):
        pair = 2 * (turn ^ place)
        taps = 1 if place >= 6 else 2
        for tap in range(taps):
            k = pair + tap + first
            part = ref[tap].astype(F32)
            for q in range(4):
                wide[q, pl.ds(k, 64, stride=16), :] = part[:, 128 * q : 128 * q + 128]
            mats[k] = part[:, 512:768]
    aux = mats[15]
    norm, scale = stat[0:1], stat[1:2]
    gains = jnp.concatenate([aux[q : q + 1, 128:256] for q in range(4)], axis=1) / norm
    gain_out[...] = gains
    ratio = gains / norm
    for q in range(4):
        lanes = slice(128 * q, 128 * q + 128)
        part = sec_ref[:, :, lanes].astype(F32).reshape(1024, 128)
        grad = scale[:, lanes] * (wide[q] - ratio[:, lanes] * part)
        sec_out[:, :, lanes] = grad.reshape(64, 16, 128)
    rows[...] = jnp.zeros_like(rows)
    for index, ref in enumerate((gt, gm, gk)):
        rows[3 * index : 3 * index + 3, 0:64] = ref[...].astype(F32)
    columns = jnp.transpose(rows[...])[0:64]
    results = []
    for b in range(3):
        three = three_ref[b].astype(F32)
        norm = jnp.sqrt(jnp.sum(jnp.sum(three * three, axis=0), axis=1, keepdims=True) + EPSILON)
        total = mats[5 * b] * three[0] + mats[5 * b + 1] * three[1] + mats[5 * b + 2] * three[2]
        gain = jnp.sum(total, axis=1, keepdims=True) / norm
        results.append(gain)
        for tap in range(3):
            grad = mats[5 * b + tap] - gain / norm * three[tap]
            three_out[b, tap] = columns[:, b : b + 1] / norm * grad
    for index, (ref, out) in enumerate(((mix_ref, mix_out), (skip_ref, skip_out))):
        for b in range(3):
            part = ref[b].astype(F32)
            grad = mats[5 * b + 3 + index]
            norm = jnp.sqrt(jnp.sum(part * part, axis=1, keepdims=True) + EPSILON)
            gain = jnp.sum(grad * part, axis=1, keepdims=True) / norm
            results.append(gain)
            place = 3 + 3 * index + b
            out[b] = columns[:, place : place + 1] / norm * (grad - gain / norm * part)
    lane = lax.broadcasted_iota(jnp.int32, (64, 128), 1)
    table = jnp.where(lane < 7, aux[:, 0:128], 0.0)
    for index, gain in enumerate(results):
        table = jnp.where(lane == 8 + index, gain, table)
    rows[:, 0:64] = jnp.transpose(table)
    bs[...] = rows[0:1, 0:64]
    bt[...] = rows[1:4, 0:64]
    bm[...] = rows[4:7, 0:64]
    bk[...] = rows[4:7, 0:64]
    gt_out[...] = rows[8:11, 0:64]
    gm_out[...] = rows[11:14, 0:64]
    gk_out[...] = rows[14:17, 0:64]


def weight_copies(places, refs, wsec, wblk, sem, block_sem):
    turn, chan = places[0], places[1]
    copies = []
    for ref, (place, first, _) in zip(refs, WEIGHT_PLACES, strict=True):
        slots = pl.ds(2 * (turn ^ place), 2)
        for k in range(ref.shape[0]):
            rows = pl.ds(pl.multiple_of(64 * (chan ^ (first + k)), 64), 64)
            copies.append(
                pltpu.make_async_copy(
                    ref.at[k, :, :, 0:512], wsec.at[slots, rows, :], sem
                )
            )
            copies.append(
                pltpu.make_async_copy(
                    ref.at[k, :, :, 512:768], wblk.at[slots, rows, :], block_sem
                )
            )
    return copies


def forward_kernel(
    places,
    sig0,
    sig1,
    sig2,
    sig3,
    ids_ref,
    gain_ref,
    *rest,
):
    pieces, rest = rest[:10], rest[10:]
    hid_out, act_out, mix_out, dsi_out = rest[0:4]
    sact_out, mask_out, stat_out = rest[4:7]
    outs = rest[7:11]
    wsec, wblk, cat, bias, wide, turned, flat = rest[11:18]
    hids, mixs, dsis, acts = rest[18:21], rest[21:24], rest[24:27], rest[27:30]
    wsem, ssem = rest[30:]
    chan = places[1]
    rows = sact_out.shape[0]
    own = rows - 2 * HALO
    pitch = own // 2 + 1
    loads = weight_copies(places, pieces, wsec, wblk, wsem, wsem)
    for copy in loads:
        copy.start()
    fill_masks(ids_ref, flat, mask_out)
    for k, ref in enumerate((sig0, sig1, sig2, sig3)):
        lanes = pl.ds(pl.multiple_of(128 * (chan ^ k), 128), 128)
        values = silu_half(0.5 * ref[0 : own // 64].reshape(own, 128).astype(F32))[0]
        to_rows(flat, values, sact_out.at[:, lanes])
        halo = silu_half(0.5 * ref[own // 64, 0:16].astype(F32))[0]
        sact_out[own:rows, lanes] = halo.astype(BF16)
    for copy in loads:
        copy.wait()

    def square(k, total):
        part = wsec[k].astype(F32)
        return total + jnp.sum((part * part).reshape(32, 8, 512), axis=0)

    total = lax.fori_loop(0, 16, square, jnp.zeros((8, 512), F32))
    norm = jnp.sqrt(jnp.sum(total, axis=0, keepdims=True) + EPSILON)
    scale = gain_ref[...] / norm
    stat_out[...] = jnp.concatenate([norm, scale, jnp.zeros((6, 512), F32)], axis=0)
    bias[...] = 0.5 * jnp.transpose(wblk[15].astype(F32))[:16]
    cat[0] = (sact_out[...].astype(F32) * (0.5 * scale)).astype(BF16)
    masked_move(cat, 1, cat[0], mask_out, -1)
    masked_move(cat, 2, cat[0], mask_out, 1)
    saves = []

    def keep(source, out, b):
        copy = pltpu.make_async_copy(source, out.at[b], ssem)
        copy.start()
        saves.append(copy)

    def enter(b, r, half):
        hids[b][r] = half.astype(BF16)
        value = silu_half(half)[0].astype(BF16)
        acts[b][9 + r] = value
        if b == 2:
            move_each(acts[b], mask_out, r, value)

    def phase_rows(values, n):
        return values[n * rows : n * rows + rows]

    def section(q, carry):
        left = jnp.concatenate([cat[0], cat[1 + q // 4]], axis=1)
        right = jnp.concatenate([wsec[q + 4], wsec[lax.rem(q + 12, 16)]], axis=1)
        enter(0, q, nt(left, right) + bias[0:1])
        return carry

    lax.fori_loop(0, 8, section, 0)
    for b in range(3):
        dilate = 3**b
        act, mix, dsi, hid = acts[b], mixs[b], dsis[b], hids[b]
        if b < 2:
            move_near(act, mask_out, dilate)
        else:
            move_far(act, mask_out)
        keep(hid, hid_out, b)
        keep(act.at[9:17], act_out, b)

        def taps(q):
            left = []
            for r in (2 * q, 2 * q + 1):
                parts = [act[9 + r - dilate], act[9 + r], act[9 + r + dilate]]
                left.append(jnp.concatenate(parts, axis=1))
            right = jnp.concatenate([wblk[5 * b], wblk[5 * b + 1], wblk[5 * b + 2]], axis=1)
            inner = nt(jnp.concatenate(left, axis=0), right)
            for n in range(2):
                half = phase_rows(inner, n) + bias[1 + b : 2 + b]
                value, turn, product = silu_half(half)
                mix[2 * q + n] = value.astype(BF16)
                dsi[2 * q + n] = slope_twice(
                    half.astype(BF16), turn.astype(BF16), product.astype(BF16)
                )

        def blend(q):
            left = []
            for r in (2 * q, 2 * q + 1):
                left.append(jnp.concatenate([mix[r], hid[r]], axis=1))
            right = jnp.concatenate([wblk[5 * b + 3], wblk[5 * b + 4]], axis=1)
            total = nt(jnp.concatenate(left, axis=0), right)
            for n in range(2):
                r = 2 * q + n
                after = phase_rows(total, n) + (bias[4 + b : 5 + b] + bias[7 + b : 8 + b])
                if b < 2:
                    enter(b + 1, r, after)
                else:
                    for tile in range(own // 16):
                        part = 2.0 * after[16 * tile : 16 * tile + 16]
                        frames = pl.ds(8 * tile + r, 16, stride=pitch)
                        wide[0, frames, :] = part[:, 0:128]
                        wide[1, frames, :] = part[:, 128:256]

        def both(q, carry):
            blend(q - 1)
            taps(q)
            return carry

        taps(0)
        lax.fori_loop(1, 4, both, 0)
        blend(3)
        keep(mix, mix_out, b)
        keep(dsi, dsi_out, b)

    def turn(q, carry):
        start = pitch * (q // 2) + 128 * lax.rem(q, 2)
        frames = pl.ds(pl.multiple_of(128 * q, 128), 128)
        for half in range(2):
            part = jnp.transpose(wide[half, pl.ds(start, 128), :])
            turned[128 * half : 128 * half + 128, frames] = part.astype(BF16)
        return carry

    lax.fori_loop(0, 8 * own // 128, turn, 0, unroll=4)
    final = []
    for k, out in enumerate(outs):
        part = turned.at[pl.ds(pl.multiple_of(64 * (chan ^ k), 64), 64), :]
        final.append(pltpu.make_async_copy(part, out, wsem))
    for copy in final:
        copy.start()
    for copy in saves + final:
        copy.wait()


def backward_kernel(
    places,
    first0,
    first1,
    first2,
    first3,
    second0,
    second1,
    second2,
    second3,
    sact_ref,
    mask_ref,
    stat_ref,
    hid_in,
    act_in,
    mix_in,
    dsi_in,
    *rest,
):
    pieces, rest = rest[:10], rest[10:]
    even_out, odd_out = rest[0:2]
    sgrads = rest[2:6]
    (wsec, wblk, turned, sigs, wide, grad, inner_a, inner_b, mix, hid, act, dsi) = rest[6:18]
    (acc_one, acc_three, through, sums, staged, wsem, vsem, csem, bsem, osem) = rest[18:]
    pitch = 4 * (sact_ref.shape[0] - 2 * HALO) // 8 + 1
    turn_index, chan = places[0], places[1]
    rows = mask_ref.shape[1]
    own = rows - 2 * HALO

    loads = weight_copies(places, pieces, wsec, wblk, wsem, vsem)
    cots = []
    count = own // 64
    section_loads = []
    pairs = ((first0, second0), (first1, second1), (first2, second2), (first3, second3))
    for k, (one, two) in enumerate(pairs):
        part = pl.ds(pl.multiple_of(64 * (chan ^ k), 64), 64)
        early = one.at[count + 1 : count + 1 + EARLY]
        cots.append(pltpu.make_async_copy(early, turned.at[0:EARLY, part, :], csem))
        late = turned.at[EARLY : 8 * own // 128 + 1, part, :]
        cots.append(pltpu.make_async_copy(two, late, csem))
        section_loads.append(pltpu.make_async_copy(one.at[0:count], sigs.at[k], wsem))

    def kept(b):
        slot = b % 2
        return [
            pltpu.make_async_copy(dsi_in.at[b], dsi.at[slot], bsem.at[slot, 0]),
            pltpu.make_async_copy(mix_in.at[b, :, 0:own], mix.at[slot], bsem.at[slot, 1]),
            pltpu.make_async_copy(hid_in.at[b], hid.at[slot], bsem.at[slot, 2]),
            pltpu.make_async_copy(act_in.at[b, :, 0:own], act.at[slot], bsem.at[slot, 3]),
        ]

    block_loads, section_loads = loads[1::2], loads[0::2] + section_loads
    for copy in cots + block_loads + kept(2) + kept(1) + section_loads:
        copy.start()
    sums[...] = jnp.zeros_like(sums)
    for copy in cots:
        copy.wait()
    def turn(q, carry):
        start = pitch * (q // 2) + 128 * lax.rem(q, 2)
        for half in range(2):
            part = turned[q, 128 * half : 128 * half + 128].astype(F32)
            wide[half, pl.ds(start, 128), :] = jnp.transpose(part)
        return carry

    lax.fori_loop(0, 8 * own // 128, turn, 0, unroll=4)
    turn(8 * own // 128, 0)

    def phases(r, carry):
        for half in range(2):
            lanes = slice(128 * half, 128 * half + 128)
            for tile in range(own // 16):
                part = wide[half, pl.ds(8 * tile + r, 16, stride=pitch), :]
                grad[r, 16 * tile : 16 * tile + 16, lanes] = part.astype(BF16)
            part = wide[half, pl.ds(16 * pitch + r, 16, stride=8), :]
            grad[r, own:rows, lanes] = part.astype(BF16)
        return carry

    lax.fori_loop(0, 8, phases, 0)
    for copy in block_loads:
        copy.wait()

    def own_sum(values):
        return jnp.sum(values[:own].astype(F32).reshape(own // 8, 8, 256), axis=0)

    def two(store, q, count):
        return jnp.concatenate([store[2 * q, 0:count], store[2 * q + 1, 0:count]], axis=0)

    def enter(b, inner, q):
        slot = b % 2
        g = two(grad, q, rows)
        down = nn(g, wblk[5 * b + 3])
        kept_rows = jnp.concatenate([mix[slot, 2 * q], mix[slot, 2 * q + 1]], axis=0)
        hidden = jnp.concatenate([hid[slot, 2 * q, 0:own], hid[slot, 2 * q + 1, 0:own]], axis=0)
        both = jnp.concatenate([kept_rows, hidden], axis=1)
        acc_one[...] += tn(two(grad, q, own), both)
        for n in range(2):
            r = 2 * q + n
            part = down[n * rows : n * rows + rows] * dsi[slot, r].astype(F32)
            part = part.astype(BF16)
            inner[9 + r] = part
            if b == 2:
                move_each(inner, mask_ref, r, part)

    def through_taps(b, inner, q):
        dilate, slot = 3**b, b % 2
        waves = []
        for r in (2 * q, 2 * q + 1):
            parts = [inner[9 + r + dilate], inner[9 + r], inner[9 + r - dilate]]
            waves.append(jnp.concatenate(parts, axis=1))
            sums[1 + b] += own_sum(parts[1])
            sums[4 + b] += own_sum(grad[r])
        deep = nn(jnp.concatenate(waves, axis=0), wblk[5 * b : 5 * b + 3].reshape(768, 256))
        skip = nn(two(grad, q, rows), wblk[5 * b + 4])
        acts = jnp.concatenate([act[slot, 2 * q], act[slot, 2 * q + 1]], axis=0)
        acc_three[...] += tn(jnp.concatenate([wave[:own] for wave in waves], axis=0), acts)
        for n in range(2):
            part = slice(n * rows, n * rows + rows)
            half = hid[slot, 2 * q + n].astype(F32)
            back = skip[part] + slope_twice(half, *silu_half(half)[1:]) * deep[part]
            grad[2 * q + n] = back.astype(BF16)

    def stage_taps(b):
        for tap in range(3):
            part = acc_three[256 * tap : 256 * tap + 256, :]
            staged[5 * b + tap, :, 512:768] = part.astype(BF16)
        acc_three[...] = jnp.zeros_like(acc_three)

    def stage_points(b):
        staged[5 * b + 3, :, 512:768] = acc_one[:, 0:256].astype(BF16)
        staged[5 * b + 4, :, 512:768] = (2.0 * acc_one[:, 256:512]).astype(BF16)
        acc_one[...] = jnp.zeros_like(acc_one)

    def arrive(b, numbers):
        for number in numbers:
            kept(b)[number].wait()

    def taps(r):
        g = grad[r]
        sums[0] += own_sum(g)
        last[r + 4] = g

        @pl.when(r < 4)
        def _():
            masked_move(last, r + 12, grad[r], mask_ref, 1)

        @pl.when(r >= 4)
        def _():
            masked_move(last, r - 4, grad[r], mask_ref, -1)

    acc_one[...] = jnp.zeros_like(acc_one)
    acc_three[...] = jnp.zeros_like(acc_three)
    arrive(2, (0, 1, 2))

    def enter_last(q, carry):
        enter(2, inner_a, q)
        return carry

    lax.fori_loop(0, 4, enter_last, 0)
    stage_points(2)
    move_far(inner_a, mask_ref)
    arrive(2, (3,))
    arrive(1, (0, 1, 2))
    for b, inner, following in ((2, inner_a, inner_b), (1, inner_b, inner_a)):

        def pipelined(q, carry):
            through_taps(b, inner, q)
            enter(b - 1, following, q - 1)
            return carry

        through_taps(b, inner, 0)
        lax.fori_loop(1, 4, pipelined, 0)
        enter(b - 1, following, 3)
        stage_taps(b)
        stage_points(b - 1)
        move_near(following, mask_ref, 3 ** (b - 1))
        if b == 2:
            for copy in kept(0):
                copy.start()
            arrive(1, (3,))
            arrive(0, (0, 1, 2))
        else:
            arrive(0, (3,))
    last = inner_b

    def final(q, carry):
        through_taps(0, inner_a, q)
        return carry

    lax.fori_loop(0, 4, final, 0)
    stage_taps(0)

    def section_taps(r, carry):
        taps(r)
        return carry

    lax.fori_loop(0, 8, section_taps, 0)
    for copy in section_loads:
        copy.wait()
    through[...] = jnp.zeros_like(through)
    sact = sact_ref[0:own]

    def collect(q, carry):
        left = jnp.concatenate([last[2 * q, 0:own], last[2 * q + 1, 0:own]], axis=1)
        through[...] += nn(left, wsec[pl.ds(2 * q, 2)].reshape(512, 512))
        grads = tn(left, sact).astype(BF16)
        staged[2 * q, :, 0:512] = grads[0:256]
        staged[2 * q + 1, :, 0:512] = grads[256:512]
        return carry

    lax.fori_loop(0, 8, collect, 0)
    deep = through[...]
    gains = jnp.sum(sact.astype(F32) * deep, axis=0, keepdims=True)
    through[...] = deep * (0.5 * stat_ref[1:2])
    biases = jnp.concatenate(
        [jnp.sum(sums[index], axis=0, keepdims=True) for index in range(8)]
        + [jnp.zeros((120, 256), F32)],
        axis=0,
    )
    staged[15, :, 512:640] = jnp.transpose(biases).astype(BF16)
    gain_rows = jnp.concatenate(
        [gains[:, 128 * q : 128 * q + 128] for q in range(4)] + [jnp.zeros((60, 128), F32)], axis=0
    ).astype(BF16)
    for part in range(4):
        staged[15, 64 * part : 64 * part + 64, 640:768] = gain_rows

    def finish(pair, carry):
        place = pair ^ turn_index
        source = staged.at[pl.ds(2 * pair, 2)]

        @pl.when(lax.rem(place, 2) == 0)
        def _():
            pltpu.make_async_copy(source, even_out.at[place // 2], osem).start()

        @pl.when(lax.rem(place, 2) == 1)
        def _():
            pltpu.make_async_copy(source, odd_out.at[place // 2], osem).start()

        return carry

    lax.fori_loop(0, 8, finish, 0)
    for k, out in enumerate(sgrads):
        lanes = pl.ds(pl.multiple_of(128 * (chan ^ k), 128), 128)
        half = 0.5 * sigs[k].reshape(own, 128).astype(F32)
        slope = slope_twice(half, *silu_half(half)[1:])
        count = own // 16
        for tile in range(count):
            part = through[16 * tile : 16 * tile + 16, lanes]
            wide[0, pl.ds(tile, 16, stride=count + 1), :] = part
        groups = [wide[0, (count + 1) * n : (count + 1) * n + count, :] for n in range(16)]
        out[...] = (jnp.concatenate(groups, axis=0) * slope).astype(BF16)
    for pair in range(8):
        pltpu.make_async_copy(staged.at[pl.ds(2 * pair, 2)], even_out.at[0], osem).wait()


def shape_of(shape, kind=BF16):
    return jax.ShapeDtypeStruct(shape, kind)


SPEC_VMEM = pl.BlockSpec(memory_space=pltpu.VMEM)
SPEC_ANY = pl.BlockSpec(memory_space=pl.ANY)
SPEC_SMEM = pl.BlockSpec(memory_space=pltpu.SMEM)


def params():
    return pltpu.CompilerParams(vmem_limit_bytes=VMEM_BYTES)


def cost(flops, moved_bytes):
    return pl.CostEstimate(flops=int(flops), bytes_accessed=int(moved_bytes), transcendentals=0)


def run_pack_weights(places, *arrays):
    return pl.pallas_call(
        pack_weights_kernel,
        out_shape=shape_of((2, 64, 768)),
        in_specs=[SPEC_SMEM] + [SPEC_VMEM] * 11,
        out_specs=SPEC_VMEM,
        scratch_shapes=[
            pltpu.VMEM((4, 1024, 128), F32),
            pltpu.VMEM((128, 128), F32),
            pltpu.VMEM((16, 64, 256), BF16),
        ],
        compiler_params=params(),
        cost_estimate=cost(2e7, 3e6),
        name="pack_weights",
    )(places, *arrays)


def run_pack_frames(places, low, high, signal, cotangent):
    own = signal.shape[0] // 4
    return pl.pallas_call(
        pack_frames_kernel,
        out_shape=[shape_of((own // 64 + 1 + EARLY, 64, 128))] * 4
        + [shape_of((8 * own // 128 + 1 - EARLY, 64, 128))] * 4,
        in_specs=[SPEC_SMEM] + [SPEC_VMEM] * 4,
        out_specs=[SPEC_VMEM] * 8,
        compiler_params=params(),
        cost_estimate=cost(1e6, 6e6),
        name="pack_frames",
    )(places, low, high, signal, cotangent)


def run_finish(places, v_section, three, v_mix, v_skip, g_dilated, g_mix, g_skip, stat, pieces):
    small = shape_of((3, 64), F32)
    out_shape = [
        shape_of((64, 16, 512), F32),
        shape_of((1, 512), F32),
        shape_of((1, 64), F32),
        shape_of((3, 3, 64, 256), F32),
        small,
        small,
        shape_of((3, 64, 256), F32),
        small,
        small,
        shape_of((3, 64, 256), F32),
        small,
        small,
    ]
    return pl.pallas_call(
        finish_kernel,
        out_shape=out_shape,
        in_specs=[SPEC_SMEM] + [SPEC_VMEM] * 18,
        out_specs=[SPEC_VMEM] * 12,
        scratch_shapes=[
            pltpu.VMEM((4, 1024, 128), F32),
            pltpu.VMEM((128, 128), F32),
            pltpu.VMEM((16, 64, 256), F32),
        ],
        compiler_params=params(),
        cost_estimate=cost(2e7, 8e6),
        name="finish_weights",
    )(places, v_section, three, v_mix, v_skip, g_dilated, g_mix, g_skip, stat, *pieces)


def run_forward(places, firsts, ids, gain, pieces):
    own = ids.shape[0] - 32
    rows = own + 2 * HALO
    kept = shape_of((3, 8, rows, 256))
    out_shape = [kept] * 4 + [
        shape_of((rows, 512)),
        shape_of((4, rows, 128)),
        shape_of((8, 512), F32),
    ]
    out_shape = out_shape + [shape_of((64, 8 * own))] * 4
    return pl.pallas_call(
        forward_kernel,
        out_shape=out_shape,
        in_specs=[SPEC_SMEM] + [SPEC_VMEM] * 6 + [SPEC_ANY] * 10,
        out_specs=[SPEC_ANY] * 4 + [SPEC_VMEM] * 3 + [SPEC_ANY] * 4,
        scratch_shapes=[
            pltpu.VMEM((16, 256, 512), BF16),
            pltpu.VMEM((16, 256, 256), BF16),
            pltpu.VMEM((3, rows, 512), BF16),
            pltpu.VMEM((16, 256), F32),
            pltpu.VMEM((2, 16 * (own // 2 + 1), 128), F32),
            pltpu.VMEM((256, 8 * own), BF16),
            pltpu.VMEM((own + 16, 128), F32),
        ]
        + [pltpu.VMEM((8, rows, 256), BF16)] * 9
        + [pltpu.VMEM((26, rows, 256), BF16)] * 3
        + [pltpu.SemaphoreType.DMA, pltpu.SemaphoreType.DMA],
        compiler_params=params(),
        cost_estimate=cost(2 * 1245184 * 8 * rows, 50e6),
        name="forward_blocks",
    )(places, *firsts, ids, gain, *pieces)


def run_backward(places, firsts, seconds, sact, masks, stat, kept, pieces):
    rows = sact.shape[0]
    own = rows - 2 * HALO
    return pl.pallas_call(
        backward_kernel,
        out_shape=[shape_of((4, 2, 256, 768))] * 2 + [shape_of((own, 128))] * 4,
        in_specs=[SPEC_SMEM]
        + [SPEC_ANY] * 8
        + [SPEC_VMEM] * 3
        + [SPEC_ANY] * 14,
        out_specs=[SPEC_ANY] * 2 + [SPEC_VMEM] * 4,
        scratch_shapes=[
            pltpu.VMEM((16, 256, 512), BF16),
            pltpu.VMEM((16, 256, 256), BF16),
            pltpu.VMEM((8 * own // 128 + 1, 256, 128), BF16),
            pltpu.VMEM((4, own // 64, 64, 128), BF16),
            pltpu.VMEM((2, 16 * (own // 2 + 1) + 128, 128), F32),
            pltpu.VMEM((8, rows, 256), BF16),
            pltpu.VMEM((26, rows, 256), BF16),
            pltpu.VMEM((26, rows, 256), BF16),
            pltpu.VMEM((2, 8, own, 256), BF16),
            pltpu.VMEM((2, 8, rows, 256), BF16),
            pltpu.VMEM((2, 8, own, 256), BF16),
            pltpu.VMEM((2, 8, rows, 256), BF16),
            pltpu.VMEM((256, 512), F32),
            pltpu.VMEM((768, 256), F32),
            pltpu.VMEM((own, 512), F32),
            pltpu.VMEM((8, 8, 256), F32),
            pltpu.VMEM((16, 256, 768), BF16),
            pltpu.SemaphoreType.DMA,
            pltpu.SemaphoreType.DMA,
            pltpu.SemaphoreType.DMA,
            pltpu.SemaphoreType.DMA((2, 4)),
            pltpu.SemaphoreType.DMA,
        ],
        compiler_params=params(),
        cost_estimate=cost(2 * 2490368 * 8 * rows, 60e6),
        name="backward_blocks",
    )(places, *firsts, *seconds, sact, masks, stat, *kept, *pieces)


def exchange(values, axis, cut):
    me = lax.axis_index(axis)
    parts = [cut(me)]
    for k in (1, 2, 3):
        parts.append(swap(cut(me ^ k), axis, k))
    return parts


def body(
    signal,
    segment_ids,
    v_section,
    g_section,
    b_section,
    v_dilated,
    g_dilated,
    b_dilated,
    v_mix,
    g_mix,
    b_mix,
    v_skip,
    g_skip,
    b_skip,
    cotangent,
):
    tm_index, chan = lax.axis_index("tm"), lax.axis_index("chan")
    tm_size = lax.axis_size("tm")
    turn = tm_index % 8
    places = jnp.stack([turn, chan]).astype(jnp.int32)
    own = signal.shape[0] // 4
    rows = own + 2 * HALO
    start = tm_index * signal.shape[0] + chan * own

    three_v = jnp.transpose(v_dilated, (0, 2, 1, 3))
    piece = run_pack_weights(
        places,
        v_section,
        three_v,
        v_mix,
        v_skip,
        b_section[None],
        b_dilated,
        b_mix,
        b_skip,
        g_dilated,
        g_mix,
        g_skip,
    )
    by_chan = [piece] + [swap(piece, "chan", k) for k in (1, 2, 3)]

    first = jnp.concatenate([signal[:16], cotangent[:, :128]], axis=0)
    final = jnp.concatenate([signal[-16:], cotangent[:, -128:]], axis=0)
    onward = [(i, i + 1) for i in range(tm_size - 1)]
    low = lax.ppermute(final, "tm", onward)
    high = lax.ppermute(first, "tm", [(target, source) for source, target in onward])
    packed = run_pack_frames(places, low, high, signal, cotangent)
    firsts, seconds = list(packed[0:4]), list(packed[4:8])
    by_chan, _ = lax.optimization_barrier((by_chan, packed[0]))
    for k in (1, 2, 3):
        firsts[k] = swap(firsts[k], "chan", k)
        seconds[k] = swap(seconds[k], "chan", k)
    pieces, firsts = gather_weights(jnp.stack(by_chan), firsts)
    firsts, seconds[1:3] = lax.optimization_barrier((firsts, seconds[1:3]))
    padded = jnp.pad(segment_ids, 16, constant_values=-1)
    nearby = lax.dynamic_slice_in_dim(padded, start, own + 32)
    ids = jnp.broadcast_to(nearby[:, None], (own + 32, 128))

    frames = 8 * own
    results = run_forward(places, firsts, ids, g_section[None].astype(F32), pieces)
    kept, sact, masks, stat, outs = results[:4], results[4], results[5], results[6], results[7:]

    outs, seconds = lax.optimization_barrier((list(outs), seconds))
    received = [outs[0]] + [swap(outs[k], "chan", k) for k in (1, 2, 3)]
    results = run_backward(places, firsts, seconds, sact, masks, stat, kept, pieces)
    even, odd, sgrads = results[0], results[1], results[2:]
    odd, received = lax.optimization_barrier((odd, received))
    output = jnp.zeros((64, 4 * frames), BF16)
    for k in range(4):
        output = lax.dynamic_update_slice_in_dim(output, received[k], (chan ^ k) * frames, axis=1)

    quarter = even + swap(odd, "tm", 1)
    far_a = swap(quarter[3, :1], "tm", 2)
    far_b = swap(quarter[3, 1:], "tm", 4)
    for_y = jnp.concatenate([quarter[2, :1] + far_a, quarter[2, 1:]], axis=0)
    for_x = jnp.concatenate([quarter[1, :1], quarter[1, 1:] + far_b], axis=0)
    summed = quarter[0] + swap(for_x, "tm", 2) + swap(for_y, "tm", 4)

    def cut_rows(place):
        return lax.dynamic_slice_in_dim(summed, place * 64, 64, axis=1)

    parts = exchange(summed, "chan", cut_rows)
    mine = parts[0] + parts[1] + parts[2] + parts[3]
    bit = 8
    while bit < tm_size:
        mine = mine + swap(mine, "tm", bit)
        bit = 2 * bit
    gathered = spread(mine)

    received = [sgrads[0]] + [swap(sgrads[k], "chan", k) for k in (1, 2, 3)]
    signal_grad = jnp.zeros((4 * own, 128), BF16)
    for k in range(4):
        signal_grad = lax.dynamic_update_slice_in_dim(
            signal_grad, received[k], (chan ^ k) * own, axis=0
        )
    (sec, gain, bs, three, gt, bt, mix, gm, bm, skip, gk, bk) = run_finish(
        places, v_section, three_v, v_mix, v_skip, g_dilated, g_mix, g_skip, stat, gathered
    )
    return (
        output,
        signal_grad,
        sec,
        gain.reshape(512),
        bs.reshape(64),
        jnp.transpose(three, (0, 2, 1, 3)),
        gt,
        bt,
        mix,
        gm,
        bm,
        skip,
        gk,
        bk,
    )


def solution(mesh):
    return jax.shard_map(
        body,
        mesh=mesh,
        in_specs=(
            P("tm", "chan"),
            P(),
            P("chan", None, None),
            P(),
            P("chan"),
            P(None, "chan", None, None),
            P(None, "chan"),
            P(None, "chan"),
            P(None, "chan", None),
            P(None, "chan"),
            P(None, "chan"),
            P(None, "chan", None),
            P(None, "chan"),
            P(None, "chan"),
            P("chan", "tm"),
        ),
        out_specs=(
            P("chan", "tm"),
            P("tm", "chan"),
            P("chan", None, None),
            P(),
            P("chan"),
            P(None, "chan", None, None),
            P(None, "chan"),
            P(None, "chan"),
            P(None, "chan", None),
            P(None, "chan"),
            P(None, "chan"),
            P(None, "chan", None),
            P(None, "chan"),
            P(None, "chan"),
        ),
        check_vma=False,
    )
```

```python
import jax
import jax.numpy as jnp
from jax import lax
from jax.experimental import pallas as pl
from jax.experimental.pallas import tpu as pltpu
from jax.sharding import PartitionSpec as P

EPSILON = 1e-06
F32 = jnp.float32
BF16 = jnp.bfloat16
HALO = 8
EARLY = 4
VMEM_BYTES = 60 * 1024 * 1024


def xor_pairs(axis, bit):
    return [(i, i ^ bit) for i in range(lax.axis_size(axis))]


def swap(values, axis, bit):
    return lax.ppermute(values, axis, xor_pairs(axis, bit))


def spread(piece):
    half = piece.shape[0] // 2
    by_x = swap(piece, "tm", 2)
    by_y = swap(piece, "tm", 4)
    far_a = swap(by_y[:half], "tm", 2)
    far_b = swap(by_x[half:], "tm", 4)
    near = [piece, by_x, by_y, far_a, far_b]
    return near + [swap(entry, "tm", 1) for entry in near]


def gather_weights(column, signals):
    by_x = swap(column, "tm", 2)
    by_y = swap(column, "tm", 4)
    by_x, by_y, signals = lax.optimization_barrier((by_x, by_y, signals))
    far_a = swap(by_y[:2], "tm", 2)
    far_b = swap(by_x[2:], "tm", 4)
    near = lax.optimization_barrier([column, by_x, by_y, far_a, far_b])
    return near + [swap(entry, "tm", 1) for entry in near], signals


WEIGHT_PLACES = [(0, 0, 4), (2, 0, 4), (4, 0, 4), (6, 0, 2), (6, 2, 2)]
WEIGHT_PLACES = WEIGHT_PLACES + [(a + 1, first, count) for a, first, count in WEIGHT_PLACES]


SPREAD_PLACES = [(0, 0, 2), (2, 0, 2), (4, 0, 2), (6, 0, 1), (6, 1, 1)]
SPREAD_PLACES = SPREAD_PLACES + [(a + 1, first, count) for a, first, count in SPREAD_PLACES]


def nt(left, right):
    return lax.dot_general(left, right, (((1,), (1,)), ((), ())), preferred_element_type=F32)


def nn(left, right):
    return lax.dot_general(left, right, (((1,), (0,)), ((), ())), preferred_element_type=F32)


def tn(left, right):
    return lax.dot_general(left, right, (((0,), (0,)), ((), ())), preferred_element_type=F32)


def sigmoid(values):
    return 0.5 * jnp.tanh(0.5 * values) + 0.5


def silu_half(half):
    turn = jnp.tanh(half)
    product = half * turn
    return half + product, turn, product


def slope_twice(half, turn, product):
    return (1.0 + turn) + (half - product * turn)


def to_rows(flat, values, target):
    count = values.shape[0] // 16
    for group in range(16):
        start = group * (count + 1)
        flat[start : start + count] = values[group * count : group * count + count]
    for tile in range(count):
        part = flat[pl.ds(tile, 16, stride=count + 1)]
        target[16 * tile : 16 * tile + 16] = part.astype(BF16)


def fill_masks(ids_ref, flat, mask_ref):
    rows = mask_ref.shape[1]
    own = rows - 2 * HALO
    for index, step in enumerate((-1, 1, -2, 2)):
        inside = (ids_ref[16 : 8 + rows] == ids_ref[16 + step : 8 + rows + step]).astype(F32)
        before = (ids_ref[8:16] == ids_ref[8 + step : 16 + step]).astype(F32)
        to_rows(flat, inside[0:own], mask_ref.at[index])
        halo = jnp.concatenate([inside[own : own + 8], before], axis=0)
        mask_ref[index, own:rows] = halo.astype(BF16)


def masked_move(store, target, values, mask_ref, step):
    rows = values.shape[0]
    own = rows - 2 * HALO
    index = {-1: 0, 1: 1, -2: 2, 2: 3}[step]
    place = lax.broadcasted_iota(jnp.int32, (16, values.shape[1]), 0)

    def tile(number):
        return values[16 * number : 16 * number + 16].astype(F32)

    def turned(part, count):
        return pltpu.roll(part, count % 16, 0)

    count = own // 16
    halo = tile(count)
    size = abs(step)
    if step > 0:
        last = {}
        outer = turned(halo, -step)
        for n in range(step):
            inner_part = turned(tile(n), -1)
            last[count - step + n] = jnp.where(place == 15, turned(halo, -1 - n), inner_part)
            outer = jnp.where(place == 16 - step + n, turned(tile(n), n - step), outer)
        kept = (0, own - 16 * size, 16 * size)
    else:
        last = {}
        outer = turned(halo, size)
        for n in range(size):
            source = tile(count - size + n)
            last[n] = jnp.where(place == 0, turned(halo, size - n), turned(source, 1))
            outer = jnp.where(place == n, turned(source, n + 1), outer)
        kept = (16 * size, own, -16 * size)
    last[count] = outer
    wide = values.shape[1] // 128

    def masked(part, first):
        mask = mask_ref[index, first : first + part.shape[0]]
        return part * jnp.concatenate([mask] * wide, axis=1)

    first, end, offset = kept
    store[target, first:end] = masked(values[first + offset : end + offset], first)
    for number, part in last.items():
        store[target, 16 * number : 16 * number + 16] = masked(part.astype(BF16), 16 * number)


def move_far(store, mask_ref):
    masked_move(store, 0, store[16], mask_ref, -2)
    masked_move(store, 25, store[9], mask_ref, 2)


def move_near(store, mask_ref, dilate):
    def before(phase, carry):
        masked_move(store, 1 + phase, store[9 + phase], mask_ref, -1)
        return carry

    def after(phase, carry):
        masked_move(store, 17 + phase, store[9 + phase], mask_ref, 1)
        return carry

    lax.fori_loop(8 - dilate, 8, before, 0)
    lax.fori_loop(0, dilate, after, 0)


def move_each(store, mask_ref, phase, values):
    masked_move(store, 1 + phase, values, mask_ref, -1)
    masked_move(store, 17 + phase, values, mask_ref, 1)


def pack_weights_kernel(
    places, sec_ref, three_ref, mix_ref, skip_ref, bs, bt, bm, bk, gt, gm, gk, out, wide, rows, mats
):
    turn = places[0]
    for q in range(4):
        part = sec_ref[:, :, 128 * q : 128 * q + 128].astype(F32)
        wide[q] = part.reshape(1024, 128)
    rows[...] = jnp.zeros_like(rows)
    rows[0:1, 0:64] = bs[...].astype(F32)
    for index, ref in enumerate((bt, bm, bk, gt, gm, gk)):
        rows[1 + 3 * index : 4 + 3 * index, 0:64] = ref[...].astype(F32)
    columns = jnp.transpose(rows[...])[0:64]
    for b in range(3):
        three = three_ref[b].astype(F32)
        gain = columns[:, 10 + b : 11 + b]
        total = jnp.sum(jnp.sum(three * three, axis=0), axis=1, keepdims=True)
        scale = 0.5 * gain / jnp.sqrt(total + EPSILON)
        for tap in range(3):
            mats[5 * b + tap] = (three[tap] * scale).astype(BF16)
        for index, ref in ((3, mix_ref), (4, skip_ref)):
            part = ref[b].astype(F32)
            gain = columns[:, 3 * index + 4 + b : 3 * index + 5 + b]
            total = jnp.sum(part * part, axis=1, keepdims=True)
            gain = 0.5 * gain if index == 3 else gain
            mats[5 * b + index] = (part * (gain / jnp.sqrt(total + EPSILON))).astype(BF16)
    mats[15, :, 0:128] = columns.astype(BF16)
    mats[15, :, 128:256] = jnp.zeros((64, 128), BF16)
    for tap in range(2):
        for q in range(4):
            part = wide[q, pl.ds(2 * turn + tap, 64, stride=16), :]
            out[tap, :, 128 * q : 128 * q + 128] = part.astype(BF16)
        out[tap, :, 512:768] = mats[2 * turn + tap]


def pack_frames_kernel(places, low, high, signal, cotangent, *rest):
    firsts, seconds = rest[0:4], rest[4:8]
    chan = places[1]
    own = signal.shape[0] // 4
    frames = 8 * own
    count = own // 64
    row = lax.broadcasted_iota(jnp.int32, (16, 128), 0)
    lane = lax.broadcasted_iota(jnp.int32, (64, 128), 1)

    def halo(dest, after, before, edges, is_after):
        last, first = jnp.where(dest == 3, 1, 0), jnp.where(dest == 0, 1, 0)
        after = jnp.where(last == 1, edges[1].astype(F32), after.astype(F32))
        before = jnp.where(first == 1, edges[0].astype(F32), before.astype(F32))
        return jnp.where(is_after, after, before).astype(BF16)

    for k in range(4):
        dest = chan ^ k
        part = signal[pl.ds(pl.multiple_of(dest * own, own), own)]
        firsts[k][0:count] = part.reshape(count, 64, 128)
        after = pl.multiple_of(jnp.minimum(dest + 1, 3) * own, 16)
        before = pl.multiple_of(jnp.maximum(dest * own - 16, 0), 16)
        edges = (low[0:16], high[0:16])
        firsts[k][count] = jnp.zeros((64, 128), BF16)
        firsts[k][count, 0:16] = halo(
            dest, signal[pl.ds(after, 16)], signal[pl.ds(before, 16)], edges, row < HALO
        )
        for q in range(frames // 128):
            lanes = pl.ds(pl.multiple_of(dest * frames + 128 * q, 128), 128)
            part = cotangent[:, lanes]
            if q < EARLY:
                firsts[k][count + 1 + q] = part
            else:
                seconds[k][q - EARLY] = part
        after = pl.multiple_of(jnp.minimum(dest + 1, 3) * frames, 128)
        before = pl.multiple_of(jnp.maximum(dest * frames - 128, 0), 128)
        edges = (low[16:80], high[16:80])
        seconds[k][frames // 128 - EARLY] = halo(
            dest,
            cotangent[:, pl.ds(after, 128)],
            cotangent[:, pl.ds(before, 128)],
            edges,
            lane < 8 * HALO,
        )


def finish_kernel(places, sec_ref, three_ref, mix_ref, skip_ref, gt, gm, gk, stat, *rest):
    pieces = rest[:10]
    sec_out, gain_out, bs, three_out, gt_out, bt, mix_out, gm_out, bm, skip_out, gk_out, bk = rest[10:22]
    wide, rows, mats = rest[22:]
    turn = places[0]
    for ref, (place, first, _) in zip(pieces, SPREAD_PLACES, strict=True):
        pair = 2 * (turn ^ place)
        taps = 1 if place >= 6 else 2
        for tap in range(taps):
            k = pair + tap + first
            part = ref[tap].astype(F32)
            for q in range(4):
                wide[q, pl.ds(k, 64, stride=17), :] = part[:, 128 * q : 128 * q + 128]
            mats[k] = part[:, 512:768]
    aux = mats[15]
    norm, scale = stat[0:1], stat[1:2]
    gains = jnp.concatenate([aux[q : q + 1, 128:256] for q in range(4)], axis=1) / norm
    gain_out[...] = gains
    ratio = gains / norm
    for q in range(4):
        lanes = slice(128 * q, 128 * q + 128)
        for o in range(64):
            part = sec_ref[o, :, lanes].astype(F32)
            grad = wide[q, 17 * o : 17 * o + 16, :] - ratio[:, lanes] * part
            sec_out[o, :, lanes] = scale[:, lanes] * grad
    rows[...] = jnp.zeros_like(rows)
    for index, ref in enumerate((gt, gm, gk)):
        rows[3 * index : 3 * index + 3, 0:64] = ref[...].astype(F32)
    columns = jnp.transpose(rows[...])[0:64]
    results = []
    for b in range(3):
        three = three_ref[b].astype(F32)
        norm = jnp.sqrt(jnp.sum(jnp.sum(three * three, axis=0), axis=1, keepdims=True) + EPSILON)
        total = mats[5 * b] * three[0] + mats[5 * b + 1] * three[1] + mats[5 * b + 2] * three[2]
        gain = jnp.sum(total, axis=1, keepdims=True) / norm
        results.append(gain)
        for tap in range(3):
            grad = mats[5 * b + tap] - gain / norm * three[tap]
            three_out[b, tap] = columns[:, b : b + 1] / norm * grad
    for index, (ref, out) in enumerate(((mix_ref, mix_out), (skip_ref, skip_out))):
        for b in range(3):
            part = ref[b].astype(F32)
            grad = mats[5 * b + 3 + index]
            norm = jnp.sqrt(jnp.sum(part * part, axis=1, keepdims=True) + EPSILON)
            gain = jnp.sum(grad * part, axis=1, keepdims=True) / norm
            results.append(gain)
            place = 3 + 3 * index + b
            out[b] = columns[:, place : place + 1] / norm * (grad - gain / norm * part)
    lane = lax.broadcasted_iota(jnp.int32, (64, 128), 1)
    table = jnp.where(lane < 7, aux[:, 0:128], 0.0)
    for index, gain in enumerate(results):
        table = jnp.where(lane == 8 + index, gain, table)
    rows[:, 0:64] = jnp.transpose(table)
    bs[...] = rows[0:1, 0:64]
    bt[...] = rows[1:4, 0:64]
    bm[...] = rows[4:7, 0:64]
    bk[...] = rows[4:7, 0:64]
    gt_out[...] = rows[8:11, 0:64]
    gm_out[...] = rows[11:14, 0:64]
    gk_out[...] = rows[14:17, 0:64]


def weight_copies(places, refs, wsec, wblk, sem, block_sem):
    turn, chan = places[0], places[1]
    copies = []
    for ref, (place, first, _) in zip(refs, WEIGHT_PLACES, strict=True):
        slots = pl.ds(2 * (turn ^ place), 2)
        for k in range(ref.shape[0]):
            rows = pl.ds(pl.multiple_of(64 * (chan ^ (first + k)), 64), 64)
            copies.append(
                pltpu.make_async_copy(
                    ref.at[k, :, :, 0:512], wsec.at[slots, rows, :], sem
                )
            )
            copies.append(
                pltpu.make_async_copy(
                    ref.at[k, :, :, 512:768], wblk.at[slots, rows, :], block_sem
                )
            )
    return copies


def forward_kernel(
    places,
    sig0,
    sig1,
    sig2,
    sig3,
    ids_ref,
    gain_ref,
    *rest,
):
    pieces, rest = rest[:10], rest[10:]
    hid_out, act_out, mix_out, inner_out = rest[0:4]
    sact_out, mask_out, stat_out = rest[4:7]
    outs = rest[7:11]
    wsec, wblk, cat, bias, wide, turned, flat = rest[11:18]
    hids, mixs, inners, acts = rest[18:21], rest[21:24], rest[24:27], rest[27:30]
    wsem, ssem = rest[30:]
    chan = places[1]
    rows = sact_out.shape[0]
    own = rows - 2 * HALO
    pitch = own // 2 + 1
    loads = weight_copies(places, pieces, wsec, wblk, wsem, wsem)
    for copy in loads:
        copy.start()
    fill_masks(ids_ref, flat, mask_out)
    for k, ref in enumerate((sig0, sig1, sig2, sig3)):
        lanes = pl.ds(pl.multiple_of(128 * (chan ^ k), 128), 128)
        values = silu_half(0.5 * ref[0 : own // 64].reshape(own, 128).astype(F32))[0]
        to_rows(flat, values, sact_out.at[:, lanes])
        halo = silu_half(0.5 * ref[own // 64, 0:16].astype(F32))[0]
        sact_out[own:rows, lanes] = halo.astype(BF16)
    for copy in loads:
        copy.wait()

    def square(k, total):
        part = wsec[k].astype(F32)
        return total + jnp.sum((part * part).reshape(32, 8, 512), axis=0)

    total = lax.fori_loop(0, 16, square, jnp.zeros((8, 512), F32))
    norm = jnp.sqrt(jnp.sum(total, axis=0, keepdims=True) + EPSILON)
    scale = gain_ref[...] / norm
    stat_out[...] = jnp.concatenate([norm, scale, jnp.zeros((6, 512), F32)], axis=0)
    bias[...] = 0.5 * jnp.transpose(wblk[15].astype(F32))[:16]
    cat[0] = (sact_out[...].astype(F32) * (0.5 * scale)).astype(BF16)
    masked_move(cat, 1, cat[0], mask_out, -1)
    masked_move(cat, 2, cat[0], mask_out, 1)
    saves = []

    def keep(source, out, b):
        copy = pltpu.make_async_copy(source, out.at[b], ssem)
        copy.start()
        saves.append(copy)

    def enter(b, r, half):
        hids[b][r] = half.astype(BF16)
        value = silu_half(half)[0].astype(BF16)
        acts[b][9 + r] = value
        if b == 2:
            move_each(acts[b], mask_out, r, value)

    def phase_rows(values, n):
        return values[n * rows : n * rows + rows]

    def section(q, carry):
        left = jnp.concatenate([cat[0], cat[1 + q // 4]], axis=1)
        right = jnp.concatenate([wsec[q + 4], wsec[lax.rem(q + 12, 16)]], axis=1)
        enter(0, q, nt(left, right) + bias[0:1])
        return carry

    lax.fori_loop(0, 8, section, 0, unroll=4)
    for b in range(3):
        dilate = 3**b
        act, mix, sum_in, hid = acts[b], mixs[b], inners[b], hids[b]
        if b < 2:
            move_near(act, mask_out, dilate)
        else:
            move_far(act, mask_out)
        keep(hid, hid_out, b)
        keep(act.at[9:17], act_out, b)

        def taps(q):
            left = []
            for r in (2 * q, 2 * q + 1):
                parts = [act[9 + r - dilate], act[9 + r], act[9 + r + dilate]]
                left.append(jnp.concatenate(parts, axis=1))
            right = jnp.concatenate([wblk[5 * b], wblk[5 * b + 1], wblk[5 * b + 2]], axis=1)
            inner = nt(jnp.concatenate(left, axis=0), right)
            for n in range(2):
                half = phase_rows(inner, n) + bias[1 + b : 2 + b]
                mix[2 * q + n] = silu_half(half)[0].astype(BF16)
                sum_in[2 * q + n] = half.astype(BF16)

        def blend(q):
            left = []
            for r in (2 * q, 2 * q + 1):
                left.append(jnp.concatenate([mix[r], hid[r]], axis=1))
            right = jnp.concatenate([wblk[5 * b + 3], wblk[5 * b + 4]], axis=1)
            totals = [nt(part, right) for part in left]
            for n in range(2):
                r = 2 * q + n
                after = totals[n] + (bias[4 + b : 5 + b] + bias[7 + b : 8 + b])
                if b < 2:
                    enter(b + 1, r, after)
                else:
                    for tile in range(own // 16):
                        part = 2.0 * after[16 * tile : 16 * tile + 16]
                        frames = pl.ds(8 * tile + r, 16, stride=pitch)
                        wide[0, frames, :] = part[:, 0:128]
                        wide[1, frames, :] = part[:, 128:256]

        def both(q, carry):
            blend(q - 1)
            taps(q)
            return carry

        taps(0)
        lax.fori_loop(1, 4, both, 0)
        blend(3)
        keep(mix, mix_out, b)
        keep(sum_in, inner_out, b)

    def turn(q, carry):
        start = pitch * (q // 2) + 128 * lax.rem(q, 2)
        frames = pl.ds(pl.multiple_of(128 * q, 128), 128)
        for half in range(2):
            part = jnp.transpose(wide[half, pl.ds(start, 128), :])
            turned[128 * half : 128 * half + 128, frames] = part.astype(BF16)
        return carry

    lax.fori_loop(0, 8 * own // 128, turn, 0, unroll=4)
    final = []
    for k, out in enumerate(outs):
        part = turned.at[pl.ds(pl.multiple_of(64 * (chan ^ k), 64), 64), :]
        final.append(pltpu.make_async_copy(part, out, wsem))
    for copy in final:
        copy.start()
    for copy in saves + final:
        copy.wait()


def backward_kernel(
    places,
    first0,
    first1,
    first2,
    first3,
    second0,
    second1,
    second2,
    second3,
    sact_ref,
    mask_ref,
    stat_ref,
    hid_in,
    act_in,
    mix_in,
    inner_in,
    *rest,
):
    pieces, rest = rest[:10], rest[10:]
    sums_out = rest[0:6]
    sgrads = rest[6:10]
    targets = [(sums_out[0], 6), (sums_out[1].at[0], 2), (sums_out[1].at[1], 4), (sums_out[2], 0)]
    targets = targets + [
        (sums_out[3], 7),
        (sums_out[4].at[0], 3),
        (sums_out[4].at[1], 5),
        (sums_out[5], 1),
    ]
    (wsec, wblk, turned, sigs, wide, grad, inner_a, inner_b, mix, hid, act, halves) = rest[10:22]
    (acc_one, acc_three, through, sums, staged, wsem, vsem, csem, bsem, osem) = rest[22:]
    pitch = 4 * (sact_ref.shape[0] - 2 * HALO) // 8 + 1
    turn_index, chan = places[0], places[1]
    rows = mask_ref.shape[1]
    own = rows - 2 * HALO

    loads = weight_copies(places, pieces, wsec, wblk, wsem, vsem)
    cots = []
    count = own // 64
    section_loads = []
    pairs = ((first0, second0), (first1, second1), (first2, second2), (first3, second3))
    for k, (one, two) in enumerate(pairs):
        part = pl.ds(pl.multiple_of(64 * (chan ^ k), 64), 64)
        early = one.at[count + 1 : count + 1 + EARLY]
        cots.append(pltpu.make_async_copy(early, turned.at[0:EARLY, part, :], csem))
        late = turned.at[EARLY : 8 * own // 128 + 1, part, :]
        cots.append(pltpu.make_async_copy(two, late, csem))
        section_loads.append(pltpu.make_async_copy(one.at[0:count], sigs.at[k], wsem))

    def kept(b):
        slot = b % 2
        return [
            pltpu.make_async_copy(inner_in.at[b], halves.at[slot], bsem.at[slot, 0]),
            pltpu.make_async_copy(mix_in.at[b, :, 0:own], mix.at[slot], bsem.at[slot, 1]),
            pltpu.make_async_copy(hid_in.at[b], hid.at[slot], bsem.at[slot, 2]),
            pltpu.make_async_copy(act_in.at[b, :, 0:own], act.at[slot], bsem.at[slot, 3]),
        ]

    block_loads, section_loads = loads[1::2], loads[0::2] + section_loads
    for copy in cots + block_loads + kept(2) + kept(1) + section_loads:
        copy.start()
    sums[...] = jnp.zeros_like(sums)
    for copy in cots:
        copy.wait()
    def turn(q, carry):
        start = pitch * (q // 2) + 128 * lax.rem(q, 2)
        for half in range(2):
            part = turned[q, 128 * half : 128 * half + 128].astype(F32)
            wide[half, pl.ds(start, 128), :] = jnp.transpose(part)
        return carry

    lax.fori_loop(0, 8 * own // 128, turn, 0, unroll=4)
    turn(8 * own // 128, 0)

    def phases(r, carry):
        for half in range(2):
            lanes = slice(128 * half, 128 * half + 128)
            for tile in range(own // 16):
                part = wide[half, pl.ds(8 * tile + r, 16, stride=pitch), :]
                grad[r, 16 * tile : 16 * tile + 16, lanes] = part.astype(BF16)
            part = wide[half, pl.ds(16 * pitch + r, 16, stride=8), :]
            grad[r, own:rows, lanes] = part.astype(BF16)
        return carry

    lax.fori_loop(0, 8, phases, 0)
    for copy in block_loads:
        copy.wait()

    def own_sum(values):
        return jnp.sum(values[:own].astype(F32).reshape(own // 8, 8, 256), axis=0)

    def two(store, q, count):
        return jnp.concatenate([store[2 * q, 0:count], store[2 * q + 1, 0:count]], axis=0)

    def enter(b, inner, q):
        slot = b % 2
        g = two(grad, q, rows)
        down = nn(g, wblk[5 * b + 3])
        kept_rows = jnp.concatenate([mix[slot, 2 * q], mix[slot, 2 * q + 1]], axis=0)
        hidden = jnp.concatenate([hid[slot, 2 * q, 0:own], hid[slot, 2 * q + 1, 0:own]], axis=0)
        both = jnp.concatenate([kept_rows, hidden], axis=1)
        acc_one[...] += tn(two(grad, q, own), both)
        for n in range(2):
            r = 2 * q + n
            half = halves[slot, r].astype(F32)
            slope = slope_twice(half, *silu_half(half)[1:])
            part = (down[n * rows : n * rows + rows] * slope).astype(BF16)
            inner[9 + r] = part
            if b == 2:
                move_each(inner, mask_ref, r, part)

    def through_taps(b, inner, q):
        dilate, slot = 3**b, b % 2
        waves = []
        for r in (2 * q, 2 * q + 1):
            parts = [inner[9 + r + dilate], inner[9 + r], inner[9 + r - dilate]]
            waves.append(jnp.concatenate(parts, axis=1))
            sums[1 + b] += own_sum(parts[1])
            sums[4 + b] += own_sum(grad[r])
        deep = nn(jnp.concatenate(waves, axis=0), wblk[5 * b : 5 * b + 3].reshape(768, 256))
        skip = nn(two(grad, q, rows), wblk[5 * b + 4])
        acts = jnp.concatenate([act[slot, 2 * q], act[slot, 2 * q + 1]], axis=0)
        acc_three[...] += tn(jnp.concatenate([wave[:own] for wave in waves], axis=0), acts)
        for n in range(2):
            part = slice(n * rows, n * rows + rows)
            half = hid[slot, 2 * q + n].astype(F32)
            back = skip[part] + slope_twice(half, *silu_half(half)[1:]) * deep[part]
            grad[2 * q + n] = back.astype(BF16)

    def stage_taps(b):
        for tap in range(3):
            part = acc_three[256 * tap : 256 * tap + 256, :]
            staged[5 * b + tap, :, 512:768] = part.astype(BF16)
        acc_three[...] = jnp.zeros_like(acc_three)

    def stage_points(b):
        staged[5 * b + 3, :, 512:768] = acc_one[:, 0:256].astype(BF16)
        staged[5 * b + 4, :, 512:768] = (2.0 * acc_one[:, 256:512]).astype(BF16)
        acc_one[...] = jnp.zeros_like(acc_one)

    def arrive(b, numbers):
        for number in numbers:
            kept(b)[number].wait()

    def taps(r):
        g = grad[r]
        sums[0] += own_sum(g)
        last[r + 4] = g

        @pl.when(r < 4)
        def _():
            masked_move(last, r + 12, grad[r], mask_ref, 1)

        @pl.when(r >= 4)
        def _():
            masked_move(last, r - 4, grad[r], mask_ref, -1)

    acc_one[...] = jnp.zeros_like(acc_one)
    acc_three[...] = jnp.zeros_like(acc_three)
    arrive(2, (0, 1, 2))

    def enter_last(q, carry):
        enter(2, inner_a, q)
        return carry

    lax.fori_loop(0, 4, enter_last, 0)
    stage_points(2)
    move_far(inner_a, mask_ref)
    arrive(2, (3,))
    arrive(1, (0, 1, 2))
    for b, inner, following in ((2, inner_a, inner_b), (1, inner_b, inner_a)):

        def pipelined(q, carry):
            through_taps(b, inner, q)
            enter(b - 1, following, q - 1)
            return carry

        through_taps(b, inner, 0)
        lax.fori_loop(1, 4, pipelined, 0)
        enter(b - 1, following, 3)
        stage_taps(b)
        stage_points(b - 1)
        move_near(following, mask_ref, 3 ** (b - 1))
        if b == 2:
            for copy in kept(0):
                copy.start()
            arrive(1, (3,))
            arrive(0, (0, 1, 2))
        else:
            arrive(0, (3,))
    last = inner_b

    def final(q, carry):
        through_taps(0, inner_a, q)
        return carry

    lax.fori_loop(0, 4, final, 0)
    stage_taps(0)

    def section_taps(r, carry):
        taps(r)
        return carry

    lax.fori_loop(0, 8, section_taps, 0)
    for copy in section_loads:
        copy.wait()
    through[...] = jnp.zeros_like(through)
    sact = sact_ref[0:own]

    def send(pair):
        place = pair ^ turn_index
        source = staged.at[pl.ds(2 * pair, 2)]
        for out, place_of in targets:

            @pl.when(place == place_of)
            def _(out=out):
                pltpu.make_async_copy(source, out, osem).start()

    def collect(q, carry):
        left = jnp.concatenate([last[2 * q, 0:own], last[2 * q + 1, 0:own]], axis=1)
        through[...] += nn(left, wsec[pl.ds(2 * q, 2)].reshape(512, 512))
        grads = tn(left, sact).astype(BF16)
        staged[2 * q, :, 0:512] = grads[0:256]
        staged[2 * q + 1, :, 0:512] = grads[256:512]

        @pl.when(q < 7)
        def _():
            send(q)

        return carry

    lax.fori_loop(0, 8, collect, 0)
    deep = through[...]
    gains = jnp.sum(sact.astype(F32) * deep, axis=0, keepdims=True)
    through[...] = deep * (0.5 * stat_ref[1:2])
    biases = jnp.concatenate(
        [jnp.sum(sums[index], axis=0, keepdims=True) for index in range(8)]
        + [jnp.zeros((120, 256), F32)],
        axis=0,
    )
    staged[15, :, 512:640] = jnp.transpose(biases).astype(BF16)
    gain_rows = jnp.concatenate(
        [gains[:, 128 * q : 128 * q + 128] for q in range(4)] + [jnp.zeros((60, 128), F32)], axis=0
    ).astype(BF16)
    for part in range(4):
        staged[15, 64 * part : 64 * part + 64, 640:768] = gain_rows

    send(7)
    for k, out in enumerate(sgrads):
        lanes = pl.ds(pl.multiple_of(128 * (chan ^ k), 128), 128)
        half = 0.5 * sigs[k].reshape(own, 128).astype(F32)
        slope = slope_twice(half, *silu_half(half)[1:])
        count = own // 16
        for tile in range(count):
            part = through[16 * tile : 16 * tile + 16, lanes]
            wide[0, pl.ds(tile, 16, stride=count + 1), :] = part
        groups = [wide[0, (count + 1) * n : (count + 1) * n + count, :] for n in range(16)]
        out[...] = (jnp.concatenate(groups, axis=0) * slope).astype(BF16)
    for pair in range(8):
        pltpu.make_async_copy(staged.at[pl.ds(2 * pair, 2)], sums_out[0], osem).wait()


def shape_of(shape, kind=BF16):
    return jax.ShapeDtypeStruct(shape, kind)


SPEC_VMEM = pl.BlockSpec(memory_space=pltpu.VMEM)
SPEC_ANY = pl.BlockSpec(memory_space=pl.ANY)
SPEC_SMEM = pl.BlockSpec(memory_space=pltpu.SMEM)


def params():
    return pltpu.CompilerParams(vmem_limit_bytes=VMEM_BYTES)


def cost(flops, moved_bytes):
    return pl.CostEstimate(flops=int(flops), bytes_accessed=int(moved_bytes), transcendentals=0)


def run_pack_weights(places, *arrays):
    return pl.pallas_call(
        pack_weights_kernel,
        out_shape=shape_of((2, 64, 768)),
        in_specs=[SPEC_SMEM] + [SPEC_VMEM] * 11,
        out_specs=SPEC_VMEM,
        scratch_shapes=[
            pltpu.VMEM((4, 1024, 128), F32),
            pltpu.VMEM((128, 128), F32),
            pltpu.VMEM((16, 64, 256), BF16),
        ],
        compiler_params=params(),
        cost_estimate=cost(2e7, 3e6),
        name="pack_weights",
    )(places, *arrays)


def run_pack_frames(places, low, high, signal, cotangent):
    own = signal.shape[0] // 4
    return pl.pallas_call(
        pack_frames_kernel,
        out_shape=[shape_of((own // 64 + 1 + EARLY, 64, 128))] * 4
        + [shape_of((8 * own // 128 + 1 - EARLY, 64, 128))] * 4,
        in_specs=[SPEC_SMEM] + [SPEC_VMEM] * 4,
        out_specs=[SPEC_VMEM] * 8,
        compiler_params=params(),
        cost_estimate=cost(1e6, 6e6),
        name="pack_frames",
    )(places, low, high, signal, cotangent)


def run_finish(places, v_section, three, v_mix, v_skip, g_dilated, g_mix, g_skip, stat, pieces):
    small = shape_of((3, 64), F32)
    out_shape = [
        shape_of((64, 16, 512), F32),
        shape_of((1, 512), F32),
        shape_of((1, 64), F32),
        shape_of((3, 3, 64, 256), F32),
        small,
        small,
        shape_of((3, 64, 256), F32),
        small,
        small,
        shape_of((3, 64, 256), F32),
        small,
        small,
    ]
    return pl.pallas_call(
        finish_kernel,
        out_shape=out_shape,
        in_specs=[SPEC_SMEM] + [SPEC_VMEM] * 18,
        out_specs=[SPEC_VMEM] * 12,
        scratch_shapes=[
            pltpu.VMEM((4, 64 * 17, 128), F32),
            pltpu.VMEM((128, 128), F32),
            pltpu.VMEM((16, 64, 256), F32),
        ],
        compiler_params=params(),
        cost_estimate=cost(2e7, 8e6),
        name="finish_weights",
    )(places, v_section, three, v_mix, v_skip, g_dilated, g_mix, g_skip, stat, *pieces)


def run_forward(places, firsts, ids, gain, pieces):
    own = ids.shape[0] - 32
    rows = own + 2 * HALO
    kept = shape_of((3, 8, rows, 256))
    out_shape = [kept] * 4 + [
        shape_of((rows, 512)),
        shape_of((4, rows, 128)),
        shape_of((8, 512), F32),
    ]
    out_shape = out_shape + [shape_of((64, 8 * own))] * 4
    return pl.pallas_call(
        forward_kernel,
        out_shape=out_shape,
        in_specs=[SPEC_SMEM] + [SPEC_VMEM] * 6 + [SPEC_ANY] * 10,
        out_specs=[SPEC_ANY] * 4 + [SPEC_VMEM] * 3 + [SPEC_ANY] * 4,
        scratch_shapes=[
            pltpu.VMEM((16, 256, 512), BF16),
            pltpu.VMEM((16, 256, 256), BF16),
            pltpu.VMEM((3, rows, 512), BF16),
            pltpu.VMEM((16, 256), F32),
            pltpu.VMEM((2, 16 * (own // 2 + 1), 128), F32),
            pltpu.VMEM((256, 8 * own), BF16),
            pltpu.VMEM((own + 16, 128), F32),
        ]
        + [pltpu.VMEM((8, rows, 256), BF16)] * 9
        + [pltpu.VMEM((26, rows, 256), BF16)] * 3
        + [pltpu.SemaphoreType.DMA, pltpu.SemaphoreType.DMA],
        compiler_params=params(),
        cost_estimate=cost(2 * 1245184 * 8 * rows, 50e6),
        name="forward_blocks",
    )(places, *firsts, ids, gain, *pieces)


def run_backward(places, firsts, seconds, sact, masks, stat, kept, pieces):
    rows = sact.shape[0]
    own = rows - 2 * HALO
    return pl.pallas_call(
        backward_kernel,
        out_shape=[
            shape_of((2, 256, 768)),
            shape_of((2, 2, 256, 768)),
            shape_of((2, 256, 768)),
        ]
        * 2
        + [shape_of((own, 128))] * 4,
        in_specs=[SPEC_SMEM]
        + [SPEC_ANY] * 8
        + [SPEC_VMEM] * 3
        + [SPEC_ANY] * 14,
        out_specs=[SPEC_ANY] * 6 + [SPEC_VMEM] * 4,
        scratch_shapes=[
            pltpu.VMEM((16, 256, 512), BF16),
            pltpu.VMEM((16, 256, 256), BF16),
            pltpu.VMEM((8 * own // 128 + 1, 256, 128), BF16),
            pltpu.VMEM((4, own // 64, 64, 128), BF16),
            pltpu.VMEM((2, 16 * (own // 2 + 1) + 128, 128), F32),
            pltpu.VMEM((8, rows, 256), BF16),
            pltpu.VMEM((26, rows, 256), BF16),
            pltpu.VMEM((26, rows, 256), BF16),
            pltpu.VMEM((2, 8, own, 256), BF16),
            pltpu.VMEM((2, 8, rows, 256), BF16),
            pltpu.VMEM((2, 8, own, 256), BF16),
            pltpu.VMEM((2, 8, rows, 256), BF16),
            pltpu.VMEM((256, 512), F32),
            pltpu.VMEM((768, 256), F32),
            pltpu.VMEM((own, 512), F32),
            pltpu.VMEM((8, 8, 256), F32),
            pltpu.VMEM((16, 256, 768), BF16),
            pltpu.SemaphoreType.DMA,
            pltpu.SemaphoreType.DMA,
            pltpu.SemaphoreType.DMA,
            pltpu.SemaphoreType.DMA((2, 4)),
            pltpu.SemaphoreType.DMA,
        ],
        compiler_params=params(),
        cost_estimate=cost(2 * 2490368 * 8 * rows, 60e6),
        name="backward_blocks",
    )(places, *firsts, *seconds, sact, masks, stat, *kept, *pieces)


def exchange(values, axis, cut):
    me = lax.axis_index(axis)
    parts = [cut(me)]
    for k in (1, 2, 3):
        parts.append(swap(cut(me ^ k), axis, k))
    return parts


def body(
    signal,
    segment_ids,
    v_section,
    g_section,
    b_section,
    v_dilated,
    g_dilated,
    b_dilated,
    v_mix,
    g_mix,
    b_mix,
    v_skip,
    g_skip,
    b_skip,
    cotangent,
):
    tm_index, chan = lax.axis_index("tm"), lax.axis_index("chan")
    tm_size = lax.axis_size("tm")
    turn = tm_index % 8
    places = jnp.stack([turn, chan]).astype(jnp.int32)
    own = signal.shape[0] // 4
    rows = own + 2 * HALO
    start = tm_index * signal.shape[0] + chan * own

    three_v = jnp.transpose(v_dilated, (0, 2, 1, 3))
    piece = run_pack_weights(
        places,
        v_section,
        three_v,
        v_mix,
        v_skip,
        b_section[None],
        b_dilated,
        b_mix,
        b_skip,
        g_dilated,
        g_mix,
        g_skip,
    )
    by_chan = [piece] + [swap(piece, "chan", k) for k in (1, 2, 3)]

    first = jnp.concatenate([signal[:16], cotangent[:, :128]], axis=0)
    final = jnp.concatenate([signal[-16:], cotangent[:, -128:]], axis=0)
    onward = [(i, i + 1) for i in range(tm_size - 1)]
    low = lax.ppermute(final, "tm", onward)
    high = lax.ppermute(first, "tm", [(target, source) for source, target in onward])
    packed = run_pack_frames(places, low, high, signal, cotangent)
    firsts, seconds = list(packed[0:4]), list(packed[4:8])
    by_chan, _ = lax.optimization_barrier((by_chan, packed[0]))
    for k in (1, 2, 3):
        firsts[k] = swap(firsts[k], "chan", k)
        seconds[k] = swap(seconds[k], "chan", k)
    pieces, firsts = gather_weights(jnp.stack(by_chan), firsts)
    firsts, seconds[1:3] = lax.optimization_barrier((firsts, seconds[1:3]))
    padded = jnp.pad(segment_ids, 16, constant_values=-1)
    nearby = lax.dynamic_slice_in_dim(padded, start, own + 32)
    ids = jnp.broadcast_to(nearby[:, None], (own + 32, 128))

    frames = 8 * own
    results = run_forward(places, firsts, ids, g_section[None].astype(F32), pieces)
    kept, sact, masks, stat, outs = results[:4], results[4], results[5], results[6], results[7:]

    outs, seconds = lax.optimization_barrier((list(outs), seconds))
    received = [outs[0]] + [swap(outs[k], "chan", k) for k in (1, 2, 3)]
    results = run_backward(places, firsts, seconds, sact, masks, stat, kept, pieces)
    far, sides, here, odd_far, odd_sides, odd_here = results[0:6]
    sgrads = results[6:]
    far, sides, here, odd_far, odd_sides, odd_here, sgrads, received = lax.optimization_barrier(
        (far, sides, here, odd_far, odd_sides, odd_here, list(sgrads), received)
    )

    def chan_sum(values):
        def cut_rows(place):
            return lax.dynamic_slice_in_dim(values, place * 64, 64, axis=1)

        parts = exchange(values, "chan", cut_rows)
        return parts[0] + parts[1] + parts[2] + parts[3]

    odd_sides = swap(odd_sides, "tm", 1)
    far = far + swap(odd_far, "tm", 1)
    odd_here = swap(odd_here, "tm", 1)
    output = jnp.zeros((64, 4 * frames), BF16)
    for k in range(4):
        output = lax.dynamic_update_slice_in_dim(output, received[k], (chan ^ k) * frames, axis=1)
    across = chan_sum(far)
    for_x, for_y = sides[0] + odd_sides[0], sides[1] + odd_sides[1]
    summed = (here + odd_here) + swap(for_x, "tm", 2) + swap(for_y, "tm", 4)
    summed, across = lax.optimization_barrier((summed, across))
    mine = chan_sum(summed) + swap(across, "tm", 6)
    bit = 8
    while bit < tm_size:
        mine = mine + swap(mine, "tm", bit)
        bit = 2 * bit
    mine, sgrads = lax.optimization_barrier((mine, sgrads))
    gathered = spread(mine)

    received = [sgrads[0]] + [swap(sgrads[k], "chan", k) for k in (1, 2, 3)]
    signal_grad = jnp.zeros((4 * own, 128), BF16)
    for k in range(4):
        signal_grad = lax.dynamic_update_slice_in_dim(
            signal_grad, received[k], (chan ^ k) * own, axis=0
        )
    (sec, gain, bs, three, gt, bt, mix, gm, bm, skip, gk, bk) = run_finish(
        places, v_section, three_v, v_mix, v_skip, g_dilated, g_mix, g_skip, stat, gathered
    )
    return (
        output,
        signal_grad,
        sec,
        gain.reshape(512),
        bs.reshape(64),
        jnp.transpose(three, (0, 2, 1, 3)),
        gt,
        bt,
        mix,
        gm,
        bm,
        skip,
        gk,
        bk,
    )


def solution(mesh):
    return jax.shard_map(
        body,
        mesh=mesh,
        in_specs=(
            P("tm", "chan"),
            P(),
            P("chan", None, None),
            P(),
            P("chan"),
            P(None, "chan", None, None),
            P(None, "chan"),
            P(None, "chan"),
            P(None, "chan", None),
            P(None, "chan"),
            P(None, "chan"),
            P(None, "chan", None),
            P(None, "chan"),
            P(None, "chan"),
            P("chan", "tm"),
        ),
        out_specs=(
            P("chan", "tm"),
            P("tm", "chan"),
            P("chan", None, None),
            P(),
            P("chan"),
            P(None, "chan", None, None),
            P(None, "chan"),
            P(None, "chan"),
            P(None, "chan", None),
            P(None, "chan"),
            P(None, "chan"),
            P(None, "chan", None),
            P(None, "chan"),
            P(None, "chan"),
        ),
        check_vma=False,
    )
```

```python
import jax
import jax.numpy as jnp
from jax import lax
from jax.experimental import pallas as pl
from jax.experimental.pallas import tpu as pltpu
from jax.sharding import PartitionSpec as P

EPSILON = 1e-06
F32 = jnp.float32
BF16 = jnp.bfloat16
HALO = 8
EARLY = 15
VMEM_BYTES = 60 * 1024 * 1024


def xor_pairs(axis, bit):
    return [(i, i ^ bit) for i in range(lax.axis_size(axis))]


def swap(values, axis, bit):
    return lax.ppermute(values, axis, xor_pairs(axis, bit))


def spread(piece):
    near = [piece] + [swap(piece, "tm", place) for place in (2, 4, 6)]
    return near + [swap(entry, "tm", 1) for entry in near]


def gather_weights(column, signals):
    near = [column] + [swap(column, "tm", place) for place in (6, 2, 4)]
    near, signals = lax.optimization_barrier((near, signals))
    return near + [swap(entry, "tm", 1) for entry in near], signals


WEIGHT_PLACES = [(0, 0, 4), (6, 0, 4), (2, 0, 4), (4, 0, 4)]
WEIGHT_PLACES = WEIGHT_PLACES + [(a + 1, first, count) for a, first, count in WEIGHT_PLACES]


SPREAD_PLACES = [0, 2, 4, 6, 1, 3, 5, 7]


def nt(left, right):
    return lax.dot_general(left, right, (((1,), (1,)), ((), ())), preferred_element_type=F32)


def nn(left, right):
    return lax.dot_general(left, right, (((1,), (0,)), ((), ())), preferred_element_type=F32)


def tn(left, right):
    return lax.dot_general(left, right, (((0,), (0,)), ((), ())), preferred_element_type=F32)


def sigmoid(values):
    return 0.5 * jnp.tanh(0.5 * values) + 0.5


def silu_half(half):
    turn = jnp.tanh(half)
    product = half * turn
    return half + product, turn, product


def slope_twice(half, turn, product):
    return (1.0 + turn) + (half - product * turn)


def to_rows(flat, values, target):
    count = values.shape[0] // 16
    for group in range(16):
        start = group * (count + 1)
        flat[start : start + count] = values[group * count : group * count + count]
    for tile in range(count):
        part = flat[pl.ds(tile, 16, stride=count + 1)]
        target[16 * tile : 16 * tile + 16] = part.astype(BF16)


def fill_masks(ids_ref, flat, mask_ref):
    rows = mask_ref.shape[1]
    own = rows - 2 * HALO
    for index, step in enumerate((-1, 1, -2, 2)):
        inside = (ids_ref[16 : 8 + rows] == ids_ref[16 + step : 8 + rows + step]).astype(F32)
        before = (ids_ref[8:16] == ids_ref[8 + step : 16 + step]).astype(F32)
        to_rows(flat, inside[0:own], mask_ref.at[index])
        halo = jnp.concatenate([inside[own : own + 8], before], axis=0)
        mask_ref[index, own:rows] = halo.astype(BF16)


def masked_move(store, target, values, mask_ref, step):
    rows = values.shape[0]
    own = rows - 2 * HALO
    index = {-1: 0, 1: 1, -2: 2, 2: 3}[step]
    place = lax.broadcasted_iota(jnp.int32, (16, values.shape[1]), 0)

    def tile(number):
        return values[16 * number : 16 * number + 16].astype(F32)

    def turned(part, count):
        return pltpu.roll(part, count % 16, 0)

    count = own // 16
    halo = tile(count)
    size = abs(step)
    if step > 0:
        last = {}
        outer = turned(halo, -step)
        for n in range(step):
            inner_part = turned(tile(n), -1)
            last[count - step + n] = jnp.where(place == 15, turned(halo, -1 - n), inner_part)
            outer = jnp.where(place == 16 - step + n, turned(tile(n), n - step), outer)
        kept = (0, own - 16 * size, 16 * size)
    else:
        last = {}
        outer = turned(halo, size)
        for n in range(size):
            source = tile(count - size + n)
            last[n] = jnp.where(place == 0, turned(halo, size - n), turned(source, 1))
            outer = jnp.where(place == n, turned(source, n + 1), outer)
        kept = (16 * size, own, -16 * size)
    last[count] = outer
    wide = values.shape[1] // 128

    def masked(part, first):
        mask = mask_ref[index, first : first + part.shape[0]]
        return part * jnp.concatenate([mask] * wide, axis=1)

    first, end, offset = kept
    store[target, first:end] = masked(values[first + offset : end + offset], first)
    for number, part in last.items():
        store[target, 16 * number : 16 * number + 16] = masked(part.astype(BF16), 16 * number)


def move_far(store, mask_ref):
    masked_move(store, 0, store[16], mask_ref, -2)
    masked_move(store, 25, store[9], mask_ref, 2)


def move_near(store, mask_ref, dilate):
    def before(phase, carry):
        masked_move(store, 1 + phase, store[9 + phase], mask_ref, -1)
        return carry

    def after(phase, carry):
        masked_move(store, 17 + phase, store[9 + phase], mask_ref, 1)
        return carry

    lax.fori_loop(8 - dilate, 8, before, 0)
    lax.fori_loop(0, dilate, after, 0)


def move_each(store, mask_ref, phase, values):
    masked_move(store, 1 + phase, values, mask_ref, -1)
    masked_move(store, 17 + phase, values, mask_ref, 1)


def pack_weights_kernel(
    places, sec_ref, three_ref, mix_ref, skip_ref, bs, bt, bm, bk, gt, gm, gk, out, wide, rows, mats
):
    turn = places[0]
    for q in range(4):
        part = sec_ref[:, :, 128 * q : 128 * q + 128].astype(F32)
        wide[q] = part.reshape(1024, 128)
    rows[...] = jnp.zeros_like(rows)
    rows[0:1, 0:64] = bs[...].astype(F32)
    for index, ref in enumerate((bt, bm, bk, gt, gm, gk)):
        rows[1 + 3 * index : 4 + 3 * index, 0:64] = ref[...].astype(F32)
    columns = jnp.transpose(rows[...])[0:64]
    for b in range(3):
        three = three_ref[b].astype(F32)
        gain = columns[:, 10 + b : 11 + b]
        total = jnp.sum(jnp.sum(three * three, axis=0), axis=1, keepdims=True)
        scale = 0.5 * gain / jnp.sqrt(total + EPSILON)
        for tap in range(3):
            mats[5 * b + tap] = (three[tap] * scale).astype(BF16)
        for index, ref in ((3, mix_ref), (4, skip_ref)):
            part = ref[b].astype(F32)
            gain = columns[:, 3 * index + 4 + b : 3 * index + 5 + b]
            total = jnp.sum(part * part, axis=1, keepdims=True)
            gain = 0.5 * gain if index == 3 else gain
            mats[5 * b + index] = (part * (gain / jnp.sqrt(total + EPSILON))).astype(BF16)
    mats[15, :, 0:128] = columns.astype(BF16)
    mats[15, :, 128:256] = jnp.zeros((64, 128), BF16)
    for tap in range(2):
        for q in range(4):
            part = wide[q, pl.ds(2 * turn + tap, 64, stride=16), :]
            out[tap, :, 128 * q : 128 * q + 128] = part.astype(BF16)
        out[tap, :, 512:768] = mats[2 * turn + tap]


def pack_frames_kernel(places, low, high, signal, cotangent, *rest):
    firsts, seconds = rest[0:4], rest[4:8]
    chan = places[1]
    own = signal.shape[0] // 4
    frames = 8 * own
    count = own // 64
    row = lax.broadcasted_iota(jnp.int32, (16, 128), 0)
    lane = lax.broadcasted_iota(jnp.int32, (64, 128), 1)

    def halo(dest, after, before, edges, is_after):
        last, first = jnp.where(dest == 3, 1, 0), jnp.where(dest == 0, 1, 0)
        after = jnp.where(last == 1, edges[1].astype(F32), after.astype(F32))
        before = jnp.where(first == 1, edges[0].astype(F32), before.astype(F32))
        return jnp.where(is_after, after, before).astype(BF16)

    for k in range(4):
        dest = chan ^ k
        part = signal[pl.ds(pl.multiple_of(dest * own, own), own)]
        firsts[k][0:count] = part.reshape(count, 64, 128)
        after = pl.multiple_of(jnp.minimum(dest + 1, 3) * own, 16)
        before = pl.multiple_of(jnp.maximum(dest * own - 16, 0), 16)
        edges = (low[0:16], high[0:16])
        firsts[k][count] = jnp.zeros((64, 128), BF16)
        firsts[k][count, 0:16] = halo(
            dest, signal[pl.ds(after, 16)], signal[pl.ds(before, 16)], edges, row < HALO
        )
        for q in range(frames // 128):
            lanes = pl.ds(pl.multiple_of(dest * frames + 128 * q, 128), 128)
            part = cotangent[:, lanes]
            if q < EARLY:
                firsts[k][count + 1 + q] = part
            else:
                seconds[k][q - EARLY] = part
        after = pl.multiple_of(jnp.minimum(dest + 1, 3) * frames, 128)
        before = pl.multiple_of(jnp.maximum(dest * frames - 128, 0), 128)
        edges = (low[16:80], high[16:80])
        seconds[k][frames // 128 - EARLY] = halo(
            dest,
            cotangent[:, pl.ds(after, 128)],
            cotangent[:, pl.ds(before, 128)],
            edges,
            lane < 8 * HALO,
        )


def finish_kernel(places, sec_ref, three_ref, mix_ref, skip_ref, gt, gm, gk, stat, *rest):
    pieces = rest[:8]
    sec_out, gain_out, bs, three_out, gt_out, bt, mix_out, gm_out, bm, skip_out, gk_out, bk = rest[8:20]
    wide, rows, mats = rest[20:]
    turn = places[0]
    for ref, place in zip(pieces, SPREAD_PLACES, strict=True):
        pair = 2 * (turn ^ place)
        for tap in range(2):
            k = pair + tap
            part = ref[tap].astype(F32)
            for q in range(4):
                wide[q, pl.ds(k, 64, stride=17), :] = part[:, 128 * q : 128 * q + 128]
            mats[k] = part[:, 512:768]
    aux = mats[15]
    norm, scale = stat[0:1], stat[1:2]
    gains = jnp.concatenate([aux[q : q + 1, 128:256] for q in range(4)], axis=1) / norm
    gain_out[...] = gains
    ratio = gains / norm
    for q in range(4):
        lanes = slice(128 * q, 128 * q + 128)
        for o in range(64):
            part = sec_ref[o, :, lanes].astype(F32)
            grad = wide[q, 17 * o : 17 * o + 16, :] - ratio[:, lanes] * part
            sec_out[o, :, lanes] = scale[:, lanes] * grad
    rows[...] = jnp.zeros_like(rows)
    for index, ref in enumerate((gt, gm, gk)):
        rows[3 * index : 3 * index + 3, 0:64] = ref[...].astype(F32)
    columns = jnp.transpose(rows[...])[0:64]
    results = []
    for b in range(3):
        three = three_ref[b].astype(F32)
        norm = jnp.sqrt(jnp.sum(jnp.sum(three * three, axis=0), axis=1, keepdims=True) + EPSILON)
        total = mats[5 * b] * three[0] + mats[5 * b + 1] * three[1] + mats[5 * b + 2] * three[2]
        gain = jnp.sum(total, axis=1, keepdims=True) / norm
        results.append(gain)
        for tap in range(3):
            grad = mats[5 * b + tap] - gain / norm * three[tap]
            three_out[b, tap] = columns[:, b : b + 1] / norm * grad
    for index, (ref, out) in enumerate(((mix_ref, mix_out), (skip_ref, skip_out))):
        for b in range(3):
            part = ref[b].astype(F32)
            grad = mats[5 * b + 3 + index]
            norm = jnp.sqrt(jnp.sum(part * part, axis=1, keepdims=True) + EPSILON)
            gain = jnp.sum(grad * part, axis=1, keepdims=True) / norm
            results.append(gain)
            place = 3 + 3 * index + b
            out[b] = columns[:, place : place + 1] / norm * (grad - gain / norm * part)
    lane = lax.broadcasted_iota(jnp.int32, (64, 128), 1)
    table = jnp.where(lane < 7, aux[:, 0:128], 0.0)
    for index, gain in enumerate(results):
        table = jnp.where(lane == 8 + index, gain, table)
    rows[:, 0:64] = jnp.transpose(table)
    bs[...] = rows[0:1, 0:64]
    bt[...] = rows[1:4, 0:64]
    bm[...] = rows[4:7, 0:64]
    bk[...] = rows[4:7, 0:64]
    gt_out[...] = rows[8:11, 0:64]
    gm_out[...] = rows[11:14, 0:64]
    gk_out[...] = rows[14:17, 0:64]


def weight_copies(places, refs, wsec, wblk, sem, block_sem):
    turn, chan = places[0], places[1]
    section, blocks = [], []
    for index, (ref, (place, _, _)) in enumerate(zip(refs, WEIGHT_PLACES, strict=True)):
        slots = pl.ds(2 * (turn ^ place), 2)
        copies = []
        for k in range(4):
            rows = pl.ds(pl.multiple_of(64 * (chan ^ k), 64), 64)
            target = wsec.at[slots, rows, :]
            copies.append(pltpu.make_async_copy(ref.at[k, :, :, 0:512], target, sem.at[index]))
            target = wblk.at[slots, rows, :]
            blocks.append(pltpu.make_async_copy(ref.at[k, :, :, 512:768], target, block_sem))
        section.append(copies)
    return section, blocks


def forward_kernel(
    places,
    sig0,
    sig1,
    sig2,
    sig3,
    ids_ref,
    gain_ref,
    *rest,
):
    pieces, rest = rest[:8], rest[8:]
    hid_out, act_out, mix_out, inner_out = rest[0:4]
    sact_out, mask_out, stat_out = rest[4:7]
    outs = rest[7:11]
    wsec, wblk, cat, bias, wide, turned, flat = rest[11:18]
    hids, mixs, inners, acts = rest[18:21], rest[21:24], rest[24:27], rest[27:30]
    wsem, vsem, ssem = rest[30:]
    chan = places[1]
    rows = sact_out.shape[0]
    own = rows - 2 * HALO
    pitch = own // 2 + 1
    section_loads, block_loads = weight_copies(places, pieces, wsec, wblk, wsem, vsem)
    for copy in sum(section_loads, []) + block_loads:
        copy.start()
    fill_masks(ids_ref, flat, mask_out)
    for k, ref in enumerate((sig0, sig1, sig2, sig3)):
        lanes = pl.ds(pl.multiple_of(128 * (chan ^ k), 128), 128)
        values = silu_half(0.5 * ref[0 : own // 64].reshape(own, 128).astype(F32))[0]
        to_rows(flat, values, sact_out.at[:, lanes])
        halo = silu_half(0.5 * ref[own // 64, 0:16].astype(F32))[0]
        sact_out[own:rows, lanes] = halo.astype(BF16)
    total = jnp.zeros((8, 512), F32)
    for (place, _, _), copies in zip(WEIGHT_PLACES, section_loads, strict=True):
        for copy in copies:
            copy.wait()
        for tap in range(2):
            part = wsec[2 * (places[0] ^ place) + tap].astype(F32)
            total = total + jnp.sum((part * part).reshape(32, 8, 512), axis=0)
    for copy in block_loads:
        copy.wait()
    norm = jnp.sqrt(jnp.sum(total, axis=0, keepdims=True) + EPSILON)
    scale = gain_ref[...] / norm
    stat_out[...] = jnp.concatenate([norm, scale, jnp.zeros((6, 512), F32)], axis=0)
    bias[...] = 0.5 * jnp.transpose(wblk[15].astype(F32))[:16]
    cat[0] = (sact_out[...].astype(F32) * (0.5 * scale)).astype(BF16)
    masked_move(cat, 1, cat[0], mask_out, -1)
    masked_move(cat, 2, cat[0], mask_out, 1)
    saves = []

    def keep(source, out, b):
        copy = pltpu.make_async_copy(source, out.at[b], ssem)
        copy.start()
        saves.append(copy)

    def enter(b, r, half):
        hids[b][r] = half.astype(BF16)
        value = silu_half(half)[0].astype(BF16)
        acts[b][9 + r] = value
        if b == 2:
            move_each(acts[b], mask_out, r, value)

    def phase_rows(values, n):
        return values[n * rows : n * rows + rows]

    def section(q, carry):
        left = jnp.concatenate([cat[0], cat[1 + q // 4]], axis=1)
        right = jnp.concatenate([wsec[q + 4], wsec[lax.rem(q + 12, 16)]], axis=1)
        enter(0, q, nt(left, right) + bias[0:1])
        return carry

    lax.fori_loop(0, 8, section, 0, unroll=4)
    for b in range(3):
        dilate = 3**b
        act, mix, sum_in, hid = acts[b], mixs[b], inners[b], hids[b]
        if b < 2:
            move_near(act, mask_out, dilate)
        else:
            move_far(act, mask_out)
        keep(hid, hid_out, b)
        keep(act.at[9:17], act_out, b)

        def taps(q):
            left = []
            for r in (2 * q, 2 * q + 1):
                parts = [act[9 + r - dilate], act[9 + r], act[9 + r + dilate]]
                left.append(jnp.concatenate(parts, axis=1))
            right = jnp.concatenate([wblk[5 * b], wblk[5 * b + 1], wblk[5 * b + 2]], axis=1)
            inner = nt(jnp.concatenate(left, axis=0), right)
            for n in range(2):
                half = phase_rows(inner, n) + bias[1 + b : 2 + b]
                mix[2 * q + n] = silu_half(half)[0].astype(BF16)
                sum_in[2 * q + n] = half.astype(BF16)

        def blend(q):
            left = []
            for r in (2 * q, 2 * q + 1):
                left.append(jnp.concatenate([mix[r], hid[r]], axis=1))
            right = jnp.concatenate([wblk[5 * b + 3], wblk[5 * b + 4]], axis=1)
            totals = [nt(part, right) for part in left]
            for n in range(2):
                r = 2 * q + n
                after = totals[n] + (bias[4 + b : 5 + b] + bias[7 + b : 8 + b])
                if b < 2:
                    enter(b + 1, r, after)
                else:
                    for tile in range(own // 16):
                        part = 2.0 * after[16 * tile : 16 * tile + 16]
                        frames = pl.ds(8 * tile + r, 16, stride=pitch)
                        wide[0, frames, :] = part[:, 0:128]
                        wide[1, frames, :] = part[:, 128:256]

        def both(q, carry):
            blend(q - 1)
            taps(q)
            return carry

        taps(0)
        lax.fori_loop(1, 4, both, 0)
        blend(3)
        keep(mix, mix_out, b)
        keep(sum_in, inner_out, b)

    def turn(q, carry):
        start = pitch * (q // 2) + 128 * lax.rem(q, 2)
        frames = pl.ds(pl.multiple_of(128 * q, 128), 128)
        for half in range(2):
            part = jnp.transpose(wide[half, pl.ds(start, 128), :])
            turned[128 * half : 128 * half + 128, frames] = part.astype(BF16)
        return carry

    lax.fori_loop(0, 8 * own // 128, turn, 0, unroll=4)
    final = []
    for k, out in enumerate(outs):
        part = turned.at[pl.ds(pl.multiple_of(64 * (chan ^ k), 64), 64), :]
        final.append(pltpu.make_async_copy(part, out, vsem))
    for copy in final:
        copy.start()
    for copy in saves + final:
        copy.wait()


def backward_kernel(
    places,
    first0,
    first1,
    first2,
    first3,
    second0,
    second1,
    second2,
    second3,
    sact_ref,
    mask_ref,
    stat_ref,
    hid_in,
    act_in,
    mix_in,
    inner_in,
    *rest,
):
    pieces, rest = rest[:8], rest[8:]
    sums_out = rest[0:6]
    sgrads = rest[6:10]
    targets = [(sums_out[0], 6), (sums_out[1].at[0], 2), (sums_out[1].at[1], 4), (sums_out[2], 0)]
    targets = targets + [
        (sums_out[3], 7),
        (sums_out[4].at[0], 3),
        (sums_out[4].at[1], 5),
        (sums_out[5], 1),
    ]
    (wsec, wblk, turned, sigs, wide, grad, inner_a, inner_b, mix, hid, act, halves) = rest[10:22]
    (acc_one, acc_three, through, sums, staged, wsem, vsem, gsem, csem, bsem, osem) = rest[22:]
    pitch = 4 * (sact_ref.shape[0] - 2 * HALO) // 8 + 1
    turn_index, chan = places[0], places[1]
    rows = mask_ref.shape[1]
    own = rows - 2 * HALO

    section_weights, block_loads = weight_copies(places, pieces, wsec, wblk, wsem, vsem)
    cots = []
    count = own // 64
    section_loads = []
    pairs = ((first0, second0), (first1, second1), (first2, second2), (first3, second3))
    for k, (one, two) in enumerate(pairs):
        part = pl.ds(pl.multiple_of(64 * (chan ^ k), 64), 64)
        early = one.at[count + 1 : count + 1 + EARLY]
        cots.append(pltpu.make_async_copy(early, turned.at[0:EARLY, part, :], csem))
        late = turned.at[EARLY : 8 * own // 128 + 1, part, :]
        cots.append(pltpu.make_async_copy(two, late, csem))
        section_loads.append(pltpu.make_async_copy(one.at[0:count], sigs.at[k], gsem))

    def kept(b):
        slot = b % 2
        return [
            pltpu.make_async_copy(inner_in.at[b], halves.at[slot], bsem.at[slot, 0]),
            pltpu.make_async_copy(mix_in.at[b, :, 0:own], mix.at[slot], bsem.at[slot, 1]),
            pltpu.make_async_copy(hid_in.at[b], hid.at[slot], bsem.at[slot, 2]),
            pltpu.make_async_copy(act_in.at[b, :, 0:own], act.at[slot], bsem.at[slot, 3]),
        ]

    section_loads = sum(section_weights, []) + section_loads
    for copy in cots + block_loads + kept(2) + kept(1) + section_loads:
        copy.start()
    sums[...] = jnp.zeros_like(sums)
    for copy in cots:
        copy.wait()
    def turn(q, carry):
        start = pitch * (q // 2) + 128 * lax.rem(q, 2)
        for half in range(2):
            part = turned[q, 128 * half : 128 * half + 128].astype(F32)
            wide[half, pl.ds(start, 128), :] = jnp.transpose(part)
        return carry

    lax.fori_loop(0, 8 * own // 128, turn, 0, unroll=4)
    turn(8 * own // 128, 0)

    def phases(r, carry):
        for half in range(2):
            lanes = slice(128 * half, 128 * half + 128)
            for tile in range(own // 16):
                part = wide[half, pl.ds(8 * tile + r, 16, stride=pitch), :]
                grad[r, 16 * tile : 16 * tile + 16, lanes] = part.astype(BF16)
            part = wide[half, pl.ds(16 * pitch + r, 16, stride=8), :]
            grad[r, own:rows, lanes] = part.astype(BF16)
        return carry

    lax.fori_loop(0, 8, phases, 0)
    for copy in block_loads:
        copy.wait()

    def own_sum(values):
        return jnp.sum(values[:own].astype(F32).reshape(own // 8, 8, 256), axis=0)

    def two(store, q, count):
        return jnp.concatenate([store[2 * q, 0:count], store[2 * q + 1, 0:count]], axis=0)

    def enter(b, inner, q):
        slot = b % 2
        g = two(grad, q, rows)
        down = nn(g, wblk[5 * b + 3])
        kept_rows = jnp.concatenate([mix[slot, 2 * q], mix[slot, 2 * q + 1]], axis=0)
        hidden = jnp.concatenate([hid[slot, 2 * q, 0:own], hid[slot, 2 * q + 1, 0:own]], axis=0)
        both = jnp.concatenate([kept_rows, hidden], axis=1)
        acc_one[...] += tn(two(grad, q, own), both)
        for n in range(2):
            r = 2 * q + n
            half = halves[slot, r].astype(F32)
            slope = slope_twice(half, *silu_half(half)[1:])
            part = (down[n * rows : n * rows + rows] * slope).astype(BF16)
            inner[9 + r] = part
            if b == 2:
                move_each(inner, mask_ref, r, part)

    def through_taps(b, inner, q):
        dilate, slot = 3**b, b % 2
        waves = []
        for r in (2 * q, 2 * q + 1):
            parts = [inner[9 + r + dilate], inner[9 + r], inner[9 + r - dilate]]
            waves.append(jnp.concatenate(parts, axis=1))
            sums[1 + b] += own_sum(parts[1])
            sums[4 + b] += own_sum(grad[r])
        deep = nn(jnp.concatenate(waves, axis=0), wblk[5 * b : 5 * b + 3].reshape(768, 256))
        skip = nn(two(grad, q, rows), wblk[5 * b + 4])
        acts = jnp.concatenate([act[slot, 2 * q], act[slot, 2 * q + 1]], axis=0)
        acc_three[...] += tn(jnp.concatenate([wave[:own] for wave in waves], axis=0), acts)
        for n in range(2):
            part = slice(n * rows, n * rows + rows)
            half = hid[slot, 2 * q + n].astype(F32)
            back = skip[part] + slope_twice(half, *silu_half(half)[1:]) * deep[part]
            grad[2 * q + n] = back.astype(BF16)

    def stage_taps(b):
        for tap in range(3):
            part = acc_three[256 * tap : 256 * tap + 256, :]
            staged[5 * b + tap, :, 512:768] = part.astype(BF16)
        acc_three[...] = jnp.zeros_like(acc_three)

    def stage_points(b):
        staged[5 * b + 3, :, 512:768] = acc_one[:, 0:256].astype(BF16)
        staged[5 * b + 4, :, 512:768] = (2.0 * acc_one[:, 256:512]).astype(BF16)
        acc_one[...] = jnp.zeros_like(acc_one)

    def arrive(b, numbers):
        for number in numbers:
            kept(b)[number].wait()

    def taps(r):
        g = grad[r]
        sums[0] += own_sum(g)
        last[r + 4] = g

        @pl.when(r < 4)
        def _():
            masked_move(last, r + 12, grad[r], mask_ref, 1)

        @pl.when(r >= 4)
        def _():
            masked_move(last, r - 4, grad[r], mask_ref, -1)

    acc_one[...] = jnp.zeros_like(acc_one)
    acc_three[...] = jnp.zeros_like(acc_three)
    arrive(2, (0, 1, 2))

    def enter_last(q, carry):
        enter(2, inner_a, q)
        return carry

    lax.fori_loop(0, 4, enter_last, 0)
    stage_points(2)
    move_far(inner_a, mask_ref)
    arrive(2, (3,))
    arrive(1, (0, 1, 2))
    for b, inner, following in ((2, inner_a, inner_b), (1, inner_b, inner_a)):

        def pipelined(q, carry):
            through_taps(b, inner, q)
            enter(b - 1, following, q - 1)
            return carry

        through_taps(b, inner, 0)
        lax.fori_loop(1, 4, pipelined, 0)
        enter(b - 1, following, 3)
        stage_taps(b)
        stage_points(b - 1)
        move_near(following, mask_ref, 3 ** (b - 1))
        if b == 2:
            for copy in kept(0):
                copy.start()
            arrive(1, (3,))
            arrive(0, (0, 1, 2))
        else:
            arrive(0, (3,))
    last = inner_b

    def final(q, carry):
        through_taps(0, inner_a, q)
        return carry

    lax.fori_loop(0, 4, final, 0)
    stage_taps(0)

    def section_taps(r, carry):
        taps(r)
        return carry

    lax.fori_loop(0, 8, section_taps, 0)
    for copy in section_loads:
        copy.wait()
    through[...] = jnp.zeros_like(through)
    sact = sact_ref[0:own]

    def send(pair):
        place = pair ^ turn_index
        source = staged.at[pl.ds(2 * pair, 2)]
        for out, place_of in targets:

            @pl.when(place == place_of)
            def _(out=out):
                pltpu.make_async_copy(source, out, osem).start()

    def collect(q, carry):
        left = jnp.concatenate([last[2 * q, 0:own], last[2 * q + 1, 0:own]], axis=1)
        through[...] += nn(left, wsec[pl.ds(2 * q, 2)].reshape(512, 512))
        grads = tn(left, sact).astype(BF16)
        staged[2 * q, :, 0:512] = grads[0:256]
        staged[2 * q + 1, :, 0:512] = grads[256:512]

        @pl.when(q < 7)
        def _():
            send(q)

        return carry

    lax.fori_loop(0, 8, collect, 0)
    deep = through[...]
    gains = jnp.sum(sact.astype(F32) * deep, axis=0, keepdims=True)
    through[...] = deep * (0.5 * stat_ref[1:2])
    biases = jnp.concatenate(
        [jnp.sum(sums[index], axis=0, keepdims=True) for index in range(8)]
        + [jnp.zeros((120, 256), F32)],
        axis=0,
    )
    staged[15, :, 512:640] = jnp.transpose(biases).astype(BF16)
    gain_rows = jnp.concatenate(
        [gains[:, 128 * q : 128 * q + 128] for q in range(4)] + [jnp.zeros((60, 128), F32)], axis=0
    ).astype(BF16)
    for part in range(4):
        staged[15, 64 * part : 64 * part + 64, 640:768] = gain_rows

    send(7)
    for k, out in enumerate(sgrads):
        lanes = pl.ds(pl.multiple_of(128 * (chan ^ k), 128), 128)
        half = 0.5 * sigs[k].reshape(own, 128).astype(F32)
        slope = slope_twice(half, *silu_half(half)[1:])
        count = own // 16
        for tile in range(count):
            part = through[16 * tile : 16 * tile + 16, lanes]
            wide[0, pl.ds(tile, 16, stride=count + 1), :] = part
        groups = [wide[0, (count + 1) * n : (count + 1) * n + count, :] for n in range(16)]
        out[...] = (jnp.concatenate(groups, axis=0) * slope).astype(BF16)
    for pair in range(8):
        pltpu.make_async_copy(staged.at[pl.ds(2 * pair, 2)], sums_out[0], osem).wait()


def shape_of(shape, kind=BF16):
    return jax.ShapeDtypeStruct(shape, kind)


SPEC_VMEM = pl.BlockSpec(memory_space=pltpu.VMEM)
SPEC_ANY = pl.BlockSpec(memory_space=pl.ANY)
SPEC_SMEM = pl.BlockSpec(memory_space=pltpu.SMEM)


def params():
    return pltpu.CompilerParams(vmem_limit_bytes=VMEM_BYTES)


def cost(flops, moved_bytes):
    return pl.CostEstimate(flops=int(flops), bytes_accessed=int(moved_bytes), transcendentals=0)


def run_pack_weights(places, *arrays):
    return pl.pallas_call(
        pack_weights_kernel,
        out_shape=shape_of((2, 64, 768)),
        in_specs=[SPEC_SMEM] + [SPEC_VMEM] * 11,
        out_specs=SPEC_VMEM,
        scratch_shapes=[
            pltpu.VMEM((4, 1024, 128), F32),
            pltpu.VMEM((128, 128), F32),
            pltpu.VMEM((16, 64, 256), BF16),
        ],
        compiler_params=params(),
        cost_estimate=cost(2e7, 3e6),
        name="pack_weights",
    )(places, *arrays)


def run_pack_frames(places, low, high, signal, cotangent):
    own = signal.shape[0] // 4
    return pl.pallas_call(
        pack_frames_kernel,
        out_shape=[shape_of((own // 64 + 1 + EARLY, 64, 128))] * 4
        + [shape_of((8 * own // 128 + 1 - EARLY, 64, 128))] * 4,
        in_specs=[SPEC_SMEM] + [SPEC_VMEM] * 4,
        out_specs=[SPEC_VMEM] * 8,
        compiler_params=params(),
        cost_estimate=cost(1e6, 6e6),
        name="pack_frames",
    )(places, low, high, signal, cotangent)


def run_finish(places, v_section, three, v_mix, v_skip, g_dilated, g_mix, g_skip, stat, pieces):
    small = shape_of((3, 64), F32)
    out_shape = [
        shape_of((64, 16, 512), F32),
        shape_of((1, 512), F32),
        shape_of((1, 64), F32),
        shape_of((3, 3, 64, 256), F32),
        small,
        small,
        shape_of((3, 64, 256), F32),
        small,
        small,
        shape_of((3, 64, 256), F32),
        small,
        small,
    ]
    return pl.pallas_call(
        finish_kernel,
        out_shape=out_shape,
        in_specs=[SPEC_SMEM] + [SPEC_VMEM] * 16,
        out_specs=[SPEC_VMEM] * 12,
        scratch_shapes=[
            pltpu.VMEM((4, 64 * 17, 128), F32),
            pltpu.VMEM((128, 128), F32),
            pltpu.VMEM((16, 64, 256), F32),
        ],
        compiler_params=params(),
        cost_estimate=cost(2e7, 8e6),
        name="finish_weights",
    )(places, v_section, three, v_mix, v_skip, g_dilated, g_mix, g_skip, stat, *pieces)


def run_forward(places, firsts, ids, gain, pieces):
    own = ids.shape[0] - 32
    rows = own + 2 * HALO
    kept = shape_of((3, 8, rows, 256))
    out_shape = [kept] * 4 + [
        shape_of((rows, 512)),
        shape_of((4, rows, 128)),
        shape_of((8, 512), F32),
    ]
    out_shape = out_shape + [shape_of((64, 8 * own))] * 4
    return pl.pallas_call(
        forward_kernel,
        out_shape=out_shape,
        in_specs=[SPEC_SMEM] + [SPEC_VMEM] * 6 + [SPEC_ANY] * 8,
        out_specs=[SPEC_ANY] * 4 + [SPEC_VMEM] * 3 + [SPEC_ANY] * 4,
        scratch_shapes=[
            pltpu.VMEM((16, 256, 512), BF16),
            pltpu.VMEM((16, 256, 256), BF16),
            pltpu.VMEM((3, rows, 512), BF16),
            pltpu.VMEM((16, 256), F32),
            pltpu.VMEM((2, 16 * (own // 2 + 1), 128), F32),
            pltpu.VMEM((256, 8 * own), BF16),
            pltpu.VMEM((own + 16, 128), F32),
        ]
        + [pltpu.VMEM((8, rows, 256), BF16)] * 9
        + [pltpu.VMEM((26, rows, 256), BF16)] * 3
        + [pltpu.SemaphoreType.DMA((8,)), pltpu.SemaphoreType.DMA, pltpu.SemaphoreType.DMA],
        compiler_params=params(),
        cost_estimate=cost(2 * 1245184 * 8 * rows, 50e6),
        name="forward_blocks",
    )(places, *firsts, ids, gain, *pieces)


def run_backward(places, firsts, seconds, sact, masks, stat, kept, pieces):
    rows = sact.shape[0]
    own = rows - 2 * HALO
    return pl.pallas_call(
        backward_kernel,
        out_shape=[
            shape_of((2, 256, 768)),
            shape_of((2, 2, 256, 768)),
            shape_of((2, 256, 768)),
        ]
        * 2
        + [shape_of((own, 128))] * 4,
        in_specs=[SPEC_SMEM]
        + [SPEC_ANY] * 8
        + [SPEC_VMEM] * 3
        + [SPEC_ANY] * 12,
        out_specs=[SPEC_ANY] * 6 + [SPEC_VMEM] * 4,
        scratch_shapes=[
            pltpu.VMEM((16, 256, 512), BF16),
            pltpu.VMEM((16, 256, 256), BF16),
            pltpu.VMEM((8 * own // 128 + 1, 256, 128), BF16),
            pltpu.VMEM((4, own // 64, 64, 128), BF16),
            pltpu.VMEM((2, 16 * (own // 2 + 1) + 128, 128), F32),
            pltpu.VMEM((8, rows, 256), BF16),
            pltpu.VMEM((26, rows, 256), BF16),
            pltpu.VMEM((26, rows, 256), BF16),
            pltpu.VMEM((2, 8, own, 256), BF16),
            pltpu.VMEM((2, 8, rows, 256), BF16),
            pltpu.VMEM((2, 8, own, 256), BF16),
            pltpu.VMEM((2, 8, rows, 256), BF16),
            pltpu.VMEM((256, 512), F32),
            pltpu.VMEM((768, 256), F32),
            pltpu.VMEM((own, 512), F32),
            pltpu.VMEM((8, 8, 256), F32),
            pltpu.VMEM((16, 256, 768), BF16),
            pltpu.SemaphoreType.DMA((8,)),
            pltpu.SemaphoreType.DMA,
            pltpu.SemaphoreType.DMA,
            pltpu.SemaphoreType.DMA,
            pltpu.SemaphoreType.DMA((2, 4)),
            pltpu.SemaphoreType.DMA,
        ],
        compiler_params=params(),
        cost_estimate=cost(2 * 2490368 * 8 * rows, 60e6),
        name="backward_blocks",
    )(places, *firsts, *seconds, sact, masks, stat, *kept, *pieces)


def exchange(values, axis, cut):
    me = lax.axis_index(axis)
    parts = [cut(me)]
    for k in (1, 2, 3):
        parts.append(swap(cut(me ^ k), axis, k))
    return parts


def body(
    signal,
    segment_ids,
    v_section,
    g_section,
    b_section,
    v_dilated,
    g_dilated,
    b_dilated,
    v_mix,
    g_mix,
    b_mix,
    v_skip,
    g_skip,
    b_skip,
    cotangent,
):
    tm_index, chan = lax.axis_index("tm"), lax.axis_index("chan")
    tm_size = lax.axis_size("tm")
    turn = tm_index % 8
    places = jnp.stack([turn, chan]).astype(jnp.int32)
    own = signal.shape[0] // 4
    rows = own + 2 * HALO
    start = tm_index * signal.shape[0] + chan * own

    three_v = jnp.transpose(v_dilated, (0, 2, 1, 3))
    piece = run_pack_weights(
        places,
        v_section,
        three_v,
        v_mix,
        v_skip,
        b_section[None],
        b_dilated,
        b_mix,
        b_skip,
        g_dilated,
        g_mix,
        g_skip,
    )
    by_chan = [piece] + [swap(piece, "chan", k) for k in (1, 2, 3)]

    first = jnp.concatenate([signal[:16], cotangent[:, :128]], axis=0)
    final = jnp.concatenate([signal[-16:], cotangent[:, -128:]], axis=0)
    onward = [(i, i + 1) for i in range(tm_size - 1)]
    low = lax.ppermute(final, "tm", onward)
    high = lax.ppermute(first, "tm", [(target, source) for source, target in onward])
    packed = run_pack_frames(places, low, high, signal, cotangent)
    firsts, seconds = list(packed[0:4]), list(packed[4:8])
    by_chan, _ = lax.optimization_barrier((by_chan, packed[0]))
    for k in (1, 2, 3):
        firsts[k] = swap(firsts[k], "chan", k)
        seconds[k] = swap(seconds[k], "chan", k)
    pieces, firsts = gather_weights(jnp.stack(by_chan), firsts)
    padded = jnp.pad(segment_ids, 16, constant_values=-1)
    nearby = lax.dynamic_slice_in_dim(padded, start, own + 32)
    ids = jnp.broadcast_to(nearby[:, None], (own + 32, 128))

    frames = 8 * own
    results = run_forward(places, firsts, ids, g_section[None].astype(F32), pieces)
    kept, sact, masks, stat, outs = results[:4], results[4], results[5], results[6], results[7:]

    outs, seconds = lax.optimization_barrier((list(outs), seconds))
    received = [outs[0]] + [swap(outs[k], "chan", k) for k in (1, 2, 3)]
    results = run_backward(places, firsts, seconds, sact, masks, stat, kept, pieces)
    far, sides, here, odd_far, odd_sides, odd_here = results[0:6]
    sgrads = results[6:]
    far, sides, here, odd_far, odd_sides, odd_here, sgrads, received = lax.optimization_barrier(
        (far, sides, here, odd_far, odd_sides, odd_here, list(sgrads), received)
    )

    def chan_sum(values):
        def cut_rows(place):
            return lax.dynamic_slice_in_dim(values, place * 64, 64, axis=1)

        parts = exchange(values, "chan", cut_rows)
        return parts[0] + parts[1] + parts[2] + parts[3]

    odd_sides = swap(odd_sides, "tm", 1)
    far = far + swap(odd_far, "tm", 1)
    odd_here = swap(odd_here, "tm", 1)
    output = jnp.zeros((64, 4 * frames), BF16)
    for k in range(4):
        output = lax.dynamic_update_slice_in_dim(output, received[k], (chan ^ k) * frames, axis=1)
    across = chan_sum(far)
    for_x, for_y = sides[0] + odd_sides[0], sides[1] + odd_sides[1]
    sgrad_near = swap(sgrads[1], "chan", 1)
    far, sgrad_near = lax.optimization_barrier((far, sgrad_near))
    summed = (here + odd_here) + swap(for_x, "tm", 2) + swap(for_y, "tm", 4)
    summed, across = lax.optimization_barrier((summed, across))
    mine = chan_sum(summed) + swap(across, "tm", 6)
    bit = 8
    while bit < tm_size:
        mine = mine + swap(mine, "tm", bit)
        bit = 2 * bit
    gathered = spread(mine)

    received = [sgrads[0], sgrad_near, swap(sgrads[2], "chan", 2), swap(sgrads[3], "chan", 3)]
    signal_grad = jnp.zeros((4 * own, 128), BF16)
    for k in range(4):
        signal_grad = lax.dynamic_update_slice_in_dim(
            signal_grad, received[k], (chan ^ k) * own, axis=0
        )
    (sec, gain, bs, three, gt, bt, mix, gm, bm, skip, gk, bk) = run_finish(
        places, v_section, three_v, v_mix, v_skip, g_dilated, g_mix, g_skip, stat, gathered
    )
    return (
        output,
        signal_grad,
        sec,
        gain.reshape(512),
        bs.reshape(64),
        jnp.transpose(three, (0, 2, 1, 3)),
        gt,
        bt,
        mix,
        gm,
        bm,
        skip,
        gk,
        bk,
    )


def solution(mesh):
    return jax.shard_map(
        body,
        mesh=mesh,
        in_specs=(
            P("tm", "chan"),
            P(),
            P("chan", None, None),
            P(),
            P("chan"),
            P(None, "chan", None, None),
            P(None, "chan"),
            P(None, "chan"),
            P(None, "chan", None),
            P(None, "chan"),
            P(None, "chan"),
            P(None, "chan", None),
            P(None, "chan"),
            P(None, "chan"),
            P("chan", "tm"),
        ),
        out_specs=(
            P("chan", "tm"),
            P("tm", "chan"),
            P("chan", None, None),
            P(),
            P("chan"),
            P(None, "chan", None, None),
            P(None, "chan"),
            P(None, "chan"),
            P(None, "chan", None),
            P(None, "chan"),
            P(None, "chan"),
            P(None, "chan", None),
            P(None, "chan"),
            P(None, "chan"),
        ),
        check_vma=False,
    )
```

```python
import jax
import jax.numpy as jnp
from jax import lax
from jax.experimental import pallas as pl
from jax.experimental.pallas import tpu as pltpu
from jax.sharding import PartitionSpec as P

EPSILON = 1e-06
F32 = jnp.float32
BF16 = jnp.bfloat16
HALO = 8
EARLY = 15
VMEM_BYTES = 60 * 1024 * 1024


def xor_pairs(axis, bit):
    return [(i, i ^ bit) for i in range(lax.axis_size(axis))]


def swap(values, axis, bit):
    return lax.ppermute(values, axis, xor_pairs(axis, bit))


def spread(piece):
    near = [piece] + [swap(piece, "tm", place) for place in (2, 4, 6)]
    return near + [swap(entry, "tm", 1) for entry in near]


def gather_weights(column, signals):
    near = [column] + [swap(column, "tm", place) for place in (6, 2, 4)]
    near, signals = lax.optimization_barrier((near, signals))
    return near + [swap(entry, "tm", 1) for entry in near], signals


WEIGHT_PLACES = [(0, 0, 4), (6, 0, 4), (2, 0, 4), (4, 0, 4)]
WEIGHT_PLACES = WEIGHT_PLACES + [(a + 1, first, count) for a, first, count in WEIGHT_PLACES]


SPREAD_PLACES = [0, 2, 4, 6, 1, 3, 5, 7]


def own_places():
    return lax.axis_index("tm") % 8, lax.axis_index("chan")


def nt(left, right):
    return lax.dot_general(left, right, (((1,), (1,)), ((), ())), preferred_element_type=F32)


def nn(left, right):
    return lax.dot_general(left, right, (((1,), (0,)), ((), ())), preferred_element_type=F32)


def tn(left, right):
    return lax.dot_general(left, right, (((0,), (0,)), ((), ())), preferred_element_type=F32)


def sigmoid(values):
    return 0.5 * jnp.tanh(0.5 * values) + 0.5


def silu_half(half):
    turn = jnp.tanh(half)
    product = half * turn
    return half + product, turn, product


def slope_twice(half, turn, product):
    return (1.0 + turn) + (half - product * turn)


def to_rows(flat, values, target):
    count = values.shape[0] // 16
    for group in range(16):
        start = group * (count + 1)
        flat[start : start + count] = values[group * count : group * count + count]
    for tile in range(count):
        part = flat[pl.ds(tile, 16, stride=count + 1)]
        target[16 * tile : 16 * tile + 16] = part.astype(BF16)


def fill_masks(ids_ref, flat, mask_ref):
    rows = mask_ref.shape[1]
    own = rows - 2 * HALO
    for index, step in enumerate((-1, 1, -2, 2)):
        inside = (ids_ref[16 : 8 + rows] == ids_ref[16 + step : 8 + rows + step]).astype(F32)
        before = (ids_ref[8:16] == ids_ref[8 + step : 16 + step]).astype(F32)
        to_rows(flat, inside[0:own], mask_ref.at[index])
        halo = jnp.concatenate([inside[own : own + 8], before], axis=0)
        mask_ref[index, own:rows] = halo.astype(BF16)


def masked_move(store, target, values, mask_ref, step):
    rows = values.shape[0]
    own = rows - 2 * HALO
    index = {-1: 0, 1: 1, -2: 2, 2: 3}[step]
    place = lax.broadcasted_iota(jnp.int32, (16, values.shape[1]), 0)

    def tile(number):
        return values[16 * number : 16 * number + 16].astype(F32)

    def turned(part, count):
        return pltpu.roll(part, count % 16, 0)

    count = own // 16
    halo = tile(count)
    size = abs(step)
    if step > 0:
        last = {}
        outer = turned(halo, -step)
        for n in range(step):
            inner_part = turned(tile(n), -1)
            last[count - step + n] = jnp.where(place == 15, turned(halo, -1 - n), inner_part)
            outer = jnp.where(place == 16 - step + n, turned(tile(n), n - step), outer)
        kept = (0, own - 16 * size, 16 * size)
    else:
        last = {}
        outer = turned(halo, size)
        for n in range(size):
            source = tile(count - size + n)
            last[n] = jnp.where(place == 0, turned(halo, size - n), turned(source, 1))
            outer = jnp.where(place == n, turned(source, n + 1), outer)
        kept = (16 * size, own, -16 * size)
    last[count] = outer
    wide = values.shape[1] // 128

    def masked(part, first):
        mask = mask_ref[index, first : first + part.shape[0]]
        return part * jnp.concatenate([mask] * wide, axis=1)

    first, end, offset = kept
    store[target, first:end] = masked(values[first + offset : end + offset], first)
    for number, part in last.items():
        store[target, 16 * number : 16 * number + 16] = masked(part.astype(BF16), 16 * number)


def move_far(store, mask_ref):
    masked_move(store, 0, store[16], mask_ref, -2)
    masked_move(store, 25, store[9], mask_ref, 2)


def move_near(store, mask_ref, dilate):
    def before(phase, carry):
        masked_move(store, 1 + phase, store[9 + phase], mask_ref, -1)
        return carry

    def after(phase, carry):
        masked_move(store, 17 + phase, store[9 + phase], mask_ref, 1)
        return carry

    lax.fori_loop(8 - dilate, 8, before, 0)
    lax.fori_loop(0, dilate, after, 0)


def move_each(store, mask_ref, phase, values):
    masked_move(store, 1 + phase, values, mask_ref, -1)
    masked_move(store, 17 + phase, values, mask_ref, 1)


def pack_weights_kernel(sec_ref, three_ref, mix_ref, skip_ref, bs, bt, bm, bk, gt, gm, gk, out, wide, rows, mats
):
    turn, _ = own_places()
    for q in range(4):
        part = sec_ref[:, :, 128 * q : 128 * q + 128].astype(F32)
        wide[q] = part.reshape(1024, 128)
    rows[...] = jnp.zeros_like(rows)
    rows[0:1, 0:64] = bs[...].astype(F32)
    for index, ref in enumerate((bt, bm, bk, gt, gm, gk)):
        rows[1 + 3 * index : 4 + 3 * index, 0:64] = ref[...].astype(F32)
    columns = jnp.transpose(rows[...])[0:64]
    for b in range(3):
        three = three_ref[b].astype(F32)
        gain = columns[:, 10 + b : 11 + b]
        total = jnp.sum(jnp.sum(three * three, axis=0), axis=1, keepdims=True)
        scale = 0.5 * gain / jnp.sqrt(total + EPSILON)
        for tap in range(3):
            mats[5 * b + tap] = (three[tap] * scale).astype(BF16)
        for index, ref in ((3, mix_ref), (4, skip_ref)):
            part = ref[b].astype(F32)
            gain = columns[:, 3 * index + 4 + b : 3 * index + 5 + b]
            total = jnp.sum(part * part, axis=1, keepdims=True)
            gain = 0.5 * gain if index == 3 else gain
            mats[5 * b + index] = (part * (gain / jnp.sqrt(total + EPSILON))).astype(BF16)
    mats[15, :, 0:128] = columns.astype(BF16)
    mats[15, :, 128:256] = jnp.zeros((64, 128), BF16)
    for tap in range(2):
        for q in range(4):
            part = wide[q, pl.ds(2 * turn + tap, 64, stride=16), :]
            out[tap, :, 128 * q : 128 * q + 128] = part.astype(BF16)
        out[tap, :, 512:768] = mats[2 * turn + tap]


def pack_frames_kernel(low, high, signal, cotangent, *rest):
    firsts, seconds = rest[0:4], rest[4:8]
    _, chan = own_places()
    own = signal.shape[0] // 4
    frames = 8 * own
    count = own // 64
    row = lax.broadcasted_iota(jnp.int32, (16, 128), 0)
    lane = lax.broadcasted_iota(jnp.int32, (64, 128), 1)

    def halo(dest, after, before, edges, is_after):
        last, first = jnp.where(dest == 3, 1, 0), jnp.where(dest == 0, 1, 0)
        after = jnp.where(last == 1, edges[1].astype(F32), after.astype(F32))
        before = jnp.where(first == 1, edges[0].astype(F32), before.astype(F32))
        return jnp.where(is_after, after, before).astype(BF16)

    for k in range(4):
        dest = chan ^ k
        part = signal[pl.ds(pl.multiple_of(dest * own, own), own)]
        firsts[k][0:count] = part.reshape(count, 64, 128)
        after = pl.multiple_of(jnp.minimum(dest + 1, 3) * own, 16)
        before = pl.multiple_of(jnp.maximum(dest * own - 16, 0), 16)
        edges = (low[0:16], high[0:16])
        firsts[k][count] = jnp.zeros((64, 128), BF16)
        firsts[k][count, 0:16] = halo(
            dest, signal[pl.ds(after, 16)], signal[pl.ds(before, 16)], edges, row < HALO
        )
        for q in range(frames // 128):
            lanes = pl.ds(pl.multiple_of(dest * frames + 128 * q, 128), 128)
            part = cotangent[:, lanes]
            if q < EARLY:
                firsts[k][count + 1 + q] = part
            else:
                seconds[k][q - EARLY] = part
        after = pl.multiple_of(jnp.minimum(dest + 1, 3) * frames, 128)
        before = pl.multiple_of(jnp.maximum(dest * frames - 128, 0), 128)
        edges = (low[16:80], high[16:80])
        seconds[k][frames // 128 - EARLY] = halo(
            dest,
            cotangent[:, pl.ds(after, 128)],
            cotangent[:, pl.ds(before, 128)],
            edges,
            lane < 8 * HALO,
        )


def finish_kernel(sec_ref, three_ref, mix_ref, skip_ref, gt, gm, gk, stat, *rest):
    pieces = rest[:8]
    sec_out, gain_out, bs, three_out, gt_out, bt, mix_out, gm_out, bm, skip_out, gk_out, bk = rest[8:20]
    wide, rows, mats = rest[20:]
    turn, _ = own_places()
    for ref, place in zip(pieces, SPREAD_PLACES, strict=True):
        pair = 2 * (turn ^ place)
        for tap in range(2):
            k = pair + tap
            part = ref[tap].astype(F32)
            for q in range(4):
                wide[q, pl.ds(k, 64, stride=17), :] = part[:, 128 * q : 128 * q + 128]
            mats[k] = part[:, 512:768]
    aux = mats[15]
    norm, scale = stat[0:1], stat[1:2]
    gains = jnp.concatenate([aux[q : q + 1, 128:256] for q in range(4)], axis=1) / norm
    gain_out[...] = gains
    ratio = gains / norm
    for q in range(4):
        lanes = slice(128 * q, 128 * q + 128)
        for o in range(64):
            part = sec_ref[o, :, lanes].astype(F32)
            grad = wide[q, 17 * o : 17 * o + 16, :] - ratio[:, lanes] * part
            sec_out[o, :, lanes] = scale[:, lanes] * grad
    rows[...] = jnp.zeros_like(rows)
    for index, ref in enumerate((gt, gm, gk)):
        rows[3 * index : 3 * index + 3, 0:64] = ref[...].astype(F32)
    columns = jnp.transpose(rows[...])[0:64]
    results = []
    for b in range(3):
        three = three_ref[b].astype(F32)
        norm = jnp.sqrt(jnp.sum(jnp.sum(three * three, axis=0), axis=1, keepdims=True) + EPSILON)
        total = mats[5 * b] * three[0] + mats[5 * b + 1] * three[1] + mats[5 * b + 2] * three[2]
        gain = jnp.sum(total, axis=1, keepdims=True) / norm
        results.append(gain)
        for tap in range(3):
            grad = mats[5 * b + tap] - gain / norm * three[tap]
            three_out[b, tap] = columns[:, b : b + 1] / norm * grad
    for index, (ref, out) in enumerate(((mix_ref, mix_out), (skip_ref, skip_out))):
        for b in range(3):
            part = ref[b].astype(F32)
            grad = mats[5 * b + 3 + index]
            norm = jnp.sqrt(jnp.sum(part * part, axis=1, keepdims=True) + EPSILON)
            gain = jnp.sum(grad * part, axis=1, keepdims=True) / norm
            results.append(gain)
            place = 3 + 3 * index + b
            out[b] = columns[:, place : place + 1] / norm * (grad - gain / norm * part)
    lane = lax.broadcasted_iota(jnp.int32, (64, 128), 1)
    table = jnp.where(lane < 7, aux[:, 0:128], 0.0)
    for index, gain in enumerate(results):
        table = jnp.where(lane == 8 + index, gain, table)
    rows[:, 0:64] = jnp.transpose(table)
    bs[...] = rows[0:1, 0:64]
    bt[...] = rows[1:4, 0:64]
    bm[...] = rows[4:7, 0:64]
    bk[...] = rows[4:7, 0:64]
    gt_out[...] = rows[8:11, 0:64]
    gm_out[...] = rows[11:14, 0:64]
    gk_out[...] = rows[14:17, 0:64]


def weight_copies(refs, wsec, wblk, sem, block_sem):
    turn, chan = own_places()
    section, blocks = [], []
    for index, (ref, (place, _, _)) in enumerate(zip(refs, WEIGHT_PLACES, strict=True)):
        slots = pl.ds(2 * (turn ^ place), 2)
        copies = []
        for k in range(4):
            rows = pl.ds(pl.multiple_of(64 * (chan ^ k), 64), 64)
            target = wsec.at[slots, rows, :]
            copies.append(pltpu.make_async_copy(ref.at[k, :, :, 0:512], target, sem.at[index]))
            target = wblk.at[slots, rows, :]
            blocks.append(pltpu.make_async_copy(ref.at[k, :, :, 512:768], target, block_sem))
        section.append(copies)
    return section, blocks


def forward_kernel(
    sig0,
    sig1,
    sig2,
    sig3,
    ids_ref,
    gain_ref,
    *rest,
):
    pieces, rest = rest[:8], rest[8:]
    hid_out, act_out, mix_out, inner_out = rest[0:4]
    sact_out, mask_out, stat_out = rest[4:7]
    outs = rest[7:11]
    wsec, wblk, cat, bias, wide, turned, flat = rest[11:18]
    hids, mixs, inners, acts = rest[18:21], rest[21:24], rest[24:27], rest[27:30]
    wsem, vsem, ssem = rest[30:]
    _, chan = own_places()
    rows = sact_out.shape[0]
    own = rows - 2 * HALO
    pitch = own // 2 + 1
    section_loads, block_loads = weight_copies(pieces, wsec, wblk, wsem, vsem)
    for copy in sum(section_loads, []) + block_loads:
        copy.start()
    fill_masks(ids_ref, flat, mask_out)
    for k, ref in enumerate((sig0, sig1, sig2, sig3)):
        lanes = pl.ds(pl.multiple_of(128 * (chan ^ k), 128), 128)
        values = silu_half(0.5 * ref[0 : own // 64].reshape(own, 128).astype(F32))[0]
        to_rows(flat, values, sact_out.at[:, lanes])
        halo = silu_half(0.5 * ref[own // 64, 0:16].astype(F32))[0]
        sact_out[own:rows, lanes] = halo.astype(BF16)
    total = jnp.zeros((8, 512), F32)
    for (place, _, _), copies in zip(WEIGHT_PLACES, section_loads, strict=True):
        for copy in copies:
            copy.wait()
        for tap in range(2):
            part = wsec[2 * (own_places()[0] ^ place) + tap].astype(F32)
            total = total + jnp.sum((part * part).reshape(32, 8, 512), axis=0)
    for copy in block_loads:
        copy.wait()
    norm = jnp.sqrt(jnp.sum(total, axis=0, keepdims=True) + EPSILON)
    scale = gain_ref[...] / norm
    stat_out[...] = jnp.concatenate([norm, scale, jnp.zeros((6, 512), F32)], axis=0)
    bias[...] = 0.5 * jnp.transpose(wblk[15].astype(F32))[:16]
    cat[0] = (sact_out[...].astype(F32) * (0.5 * scale)).astype(BF16)
    masked_move(cat, 1, cat[0], mask_out, -1)
    masked_move(cat, 2, cat[0], mask_out, 1)
    saves = []

    def keep(source, out, b):
        copy = pltpu.make_async_copy(source, out.at[b], ssem)
        copy.start()
        saves.append(copy)

    def enter(b, r, half):
        hids[b][r] = half.astype(BF16)
        value = silu_half(half)[0].astype(BF16)
        acts[b][9 + r] = value
        if b == 2:
            move_each(acts[b], mask_out, r, value)

    def phase_rows(values, n):
        return values[n * rows : n * rows + rows]

    def section(q, carry):
        left = jnp.concatenate([cat[0], cat[1 + q // 4]], axis=1)
        right = jnp.concatenate([wsec[q + 4], wsec[lax.rem(q + 12, 16)]], axis=1)
        enter(0, q, nt(left, right) + bias[0:1])
        return carry

    lax.fori_loop(0, 8, section, 0, unroll=4)
    for b in range(3):
        dilate = 3**b
        act, mix, sum_in, hid = acts[b], mixs[b], inners[b], hids[b]
        if b < 2:
            move_near(act, mask_out, dilate)
        else:
            move_far(act, mask_out)
        keep(hid, hid_out, b)
        keep(act.at[9:17], act_out, b)

        def taps(q):
            left = []
            for r in (2 * q, 2 * q + 1):
                parts = [act[9 + r - dilate], act[9 + r], act[9 + r + dilate]]
                left.append(jnp.concatenate(parts, axis=1))
            right = jnp.concatenate([wblk[5 * b], wblk[5 * b + 1], wblk[5 * b + 2]], axis=1)
            inner = nt(jnp.concatenate(left, axis=0), right)
            for n in range(2):
                half = phase_rows(inner, n) + bias[1 + b : 2 + b]
                mix[2 * q + n] = silu_half(half)[0].astype(BF16)
                sum_in[2 * q + n] = half.astype(BF16)

        def blend(q):
            left = []
            for r in (2 * q, 2 * q + 1):
                left.append(jnp.concatenate([mix[r], hid[r]], axis=1))
            right = jnp.concatenate([wblk[5 * b + 3], wblk[5 * b + 4]], axis=1)
            totals = [nt(part, right) for part in left]
            for n in range(2):
                r = 2 * q + n
                after = totals[n] + (bias[4 + b : 5 + b] + bias[7 + b : 8 + b])
                if b < 2:
                    enter(b + 1, r, after)
                else:
                    for tile in range(own // 16):
                        part = 2.0 * after[16 * tile : 16 * tile + 16]
                        frames = pl.ds(8 * tile + r, 16, stride=pitch)
                        wide[0, frames, :] = part[:, 0:128]
                        wide[1, frames, :] = part[:, 128:256]

        def both(q, carry):
            blend(q - 1)
            taps(q)
            return carry

        taps(0)
        lax.fori_loop(1, 4, both, 0)
        blend(3)
        keep(mix, mix_out, b)
        keep(sum_in, inner_out, b)

    def turn(q, carry):
        start = pitch * (q // 2) + 128 * lax.rem(q, 2)
        frames = pl.ds(pl.multiple_of(128 * q, 128), 128)
        for half in range(2):
            part = jnp.transpose(wide[half, pl.ds(start, 128), :])
            turned[128 * half : 128 * half + 128, frames] = part.astype(BF16)
        return carry

    lax.fori_loop(0, 8 * own // 128, turn, 0, unroll=4)
    final = []
    for k, out in enumerate(outs):
        part = turned.at[pl.ds(pl.multiple_of(64 * (chan ^ k), 64), 64), :]
        final.append(pltpu.make_async_copy(part, out, vsem))
    for copy in final:
        copy.start()
    for copy in saves + final:
        copy.wait()


def backward_kernel(
    first0,
    first1,
    first2,
    first3,
    second0,
    second1,
    second2,
    second3,
    sact_ref,
    mask_ref,
    stat_ref,
    hid_in,
    act_in,
    mix_in,
    inner_in,
    *rest,
):
    pieces, rest = rest[:8], rest[8:]
    sums_out = rest[0:6]
    sgrads = rest[6:10]
    targets = [(sums_out[0], 6), (sums_out[1].at[0], 2), (sums_out[1].at[1], 4), (sums_out[2], 0)]
    targets = targets + [
        (sums_out[3], 7),
        (sums_out[4].at[0], 3),
        (sums_out[4].at[1], 5),
        (sums_out[5], 1),
    ]
    (wsec, wblk, turned, sigs, wide, grad, inner_a, inner_b, mix, hid, act, halves) = rest[10:22]
    (acc_one, acc_three, through, sums, staged, wsem, vsem, gsem, csem, bsem, osem) = rest[22:]
    pitch = 4 * (sact_ref.shape[0] - 2 * HALO) // 8 + 1
    turn_index, chan = own_places()
    rows = mask_ref.shape[1]
    own = rows - 2 * HALO

    section_weights, block_loads = weight_copies(pieces, wsec, wblk, wsem, vsem)
    cots = []
    count = own // 64
    section_loads = []
    pairs = ((first0, second0), (first1, second1), (first2, second2), (first3, second3))
    for k, (one, two) in enumerate(pairs):
        part = pl.ds(pl.multiple_of(64 * (chan ^ k), 64), 64)
        early = one.at[count + 1 : count + 1 + EARLY]
        cots.append(pltpu.make_async_copy(early, turned.at[0:EARLY, part, :], csem))
        late = turned.at[EARLY : 8 * own // 128 + 1, part, :]
        cots.append(pltpu.make_async_copy(two, late, csem))
        section_loads.append(pltpu.make_async_copy(one.at[0:count], sigs.at[k], gsem))

    def kept(b):
        slot = b % 2
        return [
            pltpu.make_async_copy(inner_in.at[b], halves.at[slot], bsem.at[slot, 0]),
            pltpu.make_async_copy(mix_in.at[b, :, 0:own], mix.at[slot], bsem.at[slot, 1]),
            pltpu.make_async_copy(hid_in.at[b], hid.at[slot], bsem.at[slot, 2]),
            pltpu.make_async_copy(act_in.at[b, :, 0:own], act.at[slot], bsem.at[slot, 3]),
        ]

    section_loads = sum(section_weights, []) + section_loads
    for copy in cots + block_loads + kept(2) + kept(1) + section_loads:
        copy.start()
    sums[...] = jnp.zeros_like(sums)
    for copy in cots:
        copy.wait()
    def turn(q, carry):
        start = pitch * (q // 2) + 128 * lax.rem(q, 2)
        for half in range(2):
            part = turned[q, 128 * half : 128 * half + 128].astype(F32)
            wide[half, pl.ds(start, 128), :] = jnp.transpose(part)
        return carry

    lax.fori_loop(0, 8 * own // 128, turn, 0, unroll=4)
    turn(8 * own // 128, 0)

    def phases(r, carry):
        for half in range(2):
            lanes = slice(128 * half, 128 * half + 128)
            for tile in range(own // 16):
                part = wide[half, pl.ds(8 * tile + r, 16, stride=pitch), :]
                grad[r, 16 * tile : 16 * tile + 16, lanes] = part.astype(BF16)
            part = wide[half, pl.ds(16 * pitch + r, 16, stride=8), :]
            grad[r, own:rows, lanes] = part.astype(BF16)
        return carry

    lax.fori_loop(0, 8, phases, 0)
    for copy in block_loads:
        copy.wait()

    def own_sum(values):
        return jnp.sum(values[:own].astype(F32).reshape(own // 8, 8, 256), axis=0)

    def two(store, q, count):
        return jnp.concatenate([store[2 * q, 0:count], store[2 * q + 1, 0:count]], axis=0)

    def enter(b, inner, q):
        slot = b % 2
        g = two(grad, q, rows)
        down = nn(g, wblk[5 * b + 3])
        kept_rows = jnp.concatenate([mix[slot, 2 * q], mix[slot, 2 * q + 1]], axis=0)
        hidden = jnp.concatenate([hid[slot, 2 * q, 0:own], hid[slot, 2 * q + 1, 0:own]], axis=0)
        both = jnp.concatenate([kept_rows, hidden], axis=1)
        acc_one[...] += tn(two(grad, q, own), both)
        for n in range(2):
            r = 2 * q + n
            half = halves[slot, r].astype(F32)
            slope = slope_twice(half, *silu_half(half)[1:])
            part = (down[n * rows : n * rows + rows] * slope).astype(BF16)
            inner[9 + r] = part
            if b == 2:
                move_each(inner, mask_ref, r, part)

    def through_taps(b, inner, q):
        dilate, slot = 3**b, b % 2
        waves = []
        for r in (2 * q, 2 * q + 1):
            parts = [inner[9 + r + dilate], inner[9 + r], inner[9 + r - dilate]]
            waves.append(jnp.concatenate(parts, axis=1))
            sums[1 + b] += own_sum(parts[1])
            sums[4 + b] += own_sum(grad[r])
        deep = nn(jnp.concatenate(waves, axis=0), wblk[5 * b : 5 * b + 3].reshape(768, 256))
        skip = nn(two(grad, q, rows), wblk[5 * b + 4])
        acts = jnp.concatenate([act[slot, 2 * q], act[slot, 2 * q + 1]], axis=0)
        acc_three[...] += tn(jnp.concatenate([wave[:own] for wave in waves], axis=0), acts)
        for n in range(2):
            part = slice(n * rows, n * rows + rows)
            half = hid[slot, 2 * q + n].astype(F32)
            back = skip[part] + slope_twice(half, *silu_half(half)[1:]) * deep[part]
            grad[2 * q + n] = back.astype(BF16)

    def stage_taps(b):
        for tap in range(3):
            part = acc_three[256 * tap : 256 * tap + 256, :]
            staged[5 * b + tap, :, 512:768] = part.astype(BF16)
        acc_three[...] = jnp.zeros_like(acc_three)

    def stage_points(b):
        staged[5 * b + 3, :, 512:768] = acc_one[:, 0:256].astype(BF16)
        staged[5 * b + 4, :, 512:768] = (2.0 * acc_one[:, 256:512]).astype(BF16)
        acc_one[...] = jnp.zeros_like(acc_one)

    def arrive(b, numbers):
        for number in numbers:
            kept(b)[number].wait()

    def taps(r):
        g = grad[r]
        sums[0] += own_sum(g)
        last[r + 4] = g

        @pl.when(r < 4)
        def _():
            masked_move(last, r + 12, grad[r], mask_ref, 1)

        @pl.when(r >= 4)
        def _():
            masked_move(last, r - 4, grad[r], mask_ref, -1)

    acc_one[...] = jnp.zeros_like(acc_one)
    acc_three[...] = jnp.zeros_like(acc_three)
    arrive(2, (0, 1, 2))

    def enter_last(q, carry):
        enter(2, inner_a, q)
        return carry

    lax.fori_loop(0, 4, enter_last, 0)
    stage_points(2)
    move_far(inner_a, mask_ref)
    arrive(2, (3,))
    arrive(1, (0, 1, 2))
    for b, inner, following in ((2, inner_a, inner_b), (1, inner_b, inner_a)):

        def pipelined(q, carry):
            through_taps(b, inner, q)
            enter(b - 1, following, q - 1)
            return carry

        through_taps(b, inner, 0)
        lax.fori_loop(1, 4, pipelined, 0)
        enter(b - 1, following, 3)
        stage_taps(b)
        stage_points(b - 1)
        move_near(following, mask_ref, 3 ** (b - 1))
        if b == 2:
            for copy in kept(0):
                copy.start()
            arrive(1, (3,))
            arrive(0, (0, 1, 2))
        else:
            arrive(0, (3,))
    last = inner_b

    def final(q, carry):
        through_taps(0, inner_a, q)
        return carry

    lax.fori_loop(0, 4, final, 0)
    stage_taps(0)

    def section_taps(r, carry):
        taps(r)
        return carry

    lax.fori_loop(0, 8, section_taps, 0)
    for copy in section_loads:
        copy.wait()
    through[...] = jnp.zeros_like(through)
    sact = sact_ref[0:own]

    def send(pair):
        place = pair ^ turn_index
        source = staged.at[pl.ds(2 * pair, 2)]
        for out, place_of in targets:

            @pl.when(place == place_of)
            def _(out=out):
                pltpu.make_async_copy(source, out, osem).start()

    def collect(q, carry):
        left = jnp.concatenate([last[2 * q, 0:own], last[2 * q + 1, 0:own]], axis=1)
        through[...] += nn(left, wsec[pl.ds(2 * q, 2)].reshape(512, 512))
        grads = tn(left, sact).astype(BF16)
        staged[2 * q, :, 0:512] = grads[0:256]
        staged[2 * q + 1, :, 0:512] = grads[256:512]

        @pl.when(q < 7)
        def _():
            send(q)

        return carry

    lax.fori_loop(0, 8, collect, 0)
    deep = through[...]
    gains = jnp.sum(sact.astype(F32) * deep, axis=0, keepdims=True)
    through[...] = deep * (0.5 * stat_ref[1:2])
    biases = jnp.concatenate(
        [jnp.sum(sums[index], axis=0, keepdims=True) for index in range(8)]
        + [jnp.zeros((120, 256), F32)],
        axis=0,
    )
    staged[15, :, 512:640] = jnp.transpose(biases).astype(BF16)
    gain_rows = jnp.concatenate(
        [gains[:, 128 * q : 128 * q + 128] for q in range(4)] + [jnp.zeros((60, 128), F32)], axis=0
    ).astype(BF16)
    for part in range(4):
        staged[15, 64 * part : 64 * part + 64, 640:768] = gain_rows

    send(7)
    for k, out in enumerate(sgrads):
        lanes = pl.ds(pl.multiple_of(128 * (chan ^ k), 128), 128)
        half = 0.5 * sigs[k].reshape(own, 128).astype(F32)
        slope = slope_twice(half, *silu_half(half)[1:])
        count = own // 16
        for tile in range(count):
            part = through[16 * tile : 16 * tile + 16, lanes]
            wide[0, pl.ds(tile, 16, stride=count + 1), :] = part
        groups = [wide[0, (count + 1) * n : (count + 1) * n + count, :] for n in range(16)]
        out[...] = (jnp.concatenate(groups, axis=0) * slope).astype(BF16)
    for pair in range(8):
        pltpu.make_async_copy(staged.at[pl.ds(2 * pair, 2)], sums_out[0], osem).wait()


def shape_of(shape, kind=BF16):
    return jax.ShapeDtypeStruct(shape, kind)


SPEC_VMEM = pl.BlockSpec(memory_space=pltpu.VMEM)
SPEC_ANY = pl.BlockSpec(memory_space=pl.ANY)
SPEC_SMEM = pl.BlockSpec(memory_space=pltpu.SMEM)


def params():
    return pltpu.CompilerParams(vmem_limit_bytes=VMEM_BYTES)


def cost(flops, moved_bytes):
    return pl.CostEstimate(flops=int(flops), bytes_accessed=int(moved_bytes), transcendentals=0)


def run_pack_weights(*arrays):
    return pl.pallas_call(
        pack_weights_kernel,
        out_shape=shape_of((2, 64, 768)),
        in_specs=[SPEC_VMEM] * 11,
        out_specs=SPEC_VMEM,
        scratch_shapes=[
            pltpu.VMEM((4, 1024, 128), F32),
            pltpu.VMEM((128, 128), F32),
            pltpu.VMEM((16, 64, 256), BF16),
        ],
        compiler_params=params(),
        cost_estimate=cost(2e7, 3e6),
        name="pack_weights",
    )(*arrays)


def run_pack_frames(low, high, signal, cotangent):
    own = signal.shape[0] // 4
    return pl.pallas_call(
        pack_frames_kernel,
        out_shape=[shape_of((own // 64 + 1 + EARLY, 64, 128))] * 4
        + [shape_of((8 * own // 128 + 1 - EARLY, 64, 128))] * 4,
        in_specs=[SPEC_VMEM] * 4,
        out_specs=[SPEC_VMEM] * 8,
        compiler_params=params(),
        cost_estimate=cost(1e6, 6e6),
        name="pack_frames",
    )(low, high, signal, cotangent)


def run_finish(v_section, three, v_mix, v_skip, g_dilated, g_mix, g_skip, stat, pieces):
    small = shape_of((3, 64), F32)
    out_shape = [
        shape_of((64, 16, 512), F32),
        shape_of((1, 512), F32),
        shape_of((1, 64), F32),
        shape_of((3, 3, 64, 256), F32),
        small,
        small,
        shape_of((3, 64, 256), F32),
        small,
        small,
        shape_of((3, 64, 256), F32),
        small,
        small,
    ]
    return pl.pallas_call(
        finish_kernel,
        out_shape=out_shape,
        in_specs=[SPEC_VMEM] * 16,
        out_specs=[SPEC_VMEM] * 12,
        scratch_shapes=[
            pltpu.VMEM((4, 64 * 17, 128), F32),
            pltpu.VMEM((128, 128), F32),
            pltpu.VMEM((16, 64, 256), F32),
        ],
        compiler_params=params(),
        cost_estimate=cost(2e7, 8e6),
        name="finish_weights",
    )(v_section, three, v_mix, v_skip, g_dilated, g_mix, g_skip, stat, *pieces)


def run_forward(firsts, ids, gain, pieces):
    own = ids.shape[0] - 32
    rows = own + 2 * HALO
    kept = shape_of((3, 8, rows, 256))
    out_shape = [kept] * 4 + [
        shape_of((rows, 512)),
        shape_of((4, rows, 128)),
        shape_of((8, 512), F32),
    ]
    out_shape = out_shape + [shape_of((64, 8 * own))] * 4
    return pl.pallas_call(
        forward_kernel,
        out_shape=out_shape,
        in_specs=[SPEC_VMEM] * 6 + [SPEC_ANY] * 8,
        out_specs=[SPEC_ANY] * 4 + [SPEC_VMEM] * 3 + [SPEC_ANY] * 4,
        scratch_shapes=[
            pltpu.VMEM((16, 256, 512), BF16),
            pltpu.VMEM((16, 256, 256), BF16),
            pltpu.VMEM((3, rows, 512), BF16),
            pltpu.VMEM((16, 256), F32),
            pltpu.VMEM((2, 16 * (own // 2 + 1), 128), F32),
            pltpu.VMEM((256, 8 * own), BF16),
            pltpu.VMEM((own + 16, 128), F32),
        ]
        + [pltpu.VMEM((8, rows, 256), BF16)] * 9
        + [pltpu.VMEM((26, rows, 256), BF16)] * 3
        + [pltpu.SemaphoreType.DMA((8,)), pltpu.SemaphoreType.DMA, pltpu.SemaphoreType.DMA],
        compiler_params=params(),
        cost_estimate=cost(2 * 1245184 * 8 * rows, 50e6),
        name="forward_blocks",
    )(*firsts, ids, gain, *pieces)


def run_backward(firsts, seconds, sact, masks, stat, kept, pieces):
    rows = sact.shape[0]
    own = rows - 2 * HALO
    return pl.pallas_call(
        backward_kernel,
        out_shape=[
            shape_of((2, 256, 768)),
            shape_of((2, 2, 256, 768)),
            shape_of((2, 256, 768)),
        ]
        * 2
        + [shape_of((own, 128))] * 4,
        in_specs=[SPEC_ANY] * 8
        + [SPEC_VMEM] * 3
        + [SPEC_ANY] * 12,
        out_specs=[SPEC_ANY] * 6 + [SPEC_VMEM] * 4,
        scratch_shapes=[
            pltpu.VMEM((16, 256, 512), BF16),
            pltpu.VMEM((16, 256, 256), BF16),
            pltpu.VMEM((8 * own // 128 + 1, 256, 128), BF16),
            pltpu.VMEM((4, own // 64, 64, 128), BF16),
            pltpu.VMEM((2, 16 * (own // 2 + 1) + 128, 128), F32),
            pltpu.VMEM((8, rows, 256), BF16),
            pltpu.VMEM((26, rows, 256), BF16),
            pltpu.VMEM((26, rows, 256), BF16),
            pltpu.VMEM((2, 8, own, 256), BF16),
            pltpu.VMEM((2, 8, rows, 256), BF16),
            pltpu.VMEM((2, 8, own, 256), BF16),
            pltpu.VMEM((2, 8, rows, 256), BF16),
            pltpu.VMEM((256, 512), F32),
            pltpu.VMEM((768, 256), F32),
            pltpu.VMEM((own, 512), F32),
            pltpu.VMEM((8, 8, 256), F32),
            pltpu.VMEM((16, 256, 768), BF16),
            pltpu.SemaphoreType.DMA((8,)),
            pltpu.SemaphoreType.DMA,
            pltpu.SemaphoreType.DMA,
            pltpu.SemaphoreType.DMA,
            pltpu.SemaphoreType.DMA((2, 4)),
            pltpu.SemaphoreType.DMA,
        ],
        compiler_params=params(),
        cost_estimate=cost(2 * 2490368 * 8 * rows, 60e6),
        name="backward_blocks",
    )(*firsts, *seconds, sact, masks, stat, *kept, *pieces)


def exchange(values, axis, cut):
    me = lax.axis_index(axis)
    parts = [cut(me)]
    for k in (1, 2, 3):
        parts.append(swap(cut(me ^ k), axis, k))
    return parts


def body(
    signal,
    segment_ids,
    v_section,
    g_section,
    b_section,
    v_dilated,
    g_dilated,
    b_dilated,
    v_mix,
    g_mix,
    b_mix,
    v_skip,
    g_skip,
    b_skip,
    cotangent,
):
    tm_index, chan = lax.axis_index("tm"), lax.axis_index("chan")
    tm_size = lax.axis_size("tm")
    turn = tm_index % 8
    own = signal.shape[0] // 4
    rows = own + 2 * HALO
    start = tm_index * signal.shape[0] + chan * own

    three_v = jnp.transpose(v_dilated, (0, 2, 1, 3))
    piece = run_pack_weights(
            v_section,
        three_v,
        v_mix,
        v_skip,
        b_section[None],
        b_dilated,
        b_mix,
        b_skip,
        g_dilated,
        g_mix,
        g_skip,
    )
    by_chan = [piece] + [swap(piece, "chan", k) for k in (1, 2, 3)]

    first = jnp.concatenate([signal[:16], cotangent[:, :128]], axis=0)
    final = jnp.concatenate([signal[-16:], cotangent[:, -128:]], axis=0)
    onward = [(i, i + 1) for i in range(tm_size - 1)]
    low = lax.ppermute(final, "tm", onward)
    high = lax.ppermute(first, "tm", [(target, source) for source, target in onward])
    packed = run_pack_frames(low, high, signal, cotangent)
    firsts, seconds = list(packed[0:4]), list(packed[4:8])
    by_chan, _ = lax.optimization_barrier((by_chan, packed[0]))
    for k in (1, 2, 3):
        firsts[k] = swap(firsts[k], "chan", k)
        seconds[k] = swap(seconds[k], "chan", k)
    pieces, firsts = gather_weights(jnp.stack(by_chan), firsts)
    padded = jnp.pad(segment_ids, 16, constant_values=-1)
    nearby = lax.dynamic_slice_in_dim(padded, start, own + 32)
    ids = jnp.broadcast_to(nearby[:, None], (own + 32, 128))

    frames = 8 * own
    results = run_forward(firsts, ids, g_section[None].astype(F32), pieces)
    kept, sact, masks, stat, outs = results[:4], results[4], results[5], results[6], results[7:]

    outs, seconds = lax.optimization_barrier((list(outs), seconds))
    received = [outs[0]] + [swap(outs[k], "chan", k) for k in (1, 2, 3)]
    results = run_backward(firsts, seconds, sact, masks, stat, kept, pieces)
    far, sides, here, odd_far, odd_sides, odd_here = results[0:6]
    sgrads = results[6:]
    far, sides, here, odd_far, odd_sides, odd_here, sgrads, received = lax.optimization_barrier(
        (far, sides, here, odd_far, odd_sides, odd_here, list(sgrads), received)
    )

    def chan_sum(values):
        def cut_rows(place):
            return lax.dynamic_slice_in_dim(values, place * 64, 64, axis=1)

        parts = exchange(values, "chan", cut_rows)
        return parts[0] + parts[1] + parts[2] + parts[3]

    odd_sides = swap(odd_sides, "tm", 1)
    far = far + swap(odd_far, "tm", 1)
    odd_here = swap(odd_here, "tm", 1)
    output = jnp.zeros((64, 4 * frames), BF16)
    for k in range(4):
        output = lax.dynamic_update_slice_in_dim(output, received[k], (chan ^ k) * frames, axis=1)
    for_x, for_y = sides[0] + odd_sides[0], sides[1] + odd_sides[1]
    far, for_x, for_y, odd_here = lax.optimization_barrier((far, for_x, for_y, odd_here))
    across = chan_sum(far)
    sgrad_near = swap(sgrads[1], "chan", 1)
    far, sgrad_near = lax.optimization_barrier((far, sgrad_near))
    summed = (here + odd_here) + swap(for_x, "tm", 2) + swap(for_y, "tm", 4)
    summed, across = lax.optimization_barrier((summed, across))
    mine = chan_sum(summed) + swap(across, "tm", 6)
    bit = 8
    while bit < tm_size:
        mine = mine + swap(mine, "tm", bit)
        bit = 2 * bit
    gathered = spread(mine)

    received = [sgrads[0], sgrad_near, swap(sgrads[2], "chan", 2), swap(sgrads[3], "chan", 3)]
    signal_grad = jnp.zeros((4 * own, 128), BF16)
    for k in range(4):
        signal_grad = lax.dynamic_update_slice_in_dim(
            signal_grad, received[k], (chan ^ k) * own, axis=0
        )
    (sec, gain, bs, three, gt, bt, mix, gm, bm, skip, gk, bk) = run_finish(
        v_section, three_v, v_mix, v_skip, g_dilated, g_mix, g_skip, stat, gathered
    )
    return (
        output,
        signal_grad,
        sec,
        gain.reshape(512),
        bs.reshape(64),
        jnp.transpose(three, (0, 2, 1, 3)),
        gt,
        bt,
        mix,
        gm,
        bm,
        skip,
        gk,
        bk,
    )


def solution(mesh):
    return jax.shard_map(
        body,
        mesh=mesh,
        in_specs=(
            P("tm", "chan"),
            P(),
            P("chan", None, None),
            P(),
            P("chan"),
            P(None, "chan", None, None),
            P(None, "chan"),
            P(None, "chan"),
            P(None, "chan", None),
            P(None, "chan"),
            P(None, "chan"),
            P(None, "chan", None),
            P(None, "chan"),
            P(None, "chan"),
            P("chan", "tm"),
        ),
        out_specs=(
            P("chan", "tm"),
            P("tm", "chan"),
            P("chan", None, None),
            P(),
            P("chan"),
            P(None, "chan", None, None),
            P(None, "chan"),
            P(None, "chan"),
            P(None, "chan", None),
            P(None, "chan"),
            P(None, "chan"),
            P(None, "chan", None),
            P(None, "chan"),
            P(None, "chan"),
        ),
        check_vma=False,
    )
```

```python
import jax
import jax.numpy as jnp
from jax import lax
from jax.experimental import pallas as pl
from jax.experimental.pallas import tpu as pltpu
from jax.sharding import PartitionSpec as P

EPSILON = 1e-06
F32 = jnp.float32
BF16 = jnp.bfloat16
HALO = 8
EARLY = 15
VMEM_BYTES = 60 * 1024 * 1024


def xor_pairs(axis, bit):
    return [(i, i ^ bit) for i in range(lax.axis_size(axis))]


def swap(values, axis, bit):
    return lax.ppermute(values, axis, xor_pairs(axis, bit))


def spread(piece):
    near = [piece] + [swap(piece, "tm", place) for place in (2, 4, 6)]
    return near + [swap(entry, "tm", 1) for entry in near]


def gather_weights(column, signals):
    near = [column] + [swap(column, "tm", place) for place in (6, 2, 4)]
    near, signals = lax.optimization_barrier((near, signals))
    return near + [swap(entry, "tm", 1) for entry in near], signals


WEIGHT_PLACES = [(0, 0, 4), (6, 0, 4), (2, 0, 4), (4, 0, 4)]
WEIGHT_PLACES = WEIGHT_PLACES + [(a + 1, first, count) for a, first, count in WEIGHT_PLACES]


SPREAD_PLACES = [0, 2, 4, 6, 1, 3, 5, 7]


def own_places():
    return lax.axis_index("tm") % 8, lax.axis_index("chan")


def nt(left, right):
    return lax.dot_general(left, right, (((1,), (1,)), ((), ())), preferred_element_type=F32)


def nn(left, right):
    return lax.dot_general(left, right, (((1,), (0,)), ((), ())), preferred_element_type=F32)


def tn(left, right):
    return lax.dot_general(left, right, (((0,), (0,)), ((), ())), preferred_element_type=F32)


def sigmoid(values):
    return 0.5 * jnp.tanh(0.5 * values) + 0.5


def silu_half(half):
    turn = jnp.tanh(half)
    product = half * turn
    return half + product, turn, product


def slope_twice(half, turn, product):
    return (1.0 + turn) + (half - product * turn)


def to_rows(flat, values, target):
    count = values.shape[0] // 16
    for group in range(16):
        start = group * (count + 1)
        flat[start : start + count] = values[group * count : group * count + count]
    for tile in range(count):
        part = flat[pl.ds(tile, 16, stride=count + 1)]
        target[16 * tile : 16 * tile + 16] = part.astype(BF16)


def fill_masks(ids_ref, flat, mask_ref):
    rows = mask_ref.shape[1]
    own = rows - 2 * HALO
    for index, step in enumerate((-1, 1, -2, 2)):
        inside = (ids_ref[16 : 8 + rows] == ids_ref[16 + step : 8 + rows + step]).astype(F32)
        before = (ids_ref[8:16] == ids_ref[8 + step : 16 + step]).astype(F32)
        to_rows(flat, inside[0:own], mask_ref.at[index])
        halo = jnp.concatenate([inside[own : own + 8], before], axis=0)
        mask_ref[index, own:rows] = halo.astype(BF16)


def masked_move(store, target, values, mask_ref, step):
    rows = values.shape[0]
    own = rows - 2 * HALO
    index = {-1: 0, 1: 1, -2: 2, 2: 3}[step]
    place = lax.broadcasted_iota(jnp.int32, (16, values.shape[1]), 0)

    def tile(number):
        return values[16 * number : 16 * number + 16].astype(F32)

    def turned(part, count):
        return pltpu.roll(part, count % 16, 0)

    count = own // 16
    halo = tile(count)
    size = abs(step)
    if step > 0:
        last = {}
        outer = turned(halo, -step)
        for n in range(step):
            inner_part = turned(tile(n), -1)
            last[count - step + n] = jnp.where(place == 15, turned(halo, -1 - n), inner_part)
            outer = jnp.where(place == 16 - step + n, turned(tile(n), n - step), outer)
        kept = (0, own - 16 * size, 16 * size)
    else:
        last = {}
        outer = turned(halo, size)
        for n in range(size):
            source = tile(count - size + n)
            last[n] = jnp.where(place == 0, turned(halo, size - n), turned(source, 1))
            outer = jnp.where(place == n, turned(source, n + 1), outer)
        kept = (16 * size, own, -16 * size)
    last[count] = outer
    wide = values.shape[1] // 128

    def masked(part, first):
        mask = mask_ref[index, first : first + part.shape[0]]
        return part * jnp.concatenate([mask] * wide, axis=1)

    first, end, offset = kept
    store[target, first:end] = masked(values[first + offset : end + offset], first)
    for number, part in last.items():
        store[target, 16 * number : 16 * number + 16] = masked(part.astype(BF16), 16 * number)


def move_far(store, mask_ref):
    masked_move(store, 0, store[16], mask_ref, -2)
    masked_move(store, 25, store[9], mask_ref, 2)


def move_near(store, mask_ref, dilate):
    def before(phase, carry):
        masked_move(store, 1 + phase, store[9 + phase], mask_ref, -1)
        return carry

    def after(phase, carry):
        masked_move(store, 17 + phase, store[9 + phase], mask_ref, 1)
        return carry

    lax.fori_loop(8 - dilate, 8, before, 0)
    lax.fori_loop(0, dilate, after, 0)


def move_each(store, mask_ref, phase, values):
    masked_move(store, 1 + phase, values, mask_ref, -1)
    masked_move(store, 17 + phase, values, mask_ref, 1)


def pack_weights_kernel(sec_ref, three_ref, mix_ref, skip_ref, bs, bt, bm, bk, gt, gm, gk, out, wide, rows, mats
):
    turn, _ = own_places()
    for q in range(4):
        part = sec_ref[:, :, 128 * q : 128 * q + 128].astype(F32)
        wide[q] = part.reshape(1024, 128)
    rows[...] = jnp.zeros_like(rows)
    rows[0:1, 0:64] = bs[...].astype(F32)
    for index, ref in enumerate((bt, bm, bk, gt, gm, gk)):
        rows[1 + 3 * index : 4 + 3 * index, 0:64] = ref[...].astype(F32)
    columns = jnp.transpose(rows[...])[0:64]
    for b in range(3):
        three = three_ref[b].astype(F32)
        gain = columns[:, 10 + b : 11 + b]
        total = jnp.sum(jnp.sum(three * three, axis=0), axis=1, keepdims=True)
        scale = 0.5 * gain / jnp.sqrt(total + EPSILON)
        for tap in range(3):
            mats[5 * b + tap] = (three[tap] * scale).astype(BF16)
        for index, ref in ((3, mix_ref), (4, skip_ref)):
            part = ref[b].astype(F32)
            gain = columns[:, 3 * index + 4 + b : 3 * index + 5 + b]
            total = jnp.sum(part * part, axis=1, keepdims=True)
            gain = 0.5 * gain if index == 3 else gain
            mats[5 * b + index] = (part * (gain / jnp.sqrt(total + EPSILON))).astype(BF16)
    mats[15, :, 0:128] = columns.astype(BF16)
    mats[15, :, 128:256] = jnp.zeros((64, 128), BF16)
    for tap in range(2):
        for q in range(4):
            part = wide[q, pl.ds(2 * turn + tap, 64, stride=16), :]
            out[tap, :, 128 * q : 128 * q + 128] = part.astype(BF16)
        out[tap, :, 512:768] = mats[2 * turn + tap]


def pack_frames_kernel(low, high, signal, cotangent, *rest):
    firsts, seconds = rest[0:4], rest[4:8]
    _, chan = own_places()
    own = signal.shape[0] // 4
    frames = 8 * own
    row = lax.broadcasted_iota(jnp.int32, (16, 128), 0)
    lane = lax.broadcasted_iota(jnp.int32, (64, 128), 1)

    def halo(dest, after, before, edges, is_after):
        last, first = jnp.where(dest == 3, 1, 0), jnp.where(dest == 0, 1, 0)
        after = jnp.where(last == 1, edges[1].astype(F32), after.astype(F32))
        before = jnp.where(first == 1, edges[0].astype(F32), before.astype(F32))
        return jnp.where(is_after, after, before).astype(BF16)

    for k in range(4):
        dest = chan ^ k
        part = signal[pl.ds(pl.multiple_of(dest * own, own), own)]
        firsts[k][0:own] = part
        after = pl.multiple_of(jnp.minimum(dest + 1, 3) * own, 16)
        before = pl.multiple_of(jnp.maximum(dest * own - 16, 0), 16)
        edges = (low[0:16], high[0:16])
        firsts[k][own : own + 16] = halo(
            dest, signal[pl.ds(after, 16)], signal[pl.ds(before, 16)], edges, row < HALO
        )
        for q in range(frames // 128):
            lanes = pl.ds(pl.multiple_of(dest * frames + 128 * q, 128), 128)
            part = cotangent[:, lanes]
            if q < EARLY:
                firsts[k][own + 16 + 64 * q : own + 80 + 64 * q] = part
            else:
                seconds[k][q - EARLY] = part
        after = pl.multiple_of(jnp.minimum(dest + 1, 3) * frames, 128)
        before = pl.multiple_of(jnp.maximum(dest * frames - 128, 0), 128)
        edges = (low[16:80], high[16:80])
        seconds[k][frames // 128 - EARLY] = halo(
            dest,
            cotangent[:, pl.ds(after, 128)],
            cotangent[:, pl.ds(before, 128)],
            edges,
            lane < 8 * HALO,
        )


def finish_kernel(sec_ref, three_ref, mix_ref, skip_ref, gt, gm, gk, stat, *rest):
    pieces = rest[:8]
    sec_out, gain_out, bs, three_out, gt_out, bt, mix_out, gm_out, bm, skip_out, gk_out, bk = rest[8:20]
    wide, rows, mats = rest[20:]
    turn, _ = own_places()
    for ref, place in zip(pieces, SPREAD_PLACES, strict=True):
        pair = 2 * (turn ^ place)
        for tap in range(2):
            k = pair + tap
            part = ref[tap].astype(F32)
            for q in range(4):
                wide[q, pl.ds(k, 64, stride=17), :] = part[:, 128 * q : 128 * q + 128]
            mats[k] = part[:, 512:768]
    aux = mats[15]
    norm, scale = stat[0:1], stat[1:2]
    gains = jnp.concatenate([aux[q : q + 1, 128:256] for q in range(4)], axis=1) / norm
    gain_out[...] = gains
    ratio = gains / norm
    for q in range(4):
        lanes = slice(128 * q, 128 * q + 128)
        for o in range(64):
            part = sec_ref[o, :, lanes].astype(F32)
            grad = wide[q, 17 * o : 17 * o + 16, :] - ratio[:, lanes] * part
            sec_out[o, :, lanes] = scale[:, lanes] * grad
    rows[...] = jnp.zeros_like(rows)
    for index, ref in enumerate((gt, gm, gk)):
        rows[3 * index : 3 * index + 3, 0:64] = ref[...].astype(F32)
    columns = jnp.transpose(rows[...])[0:64]
    results = []
    for b in range(3):
        three = three_ref[b].astype(F32)
        norm = jnp.sqrt(jnp.sum(jnp.sum(three * three, axis=0), axis=1, keepdims=True) + EPSILON)
        total = mats[5 * b] * three[0] + mats[5 * b + 1] * three[1] + mats[5 * b + 2] * three[2]
        gain = jnp.sum(total, axis=1, keepdims=True) / norm
        results.append(gain)
        for tap in range(3):
            grad = mats[5 * b + tap] - gain / norm * three[tap]
            three_out[b, tap] = columns[:, b : b + 1] / norm * grad
    for index, (ref, out) in enumerate(((mix_ref, mix_out), (skip_ref, skip_out))):
        for b in range(3):
            part = ref[b].astype(F32)
            grad = mats[5 * b + 3 + index]
            norm = jnp.sqrt(jnp.sum(part * part, axis=1, keepdims=True) + EPSILON)
            gain = jnp.sum(grad * part, axis=1, keepdims=True) / norm
            results.append(gain)
            place = 3 + 3 * index + b
            out[b] = columns[:, place : place + 1] / norm * (grad - gain / norm * part)
    lane = lax.broadcasted_iota(jnp.int32, (64, 128), 1)
    table = jnp.where(lane < 7, aux[:, 0:128], 0.0)
    for index, gain in enumerate(results):
        table = jnp.where(lane == 8 + index, gain, table)
    rows[:, 0:64] = jnp.transpose(table)
    bs[...] = rows[0:1, 0:64]
    bt[...] = rows[1:4, 0:64]
    bm[...] = rows[4:7, 0:64]
    bk[...] = rows[4:7, 0:64]
    gt_out[...] = rows[8:11, 0:64]
    gm_out[...] = rows[11:14, 0:64]
    gk_out[...] = rows[14:17, 0:64]


def weight_copies(refs, wsec, wblk, sem, block_sem):
    turn, chan = own_places()
    section, blocks = [], []
    for index, (ref, (place, _, _)) in enumerate(zip(refs, WEIGHT_PLACES, strict=True)):
        slots = pl.ds(2 * (turn ^ place), 2)
        copies = []
        for k in range(4):
            rows = pl.ds(pl.multiple_of(64 * (chan ^ k), 64), 64)
            target = wsec.at[slots, rows, :]
            copies.append(pltpu.make_async_copy(ref.at[k, :, :, 0:512], target, sem.at[index]))
            target = wblk.at[slots, rows, :]
            blocks.append(pltpu.make_async_copy(ref.at[k, :, :, 512:768], target, block_sem))
        section.append(copies)
    return section, blocks


def forward_kernel(
    sig0,
    sig1,
    sig2,
    sig3,
    ids_ref,
    gain_ref,
    *rest,
):
    pieces, rest = rest[:8], rest[8:]
    hid_out, act_out, mix_out, inner_out = rest[0:4]
    sact_out, mask_out, stat_out = rest[4:7]
    outs = rest[7:11]
    wsec, wblk, cat, bias, wide, turned, flat = rest[11:18]
    hids, mixs, inners, acts = rest[18:21], rest[21:24], rest[24:27], rest[27:30]
    wsem, vsem, ssem = rest[30:]
    _, chan = own_places()
    rows = sact_out.shape[0]
    own = rows - 2 * HALO
    pitch = own // 2 + 1
    section_loads, block_loads = weight_copies(pieces, wsec, wblk, wsem, vsem)
    for copy in sum(section_loads, []) + block_loads:
        copy.start()
    fill_masks(ids_ref, flat, mask_out)
    for k, ref in enumerate((sig0, sig1, sig2, sig3)):
        lanes = pl.ds(pl.multiple_of(128 * (chan ^ k), 128), 128)
        values = silu_half(0.5 * ref[0:own].astype(F32))[0]
        to_rows(flat, values, sact_out.at[:, lanes])
        halo = silu_half(0.5 * ref[own : own + 16].astype(F32))[0]
        sact_out[own:rows, lanes] = halo.astype(BF16)
    total = jnp.zeros((8, 512), F32)
    for (place, _, _), copies in zip(WEIGHT_PLACES, section_loads, strict=True):
        for copy in copies:
            copy.wait()
        for tap in range(2):
            part = wsec[2 * (own_places()[0] ^ place) + tap].astype(F32)
            total = total + jnp.sum((part * part).reshape(32, 8, 512), axis=0)
    for copy in block_loads:
        copy.wait()
    norm = jnp.sqrt(jnp.sum(total, axis=0, keepdims=True) + EPSILON)
    scale = gain_ref[...].astype(F32) / norm
    stat_out[...] = jnp.concatenate([norm, scale, jnp.zeros((6, 512), F32)], axis=0)
    bias[...] = 0.5 * jnp.transpose(wblk[15].astype(F32))[:16]
    cat[0] = (sact_out[...].astype(F32) * (0.5 * scale)).astype(BF16)
    masked_move(cat, 1, cat[0], mask_out, -1)
    masked_move(cat, 2, cat[0], mask_out, 1)
    saves = []

    def keep(source, out, b):
        copy = pltpu.make_async_copy(source, out.at[b], ssem)
        copy.start()
        saves.append(copy)

    def enter(b, r, half):
        hids[b][r] = half.astype(BF16)
        value = silu_half(half)[0].astype(BF16)
        acts[b][9 + r] = value
        if b == 2:
            move_each(acts[b], mask_out, r, value)

    def phase_rows(values, n):
        return values[n * rows : n * rows + rows]

    def section(q, carry):
        left = jnp.concatenate([cat[0], cat[1 + q // 4]], axis=1)
        right = jnp.concatenate([wsec[q + 4], wsec[lax.rem(q + 12, 16)]], axis=1)
        enter(0, q, nt(left, right) + bias[0:1])
        return carry

    lax.fori_loop(0, 8, section, 0, unroll=4)
    for b in range(3):
        dilate = 3**b
        act, mix, sum_in, hid = acts[b], mixs[b], inners[b], hids[b]
        if b < 2:
            move_near(act, mask_out, dilate)
        else:
            move_far(act, mask_out)
        keep(hid, hid_out, b)
        keep(act.at[9:17], act_out, b)

        def taps(q):
            left = []
            for r in (2 * q, 2 * q + 1):
                parts = [act[9 + r - dilate], act[9 + r], act[9 + r + dilate]]
                left.append(jnp.concatenate(parts, axis=1))
            right = jnp.concatenate([wblk[5 * b], wblk[5 * b + 1], wblk[5 * b + 2]], axis=1)
            inner = nt(jnp.concatenate(left, axis=0), right)
            for n in range(2):
                half = phase_rows(inner, n) + bias[1 + b : 2 + b]
                mix[2 * q + n] = silu_half(half)[0].astype(BF16)
                sum_in[2 * q + n] = half.astype(BF16)

        def blend(q):
            left = []
            for r in (2 * q, 2 * q + 1):
                left.append(jnp.concatenate([mix[r], hid[r]], axis=1))
            right = jnp.concatenate([wblk[5 * b + 3], wblk[5 * b + 4]], axis=1)
            totals = [nt(part, right) for part in left]
            for n in range(2):
                r = 2 * q + n
                after = totals[n] + (bias[4 + b : 5 + b] + bias[7 + b : 8 + b])
                if b < 2:
                    enter(b + 1, r, after)
                else:
                    for tile in range(own // 16):
                        part = 2.0 * after[16 * tile : 16 * tile + 16]
                        frames = pl.ds(8 * tile + r, 16, stride=pitch)
                        wide[0, frames, :] = part[:, 0:128]
                        wide[1, frames, :] = part[:, 128:256]

        def both(q, carry):
            blend(q - 1)
            taps(q)
            return carry

        taps(0)
        lax.fori_loop(1, 4, both, 0)
        blend(3)
        keep(mix, mix_out, b)
        keep(sum_in, inner_out, b)

    def turn(q, carry):
        start = pitch * (q // 2) + 128 * lax.rem(q, 2)
        frames = pl.ds(pl.multiple_of(128 * q, 128), 128)
        for half in range(2):
            part = jnp.transpose(wide[half, pl.ds(start, 128), :])
            turned[128 * half : 128 * half + 128, frames] = part.astype(BF16)
        return carry

    lax.fori_loop(0, 8 * own // 128, turn, 0, unroll=4)
    final = []
    for k, out in enumerate(outs):
        part = turned.at[pl.ds(pl.multiple_of(64 * (chan ^ k), 64), 64), :]
        final.append(pltpu.make_async_copy(part, out, vsem))
    for copy in final:
        copy.start()
    for copy in saves + final:
        copy.wait()


def backward_kernel(
    first0,
    first1,
    first2,
    first3,
    second0,
    second1,
    second2,
    second3,
    sact_ref,
    mask_ref,
    stat_ref,
    hid_in,
    act_in,
    mix_in,
    inner_in,
    *rest,
):
    pieces, rest = rest[:8], rest[8:]
    sums_out = rest[0:6]
    sgrads = rest[6:10]
    targets = [(sums_out[0], 6), (sums_out[1].at[0], 2), (sums_out[1].at[1], 4), (sums_out[2], 0)]
    targets = targets + [
        (sums_out[3], 7),
        (sums_out[4].at[0], 3),
        (sums_out[4].at[1], 5),
        (sums_out[5], 1),
    ]
    (wsec, wblk, turned, sigs, wide, grad, inner_a, inner_b, mix, hid, act, halves) = rest[10:22]
    (acc_one, acc_three, through, sums, staged, wsem, vsem, gsem, csem, bsem, osem) = rest[22:]
    pitch = 4 * (sact_ref.shape[0] - 2 * HALO) // 8 + 1
    turn_index, chan = own_places()
    rows = mask_ref.shape[1]
    own = rows - 2 * HALO

    section_weights, block_loads = weight_copies(pieces, wsec, wblk, wsem, vsem)
    cots = []
    section_loads = []
    pairs = ((first0, second0), (first1, second1), (first2, second2), (first3, second3))
    for k, (one, two) in enumerate(pairs):
        part = pl.ds(pl.multiple_of(64 * (chan ^ k), 64), 64)
        for q in range(EARLY):
            early = one.at[own + 16 + 64 * q : own + 80 + 64 * q]
            cots.append(pltpu.make_async_copy(early, turned.at[q, part, :], csem))
        late = turned.at[EARLY : 8 * own // 128 + 1, part, :]
        cots.append(pltpu.make_async_copy(two, late, csem))
        section_loads.append(pltpu.make_async_copy(one.at[0:own], sigs.at[k], gsem))

    def kept(b):
        slot = b % 2
        return [
            pltpu.make_async_copy(inner_in.at[b], halves.at[slot], bsem.at[slot, 0]),
            pltpu.make_async_copy(mix_in.at[b, :, 0:own], mix.at[slot], bsem.at[slot, 1]),
            pltpu.make_async_copy(hid_in.at[b], hid.at[slot], bsem.at[slot, 2]),
            pltpu.make_async_copy(act_in.at[b, :, 0:own], act.at[slot], bsem.at[slot, 3]),
        ]

    section_loads = sum(section_weights, []) + section_loads
    for copy in cots + block_loads + kept(2) + kept(1) + section_loads:
        copy.start()
    sums[...] = jnp.zeros_like(sums)
    for copy in cots:
        copy.wait()
    def turn(q, carry):
        start = pitch * (q // 2) + 128 * lax.rem(q, 2)
        for half in range(2):
            part = turned[q, 128 * half : 128 * half + 128].astype(F32)
            wide[half, pl.ds(start, 128), :] = jnp.transpose(part)
        return carry

    lax.fori_loop(0, 8 * own // 128, turn, 0, unroll=4)
    turn(8 * own // 128, 0)

    def phases(r, carry):
        for half in range(2):
            lanes = slice(128 * half, 128 * half + 128)
            for tile in range(own // 16):
                part = wide[half, pl.ds(8 * tile + r, 16, stride=pitch), :]
                grad[r, 16 * tile : 16 * tile + 16, lanes] = part.astype(BF16)
            part = wide[half, pl.ds(16 * pitch + r, 16, stride=8), :]
            grad[r, own:rows, lanes] = part.astype(BF16)
        return carry

    lax.fori_loop(0, 8, phases, 0)
    for copy in block_loads:
        copy.wait()

    def own_sum(values):
        return jnp.sum(values[:own].astype(F32).reshape(own // 8, 8, 256), axis=0)

    def two(store, q, count):
        return jnp.concatenate([store[2 * q, 0:count], store[2 * q + 1, 0:count]], axis=0)

    def enter(b, inner, q):
        slot = b % 2
        g = two(grad, q, rows)
        down = nn(g, wblk[5 * b + 3])
        kept_rows = jnp.concatenate([mix[slot, 2 * q], mix[slot, 2 * q + 1]], axis=0)
        hidden = jnp.concatenate([hid[slot, 2 * q, 0:own], hid[slot, 2 * q + 1, 0:own]], axis=0)
        both = jnp.concatenate([kept_rows, hidden], axis=1)
        acc_one[...] += tn(two(grad, q, own), both)
        for n in range(2):
            r = 2 * q + n
            half = halves[slot, r].astype(F32)
            slope = slope_twice(half, *silu_half(half)[1:])
            part = (down[n * rows : n * rows + rows] * slope).astype(BF16)
            inner[9 + r] = part
            if b == 2:
                move_each(inner, mask_ref, r, part)

    def through_taps(b, inner, q):
        dilate, slot = 3**b, b % 2
        waves = []
        for r in (2 * q, 2 * q + 1):
            parts = [inner[9 + r + dilate], inner[9 + r], inner[9 + r - dilate]]
            waves.append(jnp.concatenate(parts, axis=1))
            sums[1 + b] += own_sum(parts[1])
            sums[4 + b] += own_sum(grad[r])
        deep = nn(jnp.concatenate(waves, axis=0), wblk[5 * b : 5 * b + 3].reshape(768, 256))
        skip = nn(two(grad, q, rows), wblk[5 * b + 4])
        acts = jnp.concatenate([act[slot, 2 * q], act[slot, 2 * q + 1]], axis=0)
        acc_three[...] += tn(jnp.concatenate([wave[:own] for wave in waves], axis=0), acts)
        for n in range(2):
            part = slice(n * rows, n * rows + rows)
            half = hid[slot, 2 * q + n].astype(F32)
            back = skip[part] + slope_twice(half, *silu_half(half)[1:]) * deep[part]
            grad[2 * q + n] = back.astype(BF16)

    def stage_taps(b):
        for tap in range(3):
            part = acc_three[256 * tap : 256 * tap + 256, :]
            staged[5 * b + tap, :, 512:768] = part.astype(BF16)
        acc_three[...] = jnp.zeros_like(acc_three)

    def stage_points(b):
        staged[5 * b + 3, :, 512:768] = acc_one[:, 0:256].astype(BF16)
        staged[5 * b + 4, :, 512:768] = (2.0 * acc_one[:, 256:512]).astype(BF16)
        acc_one[...] = jnp.zeros_like(acc_one)

    def arrive(b, numbers):
        for number in numbers:
            kept(b)[number].wait()

    def taps(r):
        g = grad[r]
        sums[0] += own_sum(g)
        last[r + 4] = g

        @pl.when(r < 4)
        def _():
            masked_move(last, r + 12, grad[r], mask_ref, 1)

        @pl.when(r >= 4)
        def _():
            masked_move(last, r - 4, grad[r], mask_ref, -1)

    acc_one[...] = jnp.zeros_like(acc_one)
    acc_three[...] = jnp.zeros_like(acc_three)
    arrive(2, (0, 1, 2))

    def enter_last(q, carry):
        enter(2, inner_a, q)
        return carry

    lax.fori_loop(0, 4, enter_last, 0)
    stage_points(2)
    move_far(inner_a, mask_ref)
    arrive(2, (3,))
    arrive(1, (0, 1, 2))
    for b, inner, following in ((2, inner_a, inner_b), (1, inner_b, inner_a)):

        def pipelined(q, carry):
            through_taps(b, inner, q)
            enter(b - 1, following, q - 1)
            return carry

        through_taps(b, inner, 0)
        lax.fori_loop(1, 4, pipelined, 0)
        enter(b - 1, following, 3)
        stage_taps(b)
        stage_points(b - 1)
        move_near(following, mask_ref, 3 ** (b - 1))
        if b == 2:
            for copy in kept(0):
                copy.start()
            arrive(1, (3,))
            arrive(0, (0, 1, 2))
        else:
            arrive(0, (3,))
    last = inner_b

    def final(q, carry):
        through_taps(0, inner_a, q)
        return carry

    lax.fori_loop(0, 4, final, 0)
    stage_taps(0)

    def section_taps(r, carry):
        taps(r)
        return carry

    lax.fori_loop(0, 8, section_taps, 0)
    for copy in section_loads:
        copy.wait()
    through[...] = jnp.zeros_like(through)
    sact = sact_ref[0:own]

    def send(pair):
        place = pair ^ turn_index
        source = staged.at[pl.ds(2 * pair, 2)]
        for out, place_of in targets:

            @pl.when(place == place_of)
            def _(out=out):
                pltpu.make_async_copy(source, out, osem).start()

    def collect(q, carry):
        left = jnp.concatenate([last[2 * q, 0:own], last[2 * q + 1, 0:own]], axis=1)
        through[...] += nn(left, wsec[pl.ds(2 * q, 2)].reshape(512, 512))
        grads = tn(left, sact).astype(BF16)
        staged[2 * q, :, 0:512] = grads[0:256]
        staged[2 * q + 1, :, 0:512] = grads[256:512]

        @pl.when(q < 7)
        def _():
            send(q)

        return carry

    lax.fori_loop(0, 8, collect, 0)
    deep = through[...]
    gains = jnp.sum(sact.astype(F32) * deep, axis=0, keepdims=True)
    through[...] = deep * (0.5 * stat_ref[1:2])
    biases = jnp.concatenate(
        [jnp.sum(sums[index], axis=0, keepdims=True) for index in range(8)]
        + [jnp.zeros((120, 256), F32)],
        axis=0,
    )
    staged[15, :, 512:640] = jnp.transpose(biases).astype(BF16)
    gain_rows = jnp.concatenate(
        [gains[:, 128 * q : 128 * q + 128] for q in range(4)] + [jnp.zeros((60, 128), F32)], axis=0
    ).astype(BF16)
    for part in range(4):
        staged[15, 64 * part : 64 * part + 64, 640:768] = gain_rows

    send(7)
    for k, out in enumerate(sgrads):
        lanes = pl.ds(pl.multiple_of(128 * (chan ^ k), 128), 128)
        half = 0.5 * sigs[k].astype(F32)
        slope = slope_twice(half, *silu_half(half)[1:])
        count = own // 16
        for tile in range(count):
            part = through[16 * tile : 16 * tile + 16, lanes]
            wide[0, pl.ds(tile, 16, stride=count + 1), :] = part
        groups = [wide[0, (count + 1) * n : (count + 1) * n + count, :] for n in range(16)]
        out[...] = (jnp.concatenate(groups, axis=0) * slope).astype(BF16)
    for pair in range(8):
        pltpu.make_async_copy(staged.at[pl.ds(2 * pair, 2)], sums_out[0], osem).wait()


def shape_of(shape, kind=BF16):
    return jax.ShapeDtypeStruct(shape, kind)


SPEC_VMEM = pl.BlockSpec(memory_space=pltpu.VMEM)
SPEC_ANY = pl.BlockSpec(memory_space=pl.ANY)
SPEC_SMEM = pl.BlockSpec(memory_space=pltpu.SMEM)


def params():
    return pltpu.CompilerParams(vmem_limit_bytes=VMEM_BYTES)


def cost(flops, moved_bytes):
    return pl.CostEstimate(flops=int(flops), bytes_accessed=int(moved_bytes), transcendentals=0)


def run_pack_weights(*arrays):
    return pl.pallas_call(
        pack_weights_kernel,
        out_shape=shape_of((2, 64, 768)),
        in_specs=[SPEC_VMEM] * 11,
        out_specs=SPEC_VMEM,
        scratch_shapes=[
            pltpu.VMEM((4, 1024, 128), F32),
            pltpu.VMEM((128, 128), F32),
            pltpu.VMEM((16, 64, 256), BF16),
        ],
        compiler_params=params(),
        cost_estimate=cost(2e7, 3e6),
        name="pack_weights",
    )(*arrays)


def run_pack_frames(low, high, signal, cotangent):
    own = signal.shape[0] // 4
    return pl.pallas_call(
        pack_frames_kernel,
        out_shape=[shape_of((own + 16 + 64 * EARLY, 128))] * 4
        + [shape_of((8 * own // 128 + 1 - EARLY, 64, 128))] * 4,
        in_specs=[SPEC_VMEM] * 4,
        out_specs=[SPEC_VMEM] * 8,
        compiler_params=params(),
        cost_estimate=cost(1e6, 6e6),
        name="pack_frames",
    )(low, high, signal, cotangent)


def run_finish(v_section, three, v_mix, v_skip, g_dilated, g_mix, g_skip, stat, pieces):
    small = shape_of((3, 64), F32)
    out_shape = [
        shape_of((64, 16, 512), F32),
        shape_of((1, 512), F32),
        shape_of((1, 64), F32),
        shape_of((3, 3, 64, 256), F32),
        small,
        small,
        shape_of((3, 64, 256), F32),
        small,
        small,
        shape_of((3, 64, 256), F32),
        small,
        small,
    ]
    return pl.pallas_call(
        finish_kernel,
        out_shape=out_shape,
        in_specs=[SPEC_VMEM] * 16,
        out_specs=[SPEC_VMEM] * 12,
        scratch_shapes=[
            pltpu.VMEM((4, 64 * 17, 128), F32),
            pltpu.VMEM((128, 128), F32),
            pltpu.VMEM((16, 64, 256), F32),
        ],
        compiler_params=params(),
        cost_estimate=cost(2e7, 8e6),
        name="finish_weights",
    )(v_section, three, v_mix, v_skip, g_dilated, g_mix, g_skip, stat, *pieces)


def run_forward(firsts, ids, gain, pieces):
    own = ids.shape[0] - 32
    rows = own + 2 * HALO
    kept = shape_of((3, 8, rows, 256))
    out_shape = [kept] * 4 + [
        shape_of((rows, 512)),
        shape_of((4, rows, 128)),
        shape_of((8, 512), F32),
    ]
    out_shape = out_shape + [shape_of((64, 8 * own))] * 4
    return pl.pallas_call(
        forward_kernel,
        out_shape=out_shape,
        in_specs=[SPEC_VMEM] * 6 + [SPEC_ANY] * 8,
        out_specs=[SPEC_ANY] * 4 + [SPEC_VMEM] * 3 + [SPEC_ANY] * 4,
        scratch_shapes=[
            pltpu.VMEM((16, 256, 512), BF16),
            pltpu.VMEM((16, 256, 256), BF16),
            pltpu.VMEM((3, rows, 512), BF16),
            pltpu.VMEM((16, 256), F32),
            pltpu.VMEM((2, 16 * (own // 2 + 1), 128), F32),
            pltpu.VMEM((256, 8 * own), BF16),
            pltpu.VMEM((own + 16, 128), F32),
        ]
        + [pltpu.VMEM((8, rows, 256), BF16)] * 9
        + [pltpu.VMEM((26, rows, 256), BF16)] * 3
        + [pltpu.SemaphoreType.DMA((8,)), pltpu.SemaphoreType.DMA, pltpu.SemaphoreType.DMA],
        compiler_params=params(),
        cost_estimate=cost(2 * 1245184 * 8 * rows, 50e6),
        name="forward_blocks",
    )(*firsts, ids, gain, *pieces)


def run_backward(firsts, seconds, sact, masks, stat, kept, pieces):
    rows = sact.shape[0]
    own = rows - 2 * HALO
    return pl.pallas_call(
        backward_kernel,
        out_shape=[
            shape_of((2, 256, 768)),
            shape_of((2, 2, 256, 768)),
            shape_of((2, 256, 768)),
        ]
        * 2
        + [shape_of((own, 128))] * 4,
        in_specs=[SPEC_ANY] * 8
        + [SPEC_VMEM] * 3
        + [SPEC_ANY] * 12,
        out_specs=[SPEC_ANY] * 6 + [SPEC_VMEM] * 4,
        scratch_shapes=[
            pltpu.VMEM((16, 256, 512), BF16),
            pltpu.VMEM((16, 256, 256), BF16),
            pltpu.VMEM((8 * own // 128 + 1, 256, 128), BF16),
            pltpu.VMEM((4, own, 128), BF16),
            pltpu.VMEM((2, 16 * (own // 2 + 1) + 128, 128), F32),
            pltpu.VMEM((8, rows, 256), BF16),
            pltpu.VMEM((26, rows, 256), BF16),
            pltpu.VMEM((26, rows, 256), BF16),
            pltpu.VMEM((2, 8, own, 256), BF16),
            pltpu.VMEM((2, 8, rows, 256), BF16),
            pltpu.VMEM((2, 8, own, 256), BF16),
            pltpu.VMEM((2, 8, rows, 256), BF16),
            pltpu.VMEM((256, 512), F32),
            pltpu.VMEM((768, 256), F32),
            pltpu.VMEM((own, 512), F32),
            pltpu.VMEM((8, 8, 256), F32),
            pltpu.VMEM((16, 256, 768), BF16),
            pltpu.SemaphoreType.DMA((8,)),
            pltpu.SemaphoreType.DMA,
            pltpu.SemaphoreType.DMA,
            pltpu.SemaphoreType.DMA,
            pltpu.SemaphoreType.DMA((2, 4)),
            pltpu.SemaphoreType.DMA,
        ],
        compiler_params=params(),
        cost_estimate=cost(2 * 2490368 * 8 * rows, 60e6),
        name="backward_blocks",
    )(*firsts, *seconds, sact, masks, stat, *kept, *pieces)


def exchange(values, axis, cut):
    me = lax.axis_index(axis)
    parts = [cut(me)]
    for k in (1, 2, 3):
        parts.append(swap(cut(me ^ k), axis, k))
    return parts


def body(
    signal,
    segment_ids,
    v_section,
    g_section,
    b_section,
    v_dilated,
    g_dilated,
    b_dilated,
    v_mix,
    g_mix,
    b_mix,
    v_skip,
    g_skip,
    b_skip,
    cotangent,
):
    tm_index, chan = lax.axis_index("tm"), lax.axis_index("chan")
    tm_size = lax.axis_size("tm")
    turn = tm_index % 8
    own = signal.shape[0] // 4
    rows = own + 2 * HALO
    start = tm_index * signal.shape[0] + chan * own

    three_v = jnp.transpose(v_dilated, (0, 2, 1, 3))
    piece = run_pack_weights(
            v_section,
        three_v,
        v_mix,
        v_skip,
        b_section[None],
        b_dilated,
        b_mix,
        b_skip,
        g_dilated,
        g_mix,
        g_skip,
    )
    by_chan = [piece] + [swap(piece, "chan", k) for k in (1, 2, 3)]

    first = jnp.concatenate([signal[:16], cotangent[:, :128]], axis=0)
    final = jnp.concatenate([signal[-16:], cotangent[:, -128:]], axis=0)
    onward = [(i, i + 1) for i in range(tm_size - 1)]
    low = lax.ppermute(final, "tm", onward)
    high = lax.ppermute(first, "tm", [(target, source) for source, target in onward])
    packed = run_pack_frames(low, high, signal, cotangent)
    firsts, seconds = list(packed[0:4]), list(packed[4:8])
    by_chan, _ = lax.optimization_barrier((by_chan, packed[0]))
    for k in (1, 2, 3):
        firsts[k] = swap(firsts[k], "chan", k)
        seconds[k] = swap(seconds[k], "chan", k)
    pieces, firsts = gather_weights(jnp.stack(by_chan), firsts)
    padded = jnp.pad(segment_ids, 16, constant_values=-1)
    nearby = lax.dynamic_slice_in_dim(padded, start, own + 32)
    ids = jnp.broadcast_to(nearby[:, None], (own + 32, 128))

    frames = 8 * own
    results = run_forward(firsts, ids, g_section[None], pieces)
    kept, sact, masks, stat, outs = results[:4], results[4], results[5], results[6], results[7:]

    outs, seconds = lax.optimization_barrier((list(outs), seconds))
    received = [outs[0]] + [swap(outs[k], "chan", k) for k in (1, 2, 3)]
    results = run_backward(firsts, seconds, sact, masks, stat, kept, pieces)
    far, sides, here, odd_far, odd_sides, odd_here = results[0:6]
    sgrads = results[6:]
    far, sides, here, odd_far, odd_sides, odd_here, sgrads, received = lax.optimization_barrier(
        (far, sides, here, odd_far, odd_sides, odd_here, list(sgrads), received)
    )

    def chan_sum(values):
        def cut_rows(place):
            return lax.dynamic_slice_in_dim(values, place * 64, 64, axis=1)

        parts = exchange(values, "chan", cut_rows)
        return parts[0] + parts[1] + parts[2] + parts[3]

    odd_sides = swap(odd_sides, "tm", 1)
    far = far + swap(odd_far, "tm", 1)
    odd_here = swap(odd_here, "tm", 1)
    output = jnp.zeros((64, 4 * frames), BF16)
    for k in range(4):
        output = lax.dynamic_update_slice_in_dim(output, received[k], (chan ^ k) * frames, axis=1)
    for_x, for_y = sides[0] + odd_sides[0], sides[1] + odd_sides[1]
    far, for_x, for_y, odd_here = lax.optimization_barrier((far, for_x, for_y, odd_here))
    across = chan_sum(far)
    sgrad_near = swap(sgrads[1], "chan", 1)
    far, sgrad_near = lax.optimization_barrier((far, sgrad_near))
    summed = (here + odd_here) + swap(for_x, "tm", 2) + swap(for_y, "tm", 4)
    summed, across = lax.optimization_barrier((summed, across))
    mine = chan_sum(summed) + swap(across, "tm", 6)
    bit = 8
    while bit < tm_size:
        mine = mine + swap(mine, "tm", bit)
        bit = 2 * bit
    gathered = spread(mine)

    received = [sgrads[0], sgrad_near, swap(sgrads[2], "chan", 2), swap(sgrads[3], "chan", 3)]
    signal_grad = jnp.zeros((4 * own, 128), BF16)
    for k in range(4):
        signal_grad = lax.dynamic_update_slice_in_dim(
            signal_grad, received[k], (chan ^ k) * own, axis=0
        )
    (sec, gain, bs, three, gt, bt, mix, gm, bm, skip, gk, bk) = run_finish(
        v_section, three_v, v_mix, v_skip, g_dilated, g_mix, g_skip, stat, gathered
    )
    return (
        output,
        signal_grad,
        sec,
        gain.reshape(512),
        bs.reshape(64),
        jnp.transpose(three, (0, 2, 1, 3)),
        gt,
        bt,
        mix,
        gm,
        bm,
        skip,
        gk,
        bk,
    )


def solution(mesh):
    return jax.shard_map(
        body,
        mesh=mesh,
        in_specs=(
            P("tm", "chan"),
            P(),
            P("chan", None, None),
            P(),
            P("chan"),
            P(None, "chan", None, None),
            P(None, "chan"),
            P(None, "chan"),
            P(None, "chan", None),
            P(None, "chan"),
            P(None, "chan"),
            P(None, "chan", None),
            P(None, "chan"),
            P(None, "chan"),
            P("chan", "tm"),
        ),
        out_specs=(
            P("chan", "tm"),
            P("tm", "chan"),
            P("chan", None, None),
            P(),
            P("chan"),
            P(None, "chan", None, None),
            P(None, "chan"),
            P(None, "chan"),
            P(None, "chan", None),
            P(None, "chan"),
            P(None, "chan"),
            P(None, "chan", None),
            P(None, "chan"),
            P(None, "chan"),
        ),
        check_vma=False,
    )
```
